32 devices in a mesh: fsdp: 2 (over core), ctx: 4 (over y, x), tp: 4 (over z).
Axes of the slice: x: 2, y: 2, z: 4, core: 2. Of those that a mesh axis runs over, the one named last changes fastest.
Arguments:
- inputs: bfloat16 [2, 1024, 1024], P('fsdp', 'ctx'), may hold values from -6 to 6
- query_weight: float32 [2, 1024, 1024], P(None, 'fsdp', 'tp'), may hold values from -0.1875 to 0.1875
- key_weight: float32 [2, 1024, 1024], P(None, 'fsdp', 'tp'), may hold values from -0.1875 to 0.1875
- value_weight: float32 [2, 1024, 1024], P(None, 'fsdp', 'tp'), may hold values from -0.1875 to 0.1875
- attention_weight: float32 [2, 1024, 1024], P(None, 'tp', 'fsdp'), may hold values from -4 to 4
- lookup_weight: float32 [2, 1024, 512], P(None, 'fsdp', 'tp'), may hold values from -0.1875 to 0.1875
- gate_weight: float32 [2, 1024, 1024], P(None, 'fsdp', 'tp'), may hold values from -0.1875 to 0.1875
- memory_weight: float32 [2, 1024, 1024], P(None, 'tp', 'fsdp'), may hold values from -0.75 to 0.75
- first_table: float32 [2, 4, 256, 64], P(None, 'tp', 'fsdp'), may hold values from -0.25 to 0.25
- second_table: float32 [2, 4, 256, 64], P(None, 'tp', 'fsdp'), may hold values from -0.25 to 0.25
- attention_gain: float32 [2, 1024], P(None, 'fsdp'), may hold values from 0.5 to 1.5
- memory_gain: float32 [2, 1024], P(None, 'fsdp'), may hold values from 0.5 to 1.5
- memory_values: bfloat16 [2, 65536, 1024], P(None, ('fsdp', 'ctx', 'tp')), may hold values from -6 to 6
- blocks: int32 [2, 1024], P('fsdp'), may hold values from 0 to 3, never falling along the last dimension, each value on 1 to 512 neighbouring positions
- first_picks: int32 [2, 2, 4, 1024, 4], P(None, 'fsdp', 'tp', 'ctx'), may hold values from 0 to 255, all different within a row; in each aligned block of 256 rows (0 to 255, 256 to 511, ..., all dimensions but the last counted through in order) at most 8 rows name the same one
- second_picks: int32 [2, 2, 4, 1024, 4, 8], P(None, 'fsdp', 'tp', 'ctx'), may hold values from 0 to 255, all different within a row
- cotangent: bfloat16 [2, 1024, 1024], P('fsdp', 'ctx'), may hold values from -6 to 6
Outputs:
- output: bfloat16 [2, 1024, 1024], P('fsdp', 'ctx')
- input_gradient: float32 [2, 1024, 1024], P('fsdp', 'ctx')
- query_gradient: float32 [2, 1024, 1024], P(None, 'fsdp', 'tp')
- key_gradient: float32 [2, 1024, 1024], P(None, 'fsdp', 'tp')
- value_gradient: float32 [2, 1024, 1024], P(None, 'fsdp', 'tp')
- attention_gradient: float32 [2, 1024, 1024], P(None, 'tp', 'fsdp')
- lookup_gradient: float32 [2, 1024, 512], P(None, 'fsdp', 'tp')
- gate_gradient: float32 [2, 1024, 1024], P(None, 'fsdp', 'tp')
- memory_gradient: float32 [2, 1024, 1024], P(None, 'tp', 'fsdp')
- first_gradient: float32 [2, 4, 256, 64], P(None, 'tp', 'fsdp')
- second_gradient: float32 [2, 4, 256, 64], P(None, 'tp', 'fsdp')
- attention_gain_gradient: float32 [2, 1024], P(None, 'fsdp')
- memory_gain_gradient: float32 [2, 1024], P(None, 'fsdp')
- values_gradient: float32 [2, 65536, 1024], P(None, ('fsdp', 'ctx', 'tp'))
The draws below stay inside these ranges and needn't reach their ends.
Inputs may be any that keep to these rules, and one draw needn't show every extreme that they name: `first_picks`: the 4 first sub-keys of a token and memory head differ. In each aligned block of 256 positions of one block l, sequence and memory head, no first sub-key is named by more than 8 positions, a bound that some block reaches. `second_picks`: the 8 second sub-keys under one first pick differ. `blocks`: block numbers never fall along a sequence and every number occurs; a block holds 1 to 512 positions, and some block holds exactly 512.
All inputs are finite; a program needn't handle non-finite values.
Results may differ from the reference program's by a relative error of at most 0.035.
Values may be sent and summed in bfloat16 or wider, within the bound.
No kernel may reach another device: no remote copies, remote signals or barrier semaphores. Data moves between devices by JAX's collectives and lax.ppermute only.
A program may use at most 192 MiB of HBM per device.

```python
import math
from functools import partial
import jax
import jax.numpy as jnp
import numpy as np
from jax import lax

D = 1024
H = 16
HD = 64
MH = 4
HALF = 64
NSUB = 256
NF = 4
NS = 8
BLOCK = 256
LAYERS = 2
TOK_DEV = 256
LEN = 1024
SEQS = 2
CAP = 8
MROWS = 65536


def level_of(key, dims, split, low, largest):
    factor_of, own = 1.0, jax.random.fold_in(key, 6)
    for dim, blocks in split:
        draws = jnp.exp(jax.random.uniform(jax.random.fold_in(own, dim), (blocks,), jnp.float32, low / len(split), largest / len(split)))
        factor_of = factor_of * jnp.repeat(draws, dims[dim] // blocks).reshape([-1 if axis == dim else 1 for axis in range(len(dims))])
    return factor_of


def different_ones(own_key, rows, amount, top, lift):
    order = jax.random.permutation(jax.random.fold_in(own_key, 1), amount)
    pull = order
    for power in range(3):
        pull = pull * pull // amount
    pull = pull * lift // amount
    lots = jax.random.randint(jax.random.fold_in(own_key, 2), (rows, amount), 0, 4096) + pull
    sure = jax.random.permutation(jax.random.fold_in(own_key, 3), rows)[jnp.arange(amount) % rows]
    lots = jnp.where(jnp.arange(rows)[:, None] == sure[None, :], 1 << 14, lots)
    merit = lots * amount + jnp.arange(amount)
    return lax.top_k(merit.astype(jnp.int32), top)[1].astype(jnp.int32)


def profile(number_of, total, bound, lean):
    loads = [(1 << 20) // math.isqrt(standing ** lean) + 1 for standing in range(2, number_of + 1)]
    spare, holding = total - bound - (number_of - 1), [1] * (number_of - 1)
    while spare > 0:
        candidates = [i for i in range(number_of - 1) if holding[i] < bound]
        mass, budget = sum([loads[i] for i in candidates]), spare
        for i in candidates:
            extra = min(bound - holding[i], max(1, budget * loads[i] // mass), spare)
            holding[i] = holding[i] + extra
            spare = spare - extra
    return np.array([bound] + holding)


def ragged(own_key, number_of, total, most, skew):
    if number_of == 2:
        one = jax.random.randint(own_key, (), max(1, total - most), min(most, total - 1) + 1)
        return jnp.stack([one, total - one])
    lengths = jnp.asarray(profile(number_of, total, most, skew), jnp.int32)
    pairs = (number_of - 1) // 2
    giver, receiver = lengths[1:1 + 2 * pairs:2], lengths[2:2 + 2 * pairs:2]
    slack = jnp.minimum(giver - 1, most - receiver)
    passed = jax.random.randint(jax.random.fold_in(own_key, 1), (pairs,), 0, 1 << 20) % (slack + 1)
    lengths = lengths.at[1:1 + 2 * pairs:2].set(giver - passed).at[2:2 + 2 * pairs:2].set(receiver + passed)
    return lengths[jax.random.permutation(jax.random.fold_in(own_key, 2), number_of)]


def deal_out(rng, own, number, rows, number_of, top, limit, skew):
    order = jax.random.permutation(rng, number_of)
    packed, common = load_shares(number_of, rows * top, limit, skew, True), load_shares(number_of, rows * top, limit, skew, False)
    places = jnp.arange(number_of)

    def named(lengths, offset_by):
        used = int((lengths > 0).sum())
        fixed = max(1, used // 4)
        moved = fixed + (places - fixed + offset_by * (used - fixed)) % max(1, number_of - fixed)
        return jnp.zeros((number_of,), jnp.int32).at[order[jnp.where(places < fixed, places, moved)]].set(jnp.asarray(lengths, jnp.int32))

    lengths = jnp.where(number % 4 == 0, named(packed, number // 4), named(common, number - number // 4 - 1))
    mixed = jax.random.permutation(jax.random.fold_in(own, 3), number_of)
    giver, sink = mixed[0:number_of // 2 * 2:2], mixed[1:number_of // 2 * 2:2]
    slack = jnp.minimum(lengths[giver] - 1, limit - lengths[sink]) // 2
    slack = jnp.where((giver == order[0]) | (sink == order[0]) | (lengths[sink] == 0), 0, jnp.maximum(slack, 0))
    moved = jax.random.randint(jax.random.fold_in(own, 4), (number_of // 2,), 0, 1 << 20) % (slack + 1)
    lengths = lengths.at[giver].add(-moved).at[sink].add(moved)
    labels = jnp.searchsorted(jnp.cumsum(lengths), jnp.arange(rows * top), side="right").astype(jnp.int32)
    grid = labels.reshape(top, rows).T
    grid = grid[jax.random.permutation(jax.random.fold_in(own, 1), rows)]
    offset_by = jax.random.randint(jax.random.fold_in(own, 2), (rows, 1), 0, top)
    return jnp.take_along_axis(grid, (jnp.arange(top)[None, :] + offset_by) % top, axis=1)


def load_shares(number_of, total, reach, lean, full):
    weights = [(1 << 20) // math.isqrt(standing ** lean) + 1 for standing in range(1, number_of + 1)]
    largest = reach if full else min(reach, max(-(-total // number_of), total * weights[0] // sum(weights)))
    least = 1 if total - largest >= number_of - 1 else 0
    given, spare = [largest] + [least] * (number_of - 1), total - largest - least * (number_of - 1)
    while spare > 0:
        movable = [i for i in range(1, number_of) if given[i] < largest] or [i for i in range(1, number_of) if given[i] < reach]
        pool, remaining = sum([weights[i] for i in movable]), spare
        for i in movable:
            extra = min(reach - given[i], max(1, remaining * weights[i] // pool), spare)
            given[i] = given[i] + extra
            spare = spare - extra
    return np.array(given)


def centred(own_key, extent, spread, bound, cuts=(), held_as=jnp.bfloat16):
    loudness = level_of(own_key, extent, cuts, -0.22, 0.18) if cuts else 1.0
    values = jax.random.normal(own_key, extent, jnp.float32) * spread * loudness
    return jnp.minimum(jnp.maximum(values, -bound), bound).astype(held_as)


def setup_inputs(seed: int = 0) -> dict:
    key_list = jax.random.split(jax.random.key(seed), 18)
    inputs = centred(key_list[0], (SEQS, LEN, D), 1.0, 6.0, ((0, 2), (1, 4)))
    query_weight = centred(key_list[1], (LAYERS, D, H * HD), D ** -0.5, 0.1875, ((1, 2), (2, 4)), jnp.float32)
    key_weight = centred(key_list[2], (LAYERS, D, H * HD), D ** -0.5, 0.1875, ((1, 2), (2, 4)), jnp.float32)
    value_weight = centred(key_list[3], (LAYERS, D, H * HD), D ** -0.5, 0.1875, ((1, 2), (2, 4)), jnp.float32)
    attention_weight = centred(key_list[4], (LAYERS, H * HD, D), (max(1, H * HD // 512)) ** -0.5, 4.0, ((1, 4), (2, 2)), jnp.float32)
    lookup_weight = centred(key_list[5], (LAYERS, D, MH * 2 * HALF), D ** -0.5, 0.1875, ((1, 2), (2, 4)), jnp.float32)
    gate_weight = centred(key_list[6], (LAYERS, D, D), D ** -0.5, 0.1875, ((1, 2), (2, 4)), jnp.float32)
    memory_weight = centred(key_list[7], (LAYERS, D, D), (D // 16) ** -0.5, 0.75, ((1, 4), (2, 2)), jnp.float32)
    first_table = centred(key_list[8], (LAYERS, MH, NSUB, HALF), (8 * HALF) ** -0.5, 0.25, ((1, 4), (2, 2)), jnp.float32)
    second_table = centred(key_list[9], (LAYERS, MH, NSUB, HALF), (8 * HALF) ** -0.5, 0.25, ((1, 4), (2, 2)), jnp.float32)
    attention_gain = jnp.clip(1.0 + 0.1 * jax.random.normal(key_list[10], (LAYERS, D), jnp.float32), 0.5, 1.5)
    memory_gain = jnp.clip(1.0 + 0.1 * jax.random.normal(key_list[11], (LAYERS, D), jnp.float32), 0.5, 1.5)
    memory_values = centred(key_list[12], (LAYERS, MROWS, D), 1.0, 6.0, ((1, 32),))
    blocks = jax.vmap(lambda own: jnp.searchsorted(jnp.cumsum(ragged(own, LEN // BLOCK, LEN, 2 * BLOCK, 0)), jnp.arange(LEN), side="right"))(jax.random.split(key_list[13], SEQS)).reshape((SEQS, LEN)).astype(jnp.int32)
    first_picks_keys = jax.random.split(jax.random.fold_in(key_list[14], 1), LAYERS * SEQS * MH * LEN // TOK_DEV)
    first_picks_turns = jax.random.permutation(jax.random.fold_in(key_list[14], 3), LAYERS * SEQS * MH * LEN // TOK_DEV)
    first_picks = jax.vmap(lambda own, number: deal_out(jax.random.fold_in(key_list[14], 2), own, number, TOK_DEV, NSUB, NF, CAP, 1))(first_picks_keys, first_picks_turns).reshape((LAYERS, SEQS, MH, LEN, NF))
    second_picks = different_ones(key_list[15], LAYERS * SEQS * MH * LEN * NF, NSUB, NS, 0).reshape((LAYERS, SEQS, MH, LEN, NF, NS))
    cotangent = centred(key_list[16], (SEQS, LEN, D), 1.0, 6.0, ((0, 2), (1, 4)))
    return dict(inputs=inputs, query_weight=query_weight, key_weight=key_weight, value_weight=value_weight, attention_weight=attention_weight, lookup_weight=lookup_weight, gate_weight=gate_weight, memory_weight=memory_weight, first_table=first_table, second_table=second_table, attention_gain=attention_gain, memory_gain=memory_gain, memory_values=memory_values, blocks=blocks, first_picks=first_picks, second_picks=second_picks, cotangent=cotangent)


highest = lax.Precision.HIGHEST
norm_eps = 1e-05
neg_fill = -1e+30

@jax.custom_vjp
def low(v):
    return lax.optimization_barrier(v.astype(jnp.bfloat16)).astype(jnp.float32)

@jax.custom_vjp
def low_back(v):
    return v

def low_keep(v):
    return (low(v), None)

def low_pass(kept, grad):
    return (grad,)

def back_keep(v):
    return (v, None)

def back_low(kept, grad):
    return (low(grad),)
low.defvjp(low_keep, low_pass)
low_back.defvjp(back_keep, back_low)

def matmul(left_side, right_side):
    return jnp.dot(left_side, right_side, precision=highest, preferred_element_type=jnp.float32)

def rms_norm(hidden, gain_row):
    factor = lax.rsqrt(lax.optimization_barrier(jnp.mean(hidden * hidden, axis=-1, keepdims=True)) + norm_eps)
    return hidden * factor * gain_row

def head_attention(visible, operands):
    queries, key_rows, value_rows = operands
    scores = low_back(matmul(queries, key_rows.T) * HD ** (-0.5))
    scores = jnp.where(visible, scores, neg_fill)
    weights = low(jax.nn.softmax(scores, axis=-1))
    return matmul(weights, value_rows)

def read_memory(value_table, operands):
    weights, row_ids = operands
    fetched = value_table[row_ids]
    pieces = low(jnp.einsum('thab,thabd->thad', weights, fetched, precision=highest))
    return low_back(lax.optimization_barrier(jnp.sum(pieces, axis=2)))

def one_layer(hidden, params, block_ids, first_ids, second_ids):
    query_weight, key_weight, value_weight, attention_weight, lookup_weight, gate_weight, memory_weight, first_table, second_table, attention_gain, memory_gain, value_table = params
    length = hidden.shape[0]
    normed = low(rms_norm(hidden, attention_gain))
    queries = low_back(low(matmul(normed, query_weight))).reshape(length, H, HD)
    key_rows = low_back(low(matmul(normed, key_weight))).reshape(length, H, HD)
    value_rows = low_back(low(matmul(normed, value_weight))).reshape(length, H, HD)
    visible = block_ids[None, :] <= block_ids[:, None]
    attended = lax.map(jax.checkpoint(partial(head_attention, visible)), (jnp.transpose(queries, (1, 0, 2)), jnp.transpose(key_rows, (1, 0, 2)), jnp.transpose(value_rows, (1, 0, 2))))
    mixed_heads = low_back(low(jnp.transpose(attended, (1, 0, 2)).reshape(length, D)))
    middle = hidden + low_back(matmul(mixed_heads, attention_weight))
    normed_two = low(rms_norm(middle, memory_gain))
    lookups = low_back(low(matmul(normed_two, lookup_weight))).reshape(length, MH, 2, HALF)
    score_first = low_back(jnp.einsum('thd,hjd->thj', lookups[:, :, 0], first_table, precision=highest))
    score_second = low_back(jnp.einsum('thd,hjd->thj', lookups[:, :, 1], second_table, precision=highest))
    first_ids = jnp.transpose(first_ids, (1, 0, 2))
    second_ids = jnp.transpose(second_ids, (1, 0, 2, 3))
    picked_first = jnp.take_along_axis(score_first, first_ids, axis=2)
    picked_second = jnp.take_along_axis(score_second, second_ids.reshape(length, MH, NF * NS), axis=2)
    picked_second = picked_second.reshape(length, MH, NF, NS)
    logits = (picked_first[..., None] + picked_second).reshape(length, MH, NF * NS)
    weights = low(jax.nn.softmax(logits, axis=-1)).reshape(length, MH, NF, NS)
    row_ids = first_ids[..., None] * NSUB + second_ids
    span_rows = min(128, length)
    blocks_in = length // span_rows
    head_memory = lax.map(jax.checkpoint(partial(read_memory, value_table)), (weights.reshape(blocks_in, span_rows, MH, NF, NS), row_ids.reshape(blocks_in, span_rows, MH, NF, NS)))
    memory = lax.optimization_barrier(jnp.sum(head_memory.reshape(length, MH, D), axis=1))
    gate_values = low_back(matmul(normed_two, gate_weight))
    gated_rows = low(memory * jax.nn.silu(gate_values))
    return middle + low_back(matmul(gated_rows, memory_weight))

def forward(hidden, query_weight, key_weight, value_weight, attention_weight, lookup_weight, gate_weight, memory_weight, first_table, second_table, attention_gain, memory_gain, memory_values, blocks, first_picks, second_picks):
    layer_params = []
    for layer_index in range(LAYERS):
        layer_params.append(tuple((low(master[layer_index]) for master in (query_weight, key_weight, value_weight, attention_weight, lookup_weight, gate_weight, memory_weight, first_table, second_table, attention_gain, memory_gain, memory_values))))

    def run_sequence(carried, operands):
        sequence, block_ids, first_ids, second_ids = operands
        for layer_index in range(LAYERS):
            sequence = one_layer(sequence, layer_params[layer_index], block_ids, first_ids[layer_index], second_ids[layer_index])
        return (carried, sequence)
    unused, result = lax.scan(jax.checkpoint(run_sequence), jnp.zeros((), jnp.float32), (hidden, blocks, jnp.moveaxis(first_picks, 1, 0), jnp.moveaxis(second_picks, 1, 0)))
    return result

def reference(inputs, query_weight, key_weight, value_weight, attention_weight, lookup_weight, gate_weight, memory_weight, first_table, second_table, attention_gain, memory_gain, memory_values, blocks, first_picks, second_picks, cotangent):

    def wrapped(hidden, *masters):
        return forward(hidden, *masters, blocks, first_picks, second_picks)
    result, pullback = jax.vjp(wrapped, inputs.astype(jnp.float32), query_weight, key_weight, value_weight, attention_weight, lookup_weight, gate_weight, memory_weight, first_table, second_table, attention_gain, memory_gain, memory_values.astype(jnp.float32))
    gradients = pullback(cotangent.astype(jnp.float32))
    return (result.astype(jnp.bfloat16), gradients[0], gradients[1], gradients[2], gradients[3], gradients[4], gradients[5], gradients[6], gradients[7], gradients[8], gradients[9], gradients[10], gradients[11], gradients[12])
```

```python
import functools

import jax
import jax.numpy as jnp
from jax import lax
from jax.experimental import pallas as pl
from jax.experimental.pallas import tpu as pltpu
from jax.sharding import PartitionSpec as P

HD = 64
NSUB = 256
CAP = 8
EPS = 1e-05
NEG = -1e30
f32 = jnp.float32
bf16 = jnp.bfloat16
MIB = 1 << 20


def dot(a, b):
    return jnp.dot(a, b, preferred_element_type=f32)


def dot_nt(a, b):
    return lax.dot_general(a, b, (((1,), (1,)), ((), ())), preferred_element_type=f32)


def dot_tn(a, b):
    return lax.dot_general(a, b, (((0,), (0,)), ((), ())), preferred_element_type=f32)


def swap(x, axis, step):
    size = lax.axis_size(axis)
    return lax.ppermute(x, axis, [(i, i ^ step) for i in range(size)])


def swaps(xs, axis):
    return [xs[0]] + [swap(xs[d], axis, d) for d in range(1, len(xs))]


def spread(x, axis):
    return [x] + [swap(x, axis, d) for d in range(1, lax.axis_size(axis))]


def shape(dims, dtype):
    return jax.ShapeDtypeStruct(dims, dtype)


def kernel_call(body, name, outs, idx, args, scratch=(), limit=32, flops=0):
    in_specs = [pl.BlockSpec(memory_space=pltpu.SMEM)]
    in_specs += [pl.BlockSpec(memory_space=pltpu.VMEM) for _ in args]
    moved = sum(a.size * a.dtype.itemsize for a in args)
    moved += sum(o.size * o.dtype.itemsize for o in outs)
    return pl.pallas_call(
        body,
        out_shape=outs,
        in_specs=in_specs,
        out_specs=[pl.BlockSpec(memory_space=pltpu.VMEM) for _ in outs],
        scratch_shapes=list(scratch),
        compiler_params=pltpu.CompilerParams(vmem_limit_bytes=limit * MIB),
        cost_estimate=pl.CostEstimate(flops=flops, bytes_accessed=moved, transcendentals=0),
        name=name,
    )(idx, *args)


def rows_at(index, count):
    return pl.ds(pl.multiple_of(index * count, count), count)


def rms(x, gain):
    factor = lax.rsqrt(jnp.mean(x * x, axis=1, keepdims=True) + EPS)
    return factor, x * factor * gain


def rms_back(x, factor, gain, upstream):
    scaled = upstream * gain
    return factor * scaled - x * factor**3 * jnp.mean(scaled * x, axis=1, keepdims=True)


def total4(refs):
    return (refs[0][...].astype(f32) + refs[1][...].astype(f32)) + (
        refs[2][...].astype(f32) + refs[3][...].astype(f32)
    )


def fold(x):
    half = x.shape[0] // 2
    return jnp.concatenate([x[:half], x[half:]], axis=1)


def unfold(x):
    half = x.shape[1] // 2
    return jnp.concatenate([x[:, :half], x[:, half:]], axis=0)


class Plan:
    def __init__(self, SA, TA):
        self.SA, self.TA = SA, TA
        self.si = 1 if SA == "ctx" else 2
        self.ti = 1 if TA == "ctx" else 2

    def src(self, sa, ta):
        return sa * 4 + ta if self.SA == "ctx" else ta * 4 + sa

    def rel(self, ds, dt):
        return (ds, dt) if self.SA == "ctx" else (dt, ds)


PLAN = Plan("ctx", "tp")


def slots_kernel(idx, first_ref, second_ref, slot_ref, out_ref, gbits, dbits):
    tokens = first_ref.shape[1]
    picks = first_ref.shape[0]
    lanes = out_ref.shape[0] * out_ref.shape[2]
    iota = lax.broadcasted_iota(jnp.int32, (NSUB, tokens), 0)
    onehot = jnp.zeros((NSUB, tokens), f32)
    for i in range(picks):
        onehot = jnp.where(iota == first_ref[i : i + 1, :], 1.0, onehot)
    before = lax.broadcasted_iota(jnp.int32, (tokens, tokens), 0) < lax.broadcasted_iota(
        jnp.int32, (tokens, tokens), 1
    )
    counts = dot(onehot.astype(bf16), jnp.where(before, 1.0, 0.0).astype(bf16))
    row = lax.broadcasted_iota(jnp.int32, (lanes, tokens), 0)
    token_row = (lax.broadcasted_iota(jnp.int32, (8, tokens), 1) + 1).astype(f32)
    token_row = jnp.where(
        lax.broadcasted_iota(jnp.int32, (8, tokens), 0) == 0, token_row, 0.0
    )
    total = jnp.zeros((16, lanes), f32)
    for i in range(picks):
        first = first_ref[i : i + 1, :]
        rank = jnp.sum(jnp.where(iota == first, counts, 0.0), axis=0, keepdims=True)
        shard = lax.shift_right_logical(first, gbits)
        group = lax.shift_right_logical(shard, dbits) * (1 << gbits) + (first & ((1 << gbits) - 1))
        slot = (shard & ((1 << dbits) - 1)) * out_ref.shape[2] + group * CAP + rank.astype(jnp.int32)
        slot_ref[i : i + 1, :] = slot
        names = jnp.concatenate([second_ref[8 * i : 8 * i + 8, :].astype(f32), token_row], axis=0)
        hit = jnp.where(row == slot, 1.0, 0.0).astype(bf16)
        total = total + dot_nt(names.astype(bf16), hit)
    for d in range(out_ref.shape[0]):
        out_ref[d] = total[:, d * out_ref.shape[2] : (d + 1) * out_ref.shape[2]].astype(bf16)


def emit_heads(h, w_ref, pack, outs, s):
    width = w_ref.shape[1] // 3
    qkv = dot(h, w_ref[...]).astype(bf16)
    for j in range(4):
        q = qkv[:, HD * j : HD * (j + 1)]
        k = qkv[:, width + HD * j : width + HD * (j + 1)]
        v = qkv[:, 2 * width + HD * j : 2 * width + HD * (j + 1)]
        pack[j] = jnp.concatenate([jnp.concatenate([q, k], axis=1), fold(v)], axis=0)
    for d in range(4):
        outs[d][...] = pack[s ^ d]


def qkv_first_kernel(idx, x_ref, gain_ref, w_ref, h_ref, e0, e1, e2, e3, pack, plan, row):
    _, normed = rms(x_ref[...].astype(f32), gain_ref[row : row + 1, :])
    h = normed.astype(bf16)
    h_ref[...] = h
    emit_heads(h, w_ref, pack, (e0, e1, e2, e3), idx[plan.si])


def place_chunks(refs, full, t):
    count = refs[0].shape[0]
    for d in range(4):
        full[rows_at(t ^ d, count), :] = refs[d][...]


def qkv_kernel(idx, h0, h1, h2, h3, w_ref, h_ref, e0, e1, e2, e3, pack, plan):
    place_chunks((h0, h1, h2, h3), h_ref, idx[plan.ti])
    emit_heads(h_ref[...], w_ref, pack, (e0, e1, e2, e3), idx[plan.si])


def load_heads(es, kk, vv):
    for d in range(4):
        rows = es[d].shape[0] * 2 // 3
        kk[rows * d : rows * (d + 1), :] = es[d][0:rows, HD : 2 * HD]
        vv[rows * d : rows * (d + 1), :] = unfold(es[d][rows:, :])


def load_ids(col_ref, ids_col, s):
    count = col_ref.shape[0] // 4
    for d in range(4):
        ids_col[count * d : count * (d + 1), :] = col_ref[rows_at(s ^ d, count), :]


def probabilities(kk, q, key_ids, query_ids):
    scores = dot_nt(kk, q) * (HD ** (-0.5))
    scores = jnp.where(key_ids <= query_ids, scores, NEG)
    top = jnp.max(scores, axis=0, keepdims=True)
    exponent = jnp.exp(scores - top)
    return exponent * (1.0 / jnp.sum(exponent, axis=0, keepdims=True))


def attend_kernel(idx, e0, e1, e2, e3, row_ref, col_ref, a0, a1, a2, a3, kk, vv, ids_col, plan):
    es, outs = (e0, e1, e2, e3), (a0, a1, a2, a3)
    s = idx[plan.si]
    load_heads(es, kk, vv)
    load_ids(col_ref, ids_col, s)
    count = kk.shape[0] // 4
    for d in range(4):
        query_ids = row_ref[:, rows_at(s ^ d, count)]
        p = probabilities(kk[...], es[d][0:count, 0:HD], ids_col[...], query_ids)
        blended = dot_tn(vv[...], p.astype(bf16))
        outs[d][...] = fold(blended.T.astype(bf16))


def attend_back_kernel(
    idx, e0, e1, e2, e3, u0, u1, u2, u3, row_ref, col_ref, g0, g1, g2, g3, kk, vv, ids_col, gk, gv, plan
):
    es, us, outs = (e0, e1, e2, e3), (u0, u1, u2, u3), (g0, g1, g2, g3)
    s = idx[plan.si]
    load_heads(es, kk, vv)
    load_ids(col_ref, ids_col, s)
    count = kk.shape[0] // 4
    scale = HD ** (-0.5)
    for d in range(4):
        query_ids = row_ref[:, rows_at(s ^ d, count)]
        q = es[d][0:count, 0:HD]
        up = unfold(us[d][...])
        p = probabilities(kk[...], q, ids_col[...], query_ids)
        gp = dot_nt(vv[...], up)
        centre = jnp.sum(p * gp, axis=0, keepdims=True)
        gs = (p * (gp - centre)).astype(bf16)
        gq = (dot_tn(kk[...], gs) * scale).T.astype(bf16)
        outs[d][0:count, 0:HD] = gq
        key_term = dot(gs, q)
        value_term = dot(p.astype(bf16), up)
        if d == 0:
            gk[...] = key_term
            gv[...] = value_term
        else:
            gk[...] += key_term
            gv[...] += value_term
    for d in range(4):
        outs[d][0:count, HD : 2 * HD] = (gk[count * d : count * (d + 1), :] * scale).astype(bf16)
        outs[d][count:, :] = fold(gv[count * d : count * (d + 1), :].astype(bf16))


def out_kernel(idx, a0, a1, a2, a3, w_ref, a_ref, p0, p1, p2, p3, heads, part, plan):
    s, t = idx[plan.si], idx[plan.ti]
    for d, a in enumerate((a0, a1, a2, a3)):
        heads[s ^ d] = unfold(a[...])
    a_ref[...] = jnp.concatenate([heads[j] for j in range(4)], axis=1)
    part[...] = dot(a_ref[...], w_ref[...]).astype(bf16)
    emit_chunks(part, (p0, p1, p2, p3), t)


def emit_chunks(part, outs, t):
    count = outs[0].shape[0]
    for d in range(4):
        outs[d][...] = part[rows_at(t ^ d, count), :]


def own_rows(ref, idx, plan, count):
    if ref.shape[0] == count:
        return ref[...].astype(f32)
    return ref[rows_at(idx[plan.ti], count), :].astype(f32)


def norm_kernel(idx, x_ref, p0, r1, r2, r3, gain_ref, x_out, h_out, plan, row):
    x = own_rows(x_ref, idx, plan, p0.shape[0]) + total4((p0, r1, r2, r3))
    x_out[...] = x
    _, normed = rms(x, gain_ref[row : row + 1, :])
    h_out[...] = normed.astype(bf16)


def last_kernel(idx, x_ref, p0, r1, r2, r3, out_ref, plan):
    x = own_rows(x_ref, idx, plan, p0.shape[0]) + total4((p0, r1, r2, r3))
    out_ref[...] = x.astype(bf16)


def norm_back_kernel(idx, p0, r1, r2, r3, x_ref, g_ref, gain_ref, gx_ref, round_ref, dgain_ref, plan, row):
    count = p0.shape[0]
    upstream = total4((p0, r1, r2, r3))
    x = own_rows(x_ref, idx, plan, count)
    gain = gain_ref[row : row + 1, :]
    factor, _ = rms(x, gain)
    dgain_ref[...] = jnp.sum(upstream * x * factor, axis=0, keepdims=True)
    gx = own_rows(g_ref, idx, plan, count) + rms_back(x, factor, gain, upstream)
    gx_ref[...] = gx
    round_ref[...] = gx.astype(bf16)


def lookup_kernel(
    idx, h0, h1, h2, h3, wm_ref, ka_ref, kb_ref, first_ref, second_ref, slot_ref, h_ref, u_ref, w_ref, out_ref, plan
):
    place_chunks((h0, h1, h2, h3), h_ref, idx[plan.ti])
    u = dot(h_ref[...], wm_ref[...]).astype(bf16)
    u_ref[...] = u
    half = u.shape[1] // 2
    c1 = dot_nt(ka_ref[...], u[:, :half])
    c2 = dot_nt(kb_ref[...], u[:, half:])
    tokens = u.shape[0]
    picks = first_ref.shape[0]
    inner = second_ref.shape[0] // picks
    iota = lax.broadcasted_iota(jnp.int32, (NSUB, tokens), 0)
    for i in range(picks):
        base = jnp.sum(jnp.where(iota == first_ref[i : i + 1, :], c1, 0.0), axis=0, keepdims=True)
        for b in range(inner):
            r = i * inner + b
            picked = jnp.sum(
                jnp.where(iota == second_ref[r : r + 1, :], c2, 0.0), axis=0, keepdims=True
            )
            w_ref[r : r + 1, :] = base + picked
    logits = w_ref[...]
    exponent = jnp.exp(logits - jnp.max(logits, axis=0, keepdims=True))
    w = exponent * (1.0 / jnp.sum(exponent, axis=0, keepdims=True))
    w_ref[...] = w
    lanes = out_ref.shape[0] * out_ref.shape[2]
    row = lax.broadcasted_iota(jnp.int32, (lanes, tokens), 0)
    total = jnp.zeros((inner, lanes), f32)
    for i in range(picks):
        hit = jnp.where(row == slot_ref[i : i + 1, :], 1.0, 0.0).astype(bf16)
        total = total + dot_nt(w[inner * i : inner * (i + 1), :].astype(bf16), hit)
    for d in range(out_ref.shape[0]):
        out_ref[d] = total[:, d * out_ref.shape[2] : (d + 1) * out_ref.shape[2]]


def gate_kernel(idx, m0, m1, m2, m3, z1, z2, z3, gate_ref, w_ref, mem_ref, z_ref, p0, p1, p2, p3, part, plan):
    mem = total4((m0, m1, m2, m3)) + z1[...].astype(f32) + z2[...].astype(f32) + z3[...].astype(f32)
    mem_ref[...] = mem
    gate = gate_ref[...]
    z = (mem * (gate * jax.nn.sigmoid(gate))).astype(bf16)
    z_ref[...] = z
    part[...] = dot(z, w_ref[...]).astype(bf16)
    emit_chunks(part, (p0, p1, p2, p3), idx[plan.ti])


def gate_back(gy, w_ref, gate_ref, mem_ref, gn_ref, gg_ref):
    gz = dot_nt(gy, w_ref[...])
    gate = gate_ref[...]
    sigmoid = jax.nn.sigmoid(gate)
    gn_ref[...] = (gz * (gate * sigmoid)).astype(bf16)
    gg_ref[...] = (gz * mem_ref[...] * (sigmoid * (1.0 + gate * (1.0 - sigmoid)))).astype(bf16)


def gate_back_full_kernel(idx, gy_ref, w_ref, gate_ref, mem_ref, gn_ref, gg_ref):
    gate_back(gy_ref[...], w_ref, gate_ref, mem_ref, gn_ref, gg_ref)


def gate_back_kernel(idx, g0, g1, g2, g3, w_ref, gate_ref, mem_ref, gy_ref, gn_ref, gg_ref, plan):
    place_chunks((g0, g1, g2, g3), gy_ref, idx[plan.ti])
    gate_back(gy_ref[...], w_ref, gate_ref, mem_ref, gn_ref, gg_ref)


def lookup_back_kernel(
    idx, gw_ref, slot_ref, w_ref, first_ref, second_ref, ka_ref, kb_ref, u_ref, gg_ref, wg_ref, wm_ref,
    p0, p1, p2, p3, gu_ref, dka_ref, dkb_ref, gl, part, plan,
):
    tokens = u_ref.shape[0]
    picks = first_ref.shape[0]
    inner = second_ref.shape[0] // picks
    owners, _, width = gw_ref.shape
    row = lax.broadcasted_iota(jnp.int32, (owners * width, tokens), 0)
    arrived = jnp.concatenate([gw_ref[d] for d in range(owners)], axis=1).astype(bf16)
    for i in range(picks):
        hit = jnp.where(row == slot_ref[i : i + 1, :], 1.0, 0.0).astype(bf16)
        gl[inner * i : inner * (i + 1), :] = dot(arrived, hit)
    w = w_ref[...]
    gw = gl[...]
    gl[...] = w * (gw - jnp.sum(w * gw, axis=0, keepdims=True))
    iota = lax.broadcasted_iota(jnp.int32, (NSUB, tokens), 0)
    gc1 = jnp.zeros((NSUB, tokens), f32)
    gc2 = jnp.zeros((NSUB, tokens), f32)
    for i in range(picks):
        both = jnp.sum(gl[inner * i : inner * (i + 1), :], axis=0, keepdims=True)
        gc1 = jnp.where(iota == first_ref[i : i + 1, :], both, gc1)
        for b in range(inner):
            r = i * inner + b
            gc2 = gc2 + jnp.where(iota == second_ref[r : r + 1, :], gl[r : r + 1, :], 0.0)
    gc1 = gc1.astype(bf16)
    gc2 = gc2.astype(bf16)
    half = u_ref.shape[1] // 2
    gu = jnp.concatenate([dot_tn(gc1, ka_ref[...]), dot_tn(gc2, kb_ref[...])], axis=1).astype(bf16)
    gu_ref[...] = gu
    dka_ref[...] = dot(gc1, u_ref[:, :half]).astype(bf16)
    dkb_ref[...] = dot(gc2, u_ref[:, half:]).astype(bf16)
    part[...] = (dot_nt(gg_ref[...], wg_ref[...]) + dot_nt(gu, wm_ref[...])).astype(bf16)
    emit_chunks(part, (p0, p1, p2, p3), idx[plan.ti])


def read_kernel(idx, w_ref, names_ref, v_ref, o0, o1, o2, o3, s_ref, pieces, rows, plan):
    step = pl.program_id(0)
    sources, _, width = w_ref.shape

    @pl.when(step == 0)
    def _():
        iota = lax.broadcasted_iota(jnp.int32, (NSUB, width), 0).astype(f32)

        def build(src, carry):
            names = names_ref[src].astype(f32)
            weights = w_ref[src]
            dense = jnp.zeros((NSUB, width), f32)
            for b in range(8):
                dense = jnp.where(iota == names[b : b + 1, :], weights[b : b + 1, :], dense)
            s_ref[src] = dense.T
            return carry

        lax.fori_loop(0, sources, build, 0)

    at = rows_at(step, CAP)
    left = s_ref[:, at, :].reshape(sources * CAP, NSUB).astype(bf16)
    pieces[:, at, :] = dot(left, v_ref[...]).reshape(sources, CAP, v_ref.shape[1])

    @pl.when(step == pl.num_programs(0) - 1)
    def _():
        s, t = idx[plan.si], idx[plan.ti]
        tokens = rows.shape[0]
        quarter = o0.shape[1]
        outs = (o0, o1, o2, o3)
        iota = (lax.broadcasted_iota(jnp.int32, (tokens, width), 0) + 1).astype(f32)
        for ds in range(4):
            hits, parts = [], []
            for ta in range(4):
                src = plan.src(s ^ ds, ta)
                token = names_ref[src].astype(f32)[8:9, :]
                hits.append(jnp.where(iota == token, 1.0, 0.0).astype(bf16))
                parts.append(pieces[src].astype(bf16))
            rows[...] = dot(
                jnp.concatenate(hits, axis=1), jnp.concatenate(parts, axis=0)
            ).astype(bf16)
            for dt in range(4):
                dp, dz = plan.rel(ds, dt)
                outs[dp][tokens * dz : tokens * (dz + 1), :] = rows[:, rows_at(t ^ dt, quarter)]


def read_call(idx, weights, names, layer, values, plan, tokens):
    sources, inner, width = weights.shape
    steps = width // CAP
    d_model = values.shape[2]
    quarter = d_model // 4
    out = shape((4 * tokens, quarter), bf16)
    return pl.pallas_call(
        functools.partial(read_kernel, plan=plan),
        grid=(steps,),
        out_shape=[out, out, out, out, shape((sources, width, NSUB), f32)],
        in_specs=[
            pl.BlockSpec(memory_space=pltpu.SMEM),
            pl.BlockSpec((sources, inner, width), lambda g: (0, 0, 0)),
            pl.BlockSpec((sources, 16, width), lambda g: (0, layer, 0)),
            pl.BlockSpec((None, NSUB, d_model), lambda g: (layer, g, 0)),
        ],
        out_specs=[pl.BlockSpec((4 * tokens, quarter), lambda g: (0, 0)) for _ in range(4)]
        + [pl.BlockSpec((sources, width, NSUB), lambda g: (0, 0, 0))],
        scratch_shapes=[
            pltpu.VMEM((sources, width, d_model), f32),
            pltpu.VMEM((tokens, d_model), bf16),
        ],
        compiler_params=pltpu.CompilerParams(vmem_limit_bytes=48 * MIB),
        cost_estimate=pl.CostEstimate(
            flops=4 * sources * width * NSUB * d_model, bytes_accessed=20 * MIB, transcendentals=0
        ),
        name="memory_read",
    )(idx, weights, names, values)


def write_kernel(
    idx, g0, g1, g2, g3, names_ref, s_ref, v_ref, dv_ref, gw_ref, grads, pieces, cross, plan
):
    step = pl.program_id(0)
    sources, width, _ = s_ref.shape
    d_model = v_ref.shape[1]

    @pl.when(step == 0)
    def _():
        s, t = idx[plan.si], idx[plan.ti]
        tokens = grads.shape[1]
        quarter = g0.shape[1]
        for dp, g in enumerate((g0, g1, g2, g3)):
            for dz in range(4):
                ds, dt = plan.rel(dp, dz)
                grads[s ^ ds, :, rows_at(t ^ dt, quarter)] = g[tokens * dz : tokens * (dz + 1), :]
        iota = (lax.broadcasted_iota(jnp.int32, (tokens, width), 0) + 1).astype(f32)
        for sa in range(4):
            for ta in range(4):
                src = plan.src(sa, ta)
                token = names_ref[src].astype(f32)[8:9, :]
                hit = jnp.where(iota == token, 1.0, 0.0).astype(bf16)
                pieces[src] = dot_tn(hit, grads[sa])

    at = rows_at(step, CAP)
    inbox = pieces[:, at, :].reshape(sources * CAP, d_model).astype(bf16)
    left = s_ref[:, at, :].reshape(sources * CAP, NSUB).astype(bf16)
    dv_ref[...] = dot_tn(left, inbox).astype(bf16)
    cross[:, at, :] = dot_nt(inbox, v_ref[...]).reshape(sources, CAP, NSUB)

    @pl.when(step == pl.num_programs(0) - 1)
    def _():
        iota = lax.broadcasted_iota(jnp.int32, (NSUB, width), 0).astype(f32)

        def select(src, carry):
            turned = cross[src].T
            names = names_ref[src].astype(f32)
            picked = [
                jnp.sum(jnp.where(iota == names[b : b + 1, :], turned, 0.0), axis=0, keepdims=True)
                for b in range(8)
            ]
            gw_ref[src] = jnp.concatenate(picked, axis=0)
            return carry

        lax.fori_loop(0, sources, select, 0)


def write_call(idx, grads, names, layer, dense, values, plan, tokens):
    sources, width, _ = dense.shape
    steps = width // CAP
    d_model = values.shape[2]
    quarter = d_model // 4
    return pl.pallas_call(
        functools.partial(write_kernel, plan=plan),
        grid=(steps,),
        out_shape=[shape((values.shape[1], d_model), bf16), shape((sources, 8, width), f32)],
        in_specs=[pl.BlockSpec(memory_space=pltpu.SMEM)]
        + [pl.BlockSpec((4 * tokens, quarter), lambda g: (0, 0)) for _ in range(4)]
        + [
            pl.BlockSpec((sources, 16, width), lambda g: (0, layer, 0)),
            pl.BlockSpec((sources, width, NSUB), lambda g: (0, 0, 0)),
            pl.BlockSpec((None, NSUB, d_model), lambda g: (layer, g, 0)),
        ],
        out_specs=[
            pl.BlockSpec((NSUB, d_model), lambda g: (g, 0)),
            pl.BlockSpec((sources, 8, width), lambda g: (0, 0, 0)),
        ],
        scratch_shapes=[
            pltpu.VMEM((4, tokens, d_model), bf16),
            pltpu.VMEM((sources, width, d_model), f32),
            pltpu.VMEM((sources, width, NSUB), f32),
        ],
        compiler_params=pltpu.CompilerParams(vmem_limit_bytes=48 * MIB),
        cost_estimate=pl.CostEstimate(
            flops=6 * sources * width * NSUB * d_model, bytes_accessed=28 * MIB, transcendentals=0
        ),
        name="memory_write",
    )(idx, *grads, names, dense, values)


def sum_kernel(idx, m0, r1, r2, r3, o0, o1, o2, o3):
    count = o0.shape[0]
    for dz, out in enumerate((o0, o1, o2, o3)):
        at = slice(count * dz, count * (dz + 1))
        out[...] = (
            (m0[at, :].astype(f32) + r1[at, :].astype(f32))
            + (r2[at, :].astype(f32) + r3[at, :].astype(f32))
        ).astype(bf16)


def gather_shards(x, axis):
    if lax.axis_size("fsdp") != 2:
        return lax.all_gather(x, "fsdp", axis=axis, tiled=True)
    other = swap(x, "fsdp", 1)
    mine = lax.axis_index("fsdp") == 0
    return jnp.where(
        mine, jnp.concatenate([x, other], axis=axis), jnp.concatenate([other, x], axis=axis)
    )


def body(
    inputs,
    query_weight,
    key_weight,
    value_weight,
    attention_weight,
    lookup_weight,
    gate_weight,
    memory_weight,
    first_table,
    second_table,
    attention_gain,
    memory_gain,
    memory_values,
    blocks,
    first_picks,
    second_picks,
    cotangent,
):
    plan = PLAN
    SA, TA = plan.SA, plan.TA
    layers = query_weight.shape[0]
    tokens = inputs.shape[1]
    d_model = inputs.shape[2]
    chunk = tokens // 4
    width = query_weight.shape[2]
    shards = lax.axis_size("fsdp")
    owners = lax.axis_size("ctx") * lax.axis_size("tp")
    groups = memory_values.shape[1] // NSUB
    lanes = shards * groups * CAP
    gbits = groups.bit_length() - 1
    dbits = owners.bit_length() - 1
    idx = jnp.stack(
        [lax.axis_index("fsdp"), lax.axis_index("ctx"), lax.axis_index("tp"), 0]
    ).astype(jnp.int32)

    gains = gather_shards(jnp.concatenate([attention_gain, memory_gain], axis=0).astype(bf16), 1)
    gains = gains.astype(f32)
    w_qkv, w_o, w_gate, w_look, w_mem, tab_a, tab_b = [], [], [], [], [], [], []
    for l in range(layers):
        w_qkv.append(
            gather_shards(
                jnp.concatenate([query_weight[l], key_weight[l], value_weight[l]], axis=1).astype(bf16), 0
            )
        )
        w_o.append(gather_shards(attention_weight[l].astype(bf16), 1))
        w_look.append(gather_shards(lookup_weight[l].astype(bf16), 0))
        tables = gather_shards(
            jnp.concatenate([first_table[l, 0], second_table[l, 0]], axis=1).astype(bf16), 0
        )
        tab_a.append(tables[:, :HD])
        tab_b.append(tables[:, HD:])
        w_gate.append(gather_shards(gate_weight[l].astype(bf16), 0))
        w_mem.append(gather_shards(memory_weight[l].astype(bf16), 1))
    values = lax.all_gather(memory_values, "fsdp", axis=1, tiled=True)

    ids_row = blocks
    ids_col = blocks.reshape(-1, 1)
    firsts = [first_picks[l, 0, 0].T for l in range(layers)]
    seconds = [second_picks[l, 0, 0].reshape(tokens, -1).T for l in range(layers)]
    picks = first_picks.shape[4]
    slots, names = [], []
    for l in range(layers):
        slot, name = kernel_call(
            functools.partial(slots_kernel, gbits=gbits, dbits=dbits),
            "pick_slots",
            [shape((picks, tokens), jnp.int32), shape((owners, 16, lanes), bf16)],
            idx,
            [firsts[l], seconds[l]],
        )
        slots.append(slot)
        names.append(name)
    names = lax.all_to_all(jnp.concatenate(names, axis=1), ("ctx", "tp"), 0, 0, tiled=True)

    heads_shape = shape((tokens * 3 // 2, 2 * HD), bf16)
    folded = shape((tokens // 2, 2 * HD), bf16)
    part_shape = shape((chunk, d_model), bf16)
    chunk_shape = shape((chunk, d_model), f32)
    full_shape = shape((tokens, d_model), bf16)
    pack_scratch = pltpu.VMEM((4, tokens * 3 // 2, 2 * HD), bf16)
    part_scratch = pltpu.VMEM((tokens, d_model), bf16)
    kv_scratch = [
        pltpu.VMEM((4 * tokens, HD), bf16),
        pltpu.VMEM((4 * tokens, HD), bf16),
        pltpu.VMEM((4 * tokens, 1), jnp.int32),
    ]
    x = inputs[0]
    h_chunk = None
    kept = []
    for l in range(layers):
        if l == 0:
            h1, *es = kernel_call(
                functools.partial(qkv_first_kernel, plan=plan, row=l),
                "qkv_first",
                [full_shape] + [heads_shape] * 4,
                idx,
                [x, gains, w_qkv[l]],
                [pack_scratch],
            )
        else:
            h1, *es = kernel_call(
                functools.partial(qkv_kernel, plan=plan),
                "qkv",
                [full_shape] + [heads_shape] * 4,
                idx,
                [*spread(h_chunk, TA), w_qkv[l]],
                [pack_scratch],
            )
        es = swaps(es, SA)
        heads = kernel_call(
            functools.partial(attend_kernel, plan=plan),
            "attend",
            [folded] * 4,
            idx,
            [*es, ids_row, ids_col],
            kv_scratch,
        )
        attended, *parts = kernel_call(
            functools.partial(out_kernel, plan=plan),
            "attend_out",
            [shape((tokens, width), bf16)] + [part_shape] * 4,
            idx,
            [*swaps(heads, SA), w_o[l]],
            [pltpu.VMEM((4, tokens, HD), bf16), part_scratch],
        )
        middle, h_chunk = kernel_call(
            functools.partial(norm_kernel, plan=plan, row=layers + l),
            "norm_mid",
            [chunk_shape, part_shape],
            idx,
            [x, *swaps(parts, TA), gains],
        )
        h2, u, w, outbox = kernel_call(
            functools.partial(lookup_kernel, plan=plan),
            "lookup",
            [
                full_shape,
                shape((tokens, w_look[l].shape[1]), bf16),
                shape(seconds[l].shape, f32),
                shape((owners, 8, lanes), f32),
            ],
            idx,
            [*spread(h_chunk, TA), w_look[l], tab_a[l], tab_b[l], firsts[l], seconds[l], slots[l]],
        )
        weights = lax.all_to_all(outbox, ("ctx", "tp"), 0, 0, tiled=True)
        gate = dot(h2, w_gate[l])
        *reads, dense = read_call(idx, weights, names, l, values, plan, tokens)
        sums = kernel_call(
            sum_kernel,
            "memory_sum",
            [shape((tokens, width), bf16)] * 4,
            idx,
            swaps(reads, "ctx"),
        )
        first_sum, *rest = swaps(sums, "tp")
        mem, z, *parts = kernel_call(
            functools.partial(gate_sum_kernel, plan=plan),
            "gate",
            [shape((tokens, width), f32), shape((tokens, width), bf16)] + [part_shape] * 4,
            idx,
            [first_sum, *rest, gate, w_mem[l]],
            [part_scratch],
        )
        kept.append((x, h1, es, attended, middle, h2, u, w, gate, dense, mem, z))
        if l + 1 < layers:
            x, h_chunk = kernel_call(
                functools.partial(norm_kernel, plan=plan, row=l + 1),
                "norm_next",
                [chunk_shape, part_shape],
                idx,
                [middle, *swaps(parts, TA), gains],
            )
        else:
            (out_chunk,) = kernel_call(
                functools.partial(last_kernel, plan=plan),
                "last",
                [part_shape],
                idx,
                [middle, *swaps(parts, TA)],
            )
    output = lax.all_gather(out_chunk, TA, axis=0, tiled=True)[None]

    g = cotangent[0]
    gy_chunk = None
    grads = []
    table_grads = []
    fence = None
    for l in reversed(range(layers)):
        x, h1, es, attended, middle, h2, u, w, gate, dense, mem, z = kept[l]
        pair = [shape((tokens, width), bf16)] * 2
        if l == layers - 1:
            gy = g
            gn, gg = kernel_call(
                gate_back_full_kernel, "gate_back_first", pair, idx, [gy, w_mem[l], gate, mem]
            )
        else:
            gy, gn, gg = kernel_call(
                functools.partial(gate_back_kernel, plan=plan),
                "gate_back",
                [full_shape] + pair,
                idx,
                [*spread(gy_chunk, TA), w_mem[l], gate, mem],
            )
        d_mem = dot_tn(z, gy).astype(bf16)
        d_gate = dot_tn(h2, gg).astype(bf16)
        line = jnp.concatenate(spread(gn, "tp"), axis=0)
        dv, gw = write_call(idx, spread(line, "ctx"), names, l, dense, values, plan, tokens)
        table_grads.insert(0, lax.psum_scatter(dv, "fsdp", scatter_dimension=0, tiled=True))
        gw = lax.all_to_all(gw, ("ctx", "tp"), 0, 0, tiled=True)
        *parts, gu, d_first, d_second = kernel_call(
            functools.partial(lookup_back_kernel, plan=plan),
            "lookup_back",
            [part_shape] * 4
            + [shape(u.shape, bf16), shape((NSUB, HD), bf16), shape((NSUB, HD), bf16)],
            idx,
            [gw, slots[l], w, firsts[l], seconds[l], tab_a[l], tab_b[l], u, gg, w_gate[l], w_look[l]],
            [pltpu.VMEM(w.shape, f32), part_scratch],
        )
        d_look = dot_tn(h2, gu).astype(bf16)
        g_mid, go_chunk, d_gain_two = kernel_call(
            functools.partial(norm_back_kernel, plan=plan, row=layers + l),
            "norm_mid_back",
            [chunk_shape, part_shape, shape((1, d_model), f32)],
            idx,
            [*swaps(parts, TA), middle, g, gains],
        )
        go, *ups = kernel_call(
            functools.partial(out_back_kernel, plan=plan),
            "attend_out_back",
            [full_shape] + [folded] * 4,
            idx,
            [*spread(go_chunk, TA), w_o[l]],
            [pltpu.VMEM((4, tokens // 2, 2 * HD), bf16)],
        )
        d_out = dot_tn(attended, go).astype(bf16)
        head_grads = kernel_call(
            functools.partial(attend_back_kernel, plan=plan),
            "attend_back",
            [heads_shape] * 4,
            idx,
            [*es, *swaps(ups, SA), ids_row, ids_col],
            kv_scratch + [pltpu.VMEM((4 * tokens, HD), f32)] * 2,
        )
        g_qkv, *parts = kernel_call(
            functools.partial(qkv_back_kernel, plan=plan),
            "qkv_back",
            [shape((tokens, 3 * width), bf16)] + [part_shape] * 4,
            idx,
            [*swaps(head_grads, SA), w_qkv[l]],
            [pack_scratch, part_scratch],
        )
        d_qkv = dot_tn(h1, g_qkv).astype(bf16)
        g, gy_chunk, d_gain_one = kernel_call(
            functools.partial(norm_back_kernel, plan=plan, row=l),
            "norm_back",
            [chunk_shape, part_shape, shape((1, d_model), f32)],
            idx,
            [*swaps(parts, TA), x, g_mid, gains],
        )
        gain_rows = jnp.concatenate([d_gain_one, d_gain_two], axis=0)
        gain_rows = sum(spread(gain_rows, "tp")[1:], gain_rows)
        if lax.axis_size("tp") != 4:
            raise ValueError("tp")
        pieces = [
            (jnp.concatenate([d_qkv, d_gate, d_look], axis=1), 0),
            (jnp.concatenate([d_out, d_mem], axis=0), 1),
            (jnp.concatenate([d_first, d_second], axis=1), 0),
            (gain_rows.astype(bf16), 1),
        ]
        if fence is not None:
            fenced = lax.optimization_barrier(tuple(p for p, _ in pieces) + tuple(fence))
            pieces = [(q, axis) for q, (_, axis) in zip(fenced, pieces)]
            grads[0] = fenced[len(pieces) :]
        reduced = [
            lax.psum(lax.psum_scatter(p, "fsdp", scatter_dimension=axis, tiled=True), "ctx")
            for p, axis in pieces
        ]
        fence = reduced
        grads.insert(0, reduced)
    input_gradient = lax.all_gather(gy_chunk, TA, axis=0, tiled=True).astype(f32)[None]

    def stacked(pick):
        return jnp.stack([pick(*grads[l]).astype(f32) for l in range(layers)])

    return (
        output,
        input_gradient,
        stacked(lambda a, b, c, d: a[:, :width]),
        stacked(lambda a, b, c, d: a[:, width : 2 * width]),
        stacked(lambda a, b, c, d: a[:, 2 * width : 3 * width]),
        stacked(lambda a, b, c, d: b[:width]),
        stacked(lambda a, b, c, d: a[:, 4 * width :]),
        stacked(lambda a, b, c, d: a[:, 3 * width : 4 * width]),
        stacked(lambda a, b, c, d: b[width:]),
        stacked(lambda a, b, c, d: c[None, :, :HD]),
        stacked(lambda a, b, c, d: c[None, :, HD:]),
        stacked(lambda a, b, c, d: d[0]),
        stacked(lambda a, b, c, d: d[1]),
        jnp.stack([t.astype(f32) for t in table_grads]),
    )


def gate_sum_kernel(idx, m0, m1, m2, m3, gate_ref, w_ref, mem_ref, z_ref, p0, p1, p2, p3, part, plan):
    mem = total4((m0, m1, m2, m3))
    mem_ref[...] = mem
    gate = gate_ref[...]
    z = (mem * (gate * jax.nn.sigmoid(gate))).astype(bf16)
    z_ref[...] = z
    part[...] = dot(z, w_ref[...]).astype(bf16)
    emit_chunks(part, (p0, p1, p2, p3), idx[plan.ti])


def out_back_kernel(idx, g0, g1, g2, g3, w_ref, go_ref, u0, u1, u2, u3, pack, plan):
    place_chunks((g0, g1, g2, g3), go_ref, idx[plan.ti])
    up = dot_nt(go_ref[...], w_ref[...]).astype(bf16)
    for j in range(4):
        pack[j] = fold(up[:, HD * j : HD * (j + 1)])
    for d, u in enumerate((u0, u1, u2, u3)):
        u[...] = pack[idx[plan.si] ^ d]


def qkv_back_kernel(idx, g0, g1, g2, g3, w_ref, g_ref, p0, p1, p2, p3, pack, part, plan):
    for d, g in enumerate((g0, g1, g2, g3)):
        pack[idx[plan.si] ^ d] = g[...]
    rows = g_ref.shape[0]
    columns = [pack[j, 0:rows, 0:HD] for j in range(4)]
    columns += [pack[j, 0:rows, HD : 2 * HD] for j in range(4)]
    columns += [unfold(pack[j, rows:, :]) for j in range(4)]
    g_ref[...] = jnp.concatenate(columns, axis=1)
    part[...] = dot_nt(g_ref[...], w_ref[...]).astype(bf16)
    emit_chunks(part, (p0, p1, p2, p3), idx[plan.ti])


def solution(mesh):
    placed = (
        P("fsdp", "ctx", None),
        P(None, "fsdp", "tp"),
        P(None, "fsdp", "tp"),
        P(None, "fsdp", "tp"),
        P(None, "tp", "fsdp"),
        P(None, "fsdp", "tp"),
        P(None, "fsdp", "tp"),
        P(None, "tp", "fsdp"),
        P(None, "tp", "fsdp", None),
        P(None, "tp", "fsdp", None),
        P(None, "fsdp"),
        P(None, "fsdp"),
        P(None, ("fsdp", "ctx", "tp"), None),
        P("fsdp", None),
        P(None, "fsdp", "tp", "ctx", None),
        P(None, "fsdp", "tp", "ctx", None, None),
        P("fsdp", "ctx", None),
    )
    return jax.shard_map(
        body,
        mesh=mesh,
        in_specs=placed,
        out_specs=(
            P("fsdp", "ctx", None),
            P("fsdp", "ctx", None),
            P(None, "fsdp", "tp"),
            P(None, "fsdp", "tp"),
            P(None, "fsdp", "tp"),
            P(None, "tp", "fsdp"),
            P(None, "fsdp", "tp"),
            P(None, "fsdp", "tp"),
            P(None, "tp", "fsdp"),
            P(None, "tp", "fsdp", None),
            P(None, "tp", "fsdp", None),
            P(None, "fsdp"),
            P(None, "fsdp"),
            P(None, ("fsdp", "ctx", "tp"), None),
        ),
        check_vma=False,
    )
```

```python
import functools

import jax
import jax.numpy as jnp
from jax import lax
from jax.experimental import pallas as pl
from jax.experimental.pallas import tpu as pltpu
from jax.sharding import PartitionSpec as P

HD = 64
NSUB = 256
CAP = 8
EPS = 1e-05
NEG = -1e30
f32 = jnp.float32
bf16 = jnp.bfloat16
MIB = 1 << 20


def dot(a, b):
    return jnp.dot(a, b, preferred_element_type=f32)


def dot_nt(a, b):
    return lax.dot_general(a, b, (((1,), (1,)), ((), ())), preferred_element_type=f32)


def dot_tn(a, b):
    return lax.dot_general(a, b, (((0,), (0,)), ((), ())), preferred_element_type=f32)


def swap(x, axis, step):
    size = lax.axis_size(axis)
    return lax.ppermute(x, axis, [(i, i ^ step) for i in range(size)])


def swaps(xs, axis):
    return [xs[0]] + [swap(xs[d], axis, d) for d in range(1, len(xs))]


def spread(x, axis):
    return [x] + [swap(x, axis, d) for d in range(1, lax.axis_size(axis))]


def shape(dims, dtype):
    return jax.ShapeDtypeStruct(dims, dtype)


def kernel_call(body, name, outs, idx, args, scratch=(), limit=32, flops=0):
    in_specs = [pl.BlockSpec(memory_space=pltpu.SMEM)]
    in_specs += [pl.BlockSpec(memory_space=pltpu.VMEM) for _ in args]
    moved = sum(a.size * a.dtype.itemsize for a in args)
    moved += sum(o.size * o.dtype.itemsize for o in outs)
    return pl.pallas_call(
        body,
        out_shape=outs,
        in_specs=in_specs,
        out_specs=[pl.BlockSpec(memory_space=pltpu.VMEM) for _ in outs],
        scratch_shapes=list(scratch),
        compiler_params=pltpu.CompilerParams(vmem_limit_bytes=limit * MIB),
        cost_estimate=pl.CostEstimate(flops=flops, bytes_accessed=moved, transcendentals=0),
        name=name,
    )(idx, *args)


def rows_at(index, count):
    return pl.ds(pl.multiple_of(index * count, count), count)


def rms(x, gain):
    factor = lax.rsqrt(jnp.mean(x * x, axis=1, keepdims=True) + EPS)
    return factor, x * factor * gain


def rms_back(x, factor, gain, upstream):
    scaled = upstream * gain
    return factor * scaled - x * factor**3 * jnp.mean(scaled * x, axis=1, keepdims=True)


def total4(refs):
    return (refs[0][...].astype(f32) + refs[1][...].astype(f32)) + (
        refs[2][...].astype(f32) + refs[3][...].astype(f32)
    )


def fold(x):
    half = x.shape[0] // 2
    return jnp.concatenate([x[:half], x[half:]], axis=1)


def unfold(x):
    half = x.shape[1] // 2
    return jnp.concatenate([x[:, :half], x[:, half:]], axis=0)


class Plan:
    def __init__(self, SA, TA):
        self.SA, self.TA = SA, TA
        self.si = 1 if SA == "ctx" else 2
        self.ti = 1 if TA == "ctx" else 2

    def src(self, sa, ta):
        return sa * 4 + ta if self.SA == "ctx" else ta * 4 + sa

    def rel(self, ds, dt):
        return (ds, dt) if self.SA == "ctx" else (dt, ds)


PLAN = Plan("ctx", "tp")


def slots_kernel(idx, first_ref, second_ref, out_ref, t0, t1, t2, t3, table, plan, gbits, dbits):
    layers, picks, tokens = first_ref.shape
    inner = second_ref.shape[1]
    owners, _, width = out_ref.shape
    lanes = owners * width
    chunk = tokens // 4
    iota = lax.broadcasted_iota(jnp.int32, (NSUB, tokens), 0)
    before = lax.broadcasted_iota(jnp.int32, (tokens, tokens), 0) < lax.broadcasted_iota(
        jnp.int32, (tokens, tokens), 1
    )
    before = jnp.where(before, 1.0, 0.0).astype(bf16)
    row = lax.broadcasted_iota(jnp.int32, (lanes, tokens), 0)
    token_row = (lax.broadcasted_iota(jnp.int32, (8, tokens), 1) + 1).astype(f32)
    token_row = jnp.where(
        lax.broadcasted_iota(jnp.int32, (8, tokens), 0) == 0, token_row, 0.0
    )
    for l in range(layers):
        onehot = jnp.zeros((NSUB, tokens), f32)
        for i in range(picks):
            onehot = jnp.where(iota == first_ref[l, i : i + 1, :], 1.0, onehot)
        counts = dot(onehot.astype(bf16), before)
        total = jnp.zeros((16, lanes), f32)
        slots = []
        for i in range(picks):
            first = first_ref[l, i : i + 1, :]
            rank = jnp.sum(jnp.where(iota == first, counts, 0.0), axis=0, keepdims=True)
            shard = lax.shift_right_logical(first, gbits)
            group = lax.shift_right_logical(shard, dbits) * (1 << gbits) + (first & ((1 << gbits) - 1))
            slot = (shard & ((1 << dbits) - 1)) * width + group * CAP + rank.astype(jnp.int32)
            slots.append(slot)
            names = jnp.concatenate(
                [second_ref[l, 8 * i : 8 * i + 8, :].astype(f32), token_row], axis=0
            )
            hit = jnp.where(row == slot, 1.0, 0.0).astype(bf16)
            total = total + dot_nt(names.astype(bf16), hit)
        for d in range(owners):
            out_ref[d, 16 * l : 16 * l + 16, :] = total[:, d * width : (d + 1) * width].astype(bf16)
        both = jnp.concatenate([first_ref[l], jnp.concatenate(slots, axis=0)], axis=0)
        for n in range(4):
            cut = slice(n * chunk, (n + 1) * chunk)
            at = l * (8 + inner)
            table[n, at : at + 8, :] = both[:, cut]
            table[n, at + 8 : at + 8 + inner, :] = second_ref[l, :, cut]
    for d, out in enumerate((t0, t1, t2, t3)):
        out[...] = table[idx[plan.ti] ^ d]


def pick_table_kernel(idx, t0, t1, t2, t3, out_ref, table, plan):
    for d, t in enumerate((t0, t1, t2, t3)):
        table[idx[plan.ti] ^ d] = t[...]
    rows = out_ref.shape[1]
    for l in range(out_ref.shape[0]):
        out_ref[l] = jnp.concatenate([table[n, rows * l : rows * (l + 1), :] for n in range(4)], axis=1)


def head_mask(shape_, lanes_each):
    return lax.broadcasted_iota(jnp.int32, shape_, 1) // lanes_each


def place_chunks(refs, full, t):
    count = refs[0].shape[0]
    for d in range(4):
        full[rows_at(t ^ d, count), :] = refs[d][...]


def emit_chunks(part, outs, t):
    count = outs[0].shape[0]
    for d in range(4):
        outs[d][...] = part[rows_at(t ^ d, count), :]


def piece_at(f, j, pieces, size):
    return rows_at(f ^ j, size) if len(pieces) > 1 else slice(0, size)


def emit_heads(h_ref, pieces, pack, outs, idx, plan):
    width = pieces[0].shape[1] // 3
    size = pieces[0].shape[0]
    qkv = sum(
        dot(h_ref[:, piece_at(idx[0], j, pieces, size)], w[...]) for j, w in enumerate(pieces)
    ).astype(bf16)
    for j in range(4):
        q = qkv[:, HD * j : HD * (j + 1)]
        k = qkv[:, width + HD * j : width + HD * (j + 1)]
        v = qkv[:, 2 * width + HD * j : 2 * width + HD * (j + 1)]
        pack[j] = jnp.concatenate([jnp.concatenate([q, k], axis=1), fold(v)], axis=0)
    for d in range(4):
        outs[d][...] = pack[idx[plan.si] ^ d]


def qkv_first_kernel(idx, x_ref, gain_ref, *refs, plan, row):
    *pieces, h_ref, e0, e1, e2, e3, pack = refs
    _, normed = rms(x_ref[...].astype(f32), gain_ref[row : row + 1, :])
    h_ref[...] = normed.astype(bf16)
    emit_heads(h_ref, pieces, pack, (e0, e1, e2, e3), idx, plan)


def qkv_kernel(idx, h0, h1, h2, h3, *refs, plan):
    *pieces, h_ref, e0, e1, e2, e3, pack = refs
    place_chunks((h0, h1, h2, h3), h_ref, idx[plan.ti])
    emit_heads(h_ref, pieces, pack, (e0, e1, e2, e3), idx, plan)


def load_heads(es, kk, vv):
    for d in range(4):
        rows = es[d].shape[0] * 2 // 3
        kk[rows * d : rows * (d + 1), :] = es[d][0:rows, HD : 2 * HD]
        vv[rows * d : rows * (d + 1), :] = unfold(es[d][rows:, :])


def load_ids(col_ref, ids_col, s):
    count = col_ref.shape[0] // 4
    for d in range(4):
        ids_col[count * d : count * (d + 1), :] = col_ref[rows_at(s ^ d, count), :]


def probabilities(kk, q, key_ids, query_ids):
    scores = dot_nt(kk, q) * (HD ** (-0.5))
    scores = jnp.where(key_ids <= query_ids, scores, NEG)
    top = jnp.max(scores, axis=0, keepdims=True)
    exponent = jnp.exp(scores - top)
    return exponent * (1.0 / jnp.sum(exponent, axis=0, keepdims=True))


def attend_kernel(idx, e0, e1, e2, e3, row_ref, col_ref, a0, a1, a2, a3, kk, vv, ids_col, plan):
    es, outs = (e0, e1, e2, e3), (a0, a1, a2, a3)
    s = idx[plan.si]
    load_heads(es, kk, vv)
    load_ids(col_ref, ids_col, s)
    count = kk.shape[0] // 4
    for d in range(4):
        query_ids = row_ref[:, rows_at(s ^ d, count)]
        p = probabilities(kk[...], es[d][0:count, 0:HD], ids_col[...], query_ids)
        blended = dot_tn(vv[...], p.astype(bf16))
        outs[d][...] = fold(blended.T.astype(bf16))


def attend_back_kernel(
    idx, e0, e1, e2, e3, u0, u1, u2, u3, row_ref, col_ref, g0, g1, g2, g3, kk, vv, ids_col, gk, gv, plan
):
    es, us, outs = (e0, e1, e2, e3), (u0, u1, u2, u3), (g0, g1, g2, g3)
    s = idx[plan.si]
    load_heads(es, kk, vv)
    load_ids(col_ref, ids_col, s)
    count = kk.shape[0] // 4
    scale = HD ** (-0.5)
    for d in range(4):
        query_ids = row_ref[:, rows_at(s ^ d, count)]
        q = es[d][0:count, 0:HD]
        up = unfold(us[d][...])
        p = probabilities(kk[...], q, ids_col[...], query_ids)
        gp = dot_nt(vv[...], up)
        centre = jnp.sum(p * gp, axis=0, keepdims=True)
        gs = (p * (gp - centre)).astype(bf16)
        gq = (dot_tn(kk[...], gs) * scale).T.astype(bf16)
        outs[d][0:count, 0:HD] = gq
        key_term = dot(gs, q)
        value_term = dot(p.astype(bf16), up)
        if d == 0:
            gk[...] = key_term
            gv[...] = value_term
        else:
            gk[...] += key_term
            gv[...] += value_term
    for d in range(4):
        outs[d][0:count, HD : 2 * HD] = (gk[count * d : count * (d + 1), :] * scale).astype(bf16)
        outs[d][count:, :] = fold(gv[count * d : count * (d + 1), :].astype(bf16))


def out_kernel(idx, a0, a1, a2, a3, *refs, plan):
    *pieces, a_ref, p0, p1, p2, p3, heads, part = refs
    for d, a in enumerate((a0, a1, a2, a3)):
        heads[idx[plan.si] ^ d] = unfold(a[...])
    a_ref[...] = jnp.concatenate([heads[j] for j in range(4)], axis=1)
    size = pieces[0].shape[1]
    for j, w in enumerate(pieces):
        part[:, piece_at(idx[0], j, pieces, size)] = dot(a_ref[...], w[...]).astype(bf16)
    emit_chunks(part, (p0, p1, p2, p3), idx[plan.ti])


def out_back_kernel(idx, g0, g1, g2, g3, *refs, plan):
    *pieces, go_ref, u0, u1, u2, u3, pack = refs
    place_chunks((g0, g1, g2, g3), go_ref, idx[plan.ti])
    size = pieces[0].shape[1]
    up = sum(
        dot_nt(go_ref[:, piece_at(idx[0], j, pieces, size)], w[...]) for j, w in enumerate(pieces)
    ).astype(bf16)
    for j in range(4):
        pack[j] = fold(up[:, HD * j : HD * (j + 1)])
    for d, u in enumerate((u0, u1, u2, u3)):
        u[...] = pack[idx[plan.si] ^ d]


def qkv_back_kernel(idx, g0, g1, g2, g3, *refs, plan):
    *pieces, g_ref, p0, p1, p2, p3, pack, part = refs
    for d, g in enumerate((g0, g1, g2, g3)):
        pack[idx[plan.si] ^ d] = g[...]
    rows = g_ref.shape[0]
    columns = [pack[j, 0:rows, 0:HD] for j in range(4)]
    columns += [pack[j, 0:rows, HD : 2 * HD] for j in range(4)]
    columns += [unfold(pack[j, rows:, :]) for j in range(4)]
    g_ref[...] = jnp.concatenate(columns, axis=1)
    size = pieces[0].shape[0]
    for j, w in enumerate(pieces):
        part[:, piece_at(idx[0], j, pieces, size)] = dot_nt(g_ref[...], w[...]).astype(bf16)
    emit_chunks(part, (p0, p1, p2, p3), idx[plan.ti])


def to_pack(x):
    rows, width = x.shape
    if width >= 256:
        return jnp.concatenate([x[:, 256 * i : 256 * (i + 1)] for i in range(width // 256)], axis=0)
    fold_by = 256 // width
    rows = rows // fold_by
    return jnp.concatenate([x[rows * i : rows * (i + 1)] for i in range(fold_by)], axis=1)


def from_pack(p, rows, width):
    if width >= 256:
        return jnp.concatenate([p[rows * i : rows * (i + 1)] for i in range(width // 256)], axis=1)
    return jnp.concatenate([p[:, width * i : width * (i + 1)] for i in range(256 // width)], axis=0)


def shard_rows(x, f, shards):
    size = x.shape[0] // shards
    return x[size * f : size * (f + 1)]


def shard_columns(x, f, shards):
    size = x.shape[1] // shards
    return x[:, size * f : size * (f + 1)]


def out_grad_kernel(idx, a_ref, go_ref, pack_ref):
    shards = pack_ref.shape[0]
    change = dot_tn(a_ref[...], go_ref[...])
    for f in range(shards):
        pack_ref[f] = to_pack(shard_columns(change, f, shards)).astype(bf16)


def qkv_grad_kernel(idx, h_ref, g_ref, pack_ref):
    shards = pack_ref.shape[0]
    change = dot_tn(h_ref[...], g_ref[...])
    for f in range(shards):
        pack_ref[f] = to_pack(shard_rows(change, f, shards)).astype(bf16)


def qkv_grad_split_kernel(idx, h_ref, g_ref, mine_ref, other_ref, change):
    change[...] = dot_tn(h_ref[...], g_ref[...])
    size = change.shape[0] // 2
    for j, out in enumerate((mine_ref, other_ref)):
        out[...] = to_pack(change[rows_at(idx[0] ^ j, size), :]).astype(bf16)


def memory_grad_kernel(idx, *refs, plan, has_full):
    forward, back = refs[0:4], refs[4:8]
    full = refs[8] if has_full else None
    pack_ref, h, z, gg, gu, gy = refs[-6:]
    chunk = forward[0].shape[0]
    d_model = h.shape[1]
    quarter = z.shape[1]
    shards = pack_ref.shape[0]
    tables = jnp.zeros((NSUB, 2 * HD), f32)
    for d in range(4):
        at = slice(chunk * d, chunk * (d + 1))
        h[at, :] = forward[d][:, 0:d_model]
        z[at, :] = forward[d][:, d_model:]
        gg[at, :] = back[d][:, 0:quarter]
        gu[at, :] = back[d][:, quarter : quarter + 2 * HD]
        folded = back[d][:, quarter + 2 * HD : quarter + 10 * HD].astype(f32)
        tables = tables + jnp.concatenate(
            [folded[:, 2 * HD * i : 2 * HD * (i + 1)] for i in range(4)], axis=0
        )
        if has_full:
            gy[at, :] = full[rows_at(idx[plan.ti] ^ d, chunk), :]
        else:
            gy[at, :] = back[d][:, quarter + 10 * HD :]
    gate_change = dot_tn(h[...], gg[...])
    look_change = dot_tn(h[...], gu[...])
    mem_change = dot_tn(z[...], gy[...])
    for f in range(shards):
        pack_ref[f] = jnp.concatenate(
            [
                to_pack(shard_rows(gate_change, f, shards)),
                to_pack(shard_columns(mem_change, f, shards)),
                to_pack(shard_rows(look_change, f, shards)),
                to_pack(shard_rows(tables, f, shards)),
            ],
            axis=0,
        ).astype(bf16)


def finalize_kernel(idx, *refs, layers, late):
    count = 3 * layers - 1 + (4 if late else 1)
    packs = refs[:count]
    q_ref, k_ref, v_ref, o_ref, look_ref, gate_ref, mem_ref, first_ref, second_ref, merged = refs[count:]
    part = q_ref.shape[1]
    for l in range(layers):
        if l == 0:
            memory, out = packs[0], packs[1]
            if late:
                chunk = packs[2].shape[0]
                for d in range(4):
                    merged[rows_at(idx[1] ^ d, chunk), :] = packs[2 + d][...]
            else:
                merged[...] = packs[2][...]
            qkv = merged
        else:
            memory, out, qkv = packs[count - 3 * (layers - l) : count - 3 * (layers - l) + 3]
        for n, ref in enumerate((q_ref, k_ref, v_ref)):
            ref[l] = qkv[part * n : part * (n + 1), :].astype(f32)
        o_ref[l] = from_pack(out[...], o_ref.shape[1], o_ref.shape[2]).astype(f32)
        gate_ref[l] = memory[0:part, :].astype(f32)
        mem_ref[l] = from_pack(memory[part : 2 * part, :], mem_ref.shape[1], mem_ref.shape[2]).astype(f32)
        look_ref[l] = from_pack(
            memory[2 * part : 2 * part + part // 2, :].astype(f32), part, look_ref.shape[2]
        )
        tables = from_pack(
            memory[2 * part + part // 2 :, :].astype(f32), first_ref.shape[2], 2 * HD
        )
        first_ref[l, 0] = tables[:, :HD]
        second_ref[l, 0] = tables[:, HD:]


def add_four_kernel(idx, a, b, c, d, out):
    out[...] = total4((a, b, c, d)).astype(out.dtype)


def add_two_kernel(idx, a, b, o0, o1, o2, o3):
    chunk = o0.shape[0]
    for d, out in enumerate((o0, o1, o2, o3)):
        at = rows_at(idx[1] ^ d, chunk)
        out[...] = (a[at, :].astype(f32) + b[at, :].astype(f32)).astype(bf16)


def place_kernel(idx, c0, c1, c2, c3, out_ref, plan):
    chunk = c0.shape[0]
    for d, c in enumerate((c0, c1, c2, c3)):
        out_ref[rows_at(idx[plan.ti] ^ d, chunk), :] = c[...].astype(out_ref.dtype)


def own_rows(ref, idx, plan, count):
    if ref.shape[0] == count:
        return ref[...].astype(f32)
    return ref[rows_at(idx[plan.ti], count), :].astype(f32)


def table_of(a_ref, m, shards):
    size = a_ref.shape[1] * 4 // 5
    both = [a_ref[f * 4 + m, size:, :] for f in range(shards)]
    both = both[0] if shards == 1 else jnp.concatenate(both, axis=0)
    return both[:, :HD], both[:, HD:]


def only_head(x, m, chunk):
    lane = lax.broadcasted_iota(jnp.int32, x.shape, 1)
    return jnp.where((lane >= m * chunk) & (lane < (m + 1) * chunk), x, 0.0)


def lookup_kernel(
    idx, x_ref, p0, r1, r2, r3, gain_ref, a_ref, pick_ref, x_out, h_ref, u_ref, w_ref, out_ref, plan, row, layer, shards
):
    chunk = p0.shape[0]
    x = own_rows(x_ref, idx, plan, chunk) + total4((p0, r1, r2, r3))
    x_out[...] = x
    _, normed = rms(x, gain_ref[row : row + 1, :])
    h_ref[...] = normed.astype(bf16)
    size = a_ref.shape[1] * 4 // 5
    c1, c2 = [], []
    for m in range(4):
        u = sum(
            dot(h_ref[:, size * f : size * (f + 1)], a_ref[f * 4 + m, 0:size, :]) for f in range(shards)
        ).astype(bf16)
        u_ref[:, 2 * HD * m : 2 * HD * (m + 1)] = u
        ka, kb = table_of(a_ref, m, shards)
        c1.append(dot_nt(ka, u[:, :HD]))
        c2.append(dot_nt(kb, u[:, HD:]))
    c1 = jnp.concatenate(c1, axis=1)
    c2 = jnp.concatenate(c2, axis=1)
    lanes = c1.shape[1]
    iota = lax.broadcasted_iota(jnp.int32, (NSUB, lanes), 0)
    for i in range(4):
        first = pick_ref[layer, i : i + 1, :]
        base = jnp.sum(jnp.where(iota == first, c1, 0.0), axis=0, keepdims=True)
        for b in range(8):
            r = i * 8 + b
            second = pick_ref[layer, 8 + r : 9 + r, :]
            picked = jnp.sum(jnp.where(iota == second, c2, 0.0), axis=0, keepdims=True)
            w_ref[r : r + 1, :] = base + picked
    logits = w_ref[...]
    exponent = jnp.exp(logits - jnp.max(logits, axis=0, keepdims=True))
    w = exponent * (1.0 / jnp.sum(exponent, axis=0, keepdims=True))
    w_ref[...] = w
    owners, _, width = out_ref.shape
    slots = lax.broadcasted_iota(jnp.int32, (owners * width, lanes), 0)
    total = jnp.zeros((32, owners * width), f32)
    for i in range(4):
        hit = jnp.where(slots == pick_ref[layer, 4 + i : 5 + i, :], 1.0, 0.0).astype(bf16)
        mine = w[8 * i : 8 * (i + 1), :]
        split = jnp.concatenate([only_head(mine, m, chunk) for m in range(4)], axis=0)
        total = total + dot_nt(split.astype(bf16), hit)
    for d in range(owners):
        out_ref[d] = total[:, d * width : (d + 1) * width].astype(bf16)


def gate_values_kernel(idx, h_ref, wg_ref, gate_ref, shards):
    size = wg_ref.shape[1]
    quarter = wg_ref.shape[2]
    for t in range(4):
        gate_ref[:, quarter * t : quarter * (t + 1)] = sum(
            dot(h_ref[:, size * f : size * (f + 1)], wg_ref[f * 4 + t]) for f in range(shards)
        )


def gate_kernel(
    idx, s0, s1, s2, s3, gate_ref, wp_ref, x_ref, h_ref, gain_ref,
    mem_ref, z_ref, x_out, h_out, f0, f1, f2, f3, plan, row, shards,
):
    mem = total4((s0, s1, s2, s3))
    mem_ref[...] = mem
    gate = gate_ref[...]
    z_ref[...] = (mem * (gate * jax.nn.sigmoid(gate))).astype(bf16)
    quarter, size = wp_ref.shape[1], wp_ref.shape[2]
    for f in range(shards):
        at = slice(size * f, size * (f + 1))
        x_out[:, at] = x_ref[:, at] + sum(
            dot(z_ref[:, quarter * t : quarter * (t + 1)], wp_ref[f * 4 + t]) for t in range(4)
        )
    x = x_out[...]
    if row is None:
        h_out[...] = x.astype(bf16)
    else:
        h_out[...] = rms(x, gain_ref[row : row + 1, :])[1].astype(bf16)
    d_model = x.shape[1]
    for d, f in enumerate((f0, f1, f2, f3)):
        f[:, 0:d_model] = h_ref[...]
        f[:, d_model:] = z_ref[:, rows_at(idx[plan.ti] ^ d, quarter)]


def gate_back(gy_ref, wp_ref, gate_ref, mem_ref, gn_ref, gg_ref, shards):
    quarter, size = wp_ref.shape[1], wp_ref.shape[2]
    for t in range(4):
        at = slice(quarter * t, quarter * (t + 1))
        gz = sum(dot_nt(gy_ref[:, size * f : size * (f + 1)], wp_ref[f * 4 + t]) for f in range(shards))
        gate = gate_ref[:, at]
        sigmoid = jax.nn.sigmoid(gate)
        gn_ref[:, at] = (gz * (gate * sigmoid)).astype(bf16)
        slope = sigmoid * (1.0 + gate * (1.0 - sigmoid))
        gg_ref[:, at] = (gz * mem_ref[:, at] * slope).astype(bf16)


def start_back_kernel(idx, g_ref, wp_ref, gate_ref, mem_ref, gy_ref, gn_ref, gg_ref, plan, shards):
    gy_ref[...] = g_ref[rows_at(idx[plan.ti], gy_ref.shape[0]), :]
    gate_back(gy_ref, wp_ref, gate_ref, mem_ref, gn_ref, gg_ref, shards)


def norm_back(idx, parts, x_ref, g_ref, gain_ref, dgain_ref, plan, row):
    count = parts[0].shape[0]
    upstream = total4(parts)
    x = own_rows(x_ref, idx, plan, count)
    gain = gain_ref[row : row + 1, :]
    factor, _ = rms(x, gain)
    dgain_ref[...] = jnp.sum(upstream * x * factor, axis=0, keepdims=True)
    return g_ref[...] + rms_back(x, factor, gain, upstream)


def norm_back_kernel(
    idx, p0, r1, r2, r3, x_ref, g_ref, gain_ref, wp_ref, gate_ref, mem_ref,
    gx_ref, gy_ref, dgain_ref, gn_ref, gg_ref, plan, row, shards,
):
    gx = norm_back(idx, (p0, r1, r2, r3), x_ref, g_ref, gain_ref, dgain_ref, plan, row)
    gx_ref[...] = gx
    gy_ref[...] = gx.astype(bf16)
    gate_back(gy_ref, wp_ref, gate_ref, mem_ref, gn_ref, gg_ref, shards)


def norm_back_last_kernel(idx, p0, r1, r2, r3, x_ref, g_ref, gain_ref, gx_ref, dgain_ref, plan, row):
    gx = norm_back(idx, (p0, r1, r2, r3), x_ref, g_ref, gain_ref, dgain_ref, plan, row)
    gx_ref[...] = gx.astype(bf16)


def lookup_back_kernel(
    idx, gw_ref, pick_ref, w_ref, a_ref, u_ref, gg_ref, gy_ref, wg_ref, x_ref, g_ref, gain_ref,
    gx_ref, go_ref, dgain_ref, b0, b1, b2, b3, gl, gu_all, tables, gh, plan, row, layer, shards,
):
    chunk = u_ref.shape[0]
    owners, _, width = gw_ref.shape
    lanes = w_ref.shape[1]
    slots = lax.broadcasted_iota(jnp.int32, (owners * width, lanes), 0)
    arrived = jnp.concatenate([gw_ref[d] for d in range(owners)], axis=1)
    for i in range(4):
        hit = jnp.where(slots == pick_ref[layer, 4 + i : 5 + i, :], 1.0, 0.0).astype(bf16)
        mixed = dot(arrived, hit)
        gl[8 * i : 8 * (i + 1), :] = sum(
            only_head(mixed[8 * m : 8 * (m + 1), :], m, chunk) for m in range(4)
        )
    w = w_ref[...]
    gw = gl[...]
    gl[...] = w * (gw - jnp.sum(w * gw, axis=0, keepdims=True))
    iota = lax.broadcasted_iota(jnp.int32, (NSUB, lanes), 0)
    gc1 = jnp.zeros((NSUB, lanes), f32)
    gc2 = jnp.zeros((NSUB, lanes), f32)
    for i in range(4):
        both = jnp.sum(gl[8 * i : 8 * (i + 1), :], axis=0, keepdims=True)
        gc1 = jnp.where(iota == pick_ref[layer, i : i + 1, :], both, gc1)
        for b in range(8):
            r = i * 8 + b
            gc2 = gc2 + jnp.where(iota == pick_ref[layer, 8 + r : 9 + r, :], gl[r : r + 1, :], 0.0)
    gc1 = gc1.astype(bf16)
    gc2 = gc2.astype(bf16)
    for m in range(4):
        ka, kb = table_of(a_ref, m, shards)
        one = gc1[:, chunk * m : chunk * (m + 1)]
        two = gc2[:, chunk * m : chunk * (m + 1)]
        gu_all[:, 2 * HD * m : 2 * HD * (m + 1)] = jnp.concatenate(
            [dot_tn(one, ka), dot_tn(two, kb)], axis=1
        ).astype(bf16)
        change = jnp.concatenate(
            [
                dot(one, u_ref[:, 2 * HD * m : 2 * HD * m + HD]),
                dot(two, u_ref[:, 2 * HD * m + HD : 2 * HD * (m + 1)]),
            ],
            axis=1,
        ).astype(bf16)
        tables[m] = jnp.concatenate(
            [change[NSUB // 4 * n : NSUB // 4 * (n + 1), :] for n in range(4)], axis=1
        )
    size, quarter = wg_ref.shape[1], wg_ref.shape[2]
    for f in range(shards):
        gh[:, size * f : size * (f + 1)] = sum(
            dot_nt(gg_ref[:, quarter * t : quarter * (t + 1)], wg_ref[f * 4 + t])
            + dot_nt(gu_all[:, 2 * HD * t : 2 * HD * (t + 1)], a_ref[f * 4 + t, 0:size, :])
            for t in range(4)
        )
    upstream = gh[...]
    x = x_ref[...]
    gain = gain_ref[row : row + 1, :]
    factor, _ = rms(x, gain)
    dgain_ref[...] = jnp.sum(upstream * x * factor, axis=0, keepdims=True)
    gx = own_rows(g_ref, idx, plan, chunk) + rms_back(x, factor, gain, upstream)
    gx_ref[...] = gx
    go_ref[...] = gx.astype(bf16)
    for d, b in enumerate((b0, b1, b2, b3)):
        n = idx[plan.ti] ^ d
        b[:, 0:quarter] = gg_ref[:, rows_at(n, quarter)]
        b[:, quarter : quarter + 2 * HD] = gu_all[:, rows_at(n, 2 * HD)]
        b[:, quarter + 2 * HD : quarter + 10 * HD] = tables[n]
        if b.shape[1] > quarter + 10 * HD:
            b[:, quarter + 10 * HD :] = gy_ref[...]


STEP_GROUPS = 4


def step_base(idx, step, pieces, per_piece):
    if pieces == 1:
        return step * STEP_GROUPS
    piece = step // per_piece
    return ((idx[0] ^ piece) * per_piece + step % per_piece) * STEP_GROUPS


def read_kernel(idx, w_ref, names_ref, *refs, plan, pieces, per_piece):
    vs = refs[:pieces]
    o0, o1, o2, o3, s_ref, partial, rows = refs[pieces:]
    step = pl.program_id(0)
    sources, _, width = w_ref.shape

    @pl.when(step == 0)
    def _():
        iota = lax.broadcasted_iota(jnp.int32, (NSUB, width), 0).astype(f32)

        def build(sa, carry):
            weights = sum(w_ref[plan.src(sa, ta)].astype(f32) for ta in range(4))
            for m in range(4):
                src = plan.src(sa, m)
                names = names_ref[src].astype(f32)
                dense = jnp.zeros((NSUB, width), f32)
                for b in range(8):
                    r = 8 * m + b
                    dense = jnp.where(iota == names[b : b + 1, :], weights[r : r + 1, :], dense)
                s_ref[src] = dense.T
            return carry

        lax.fori_loop(0, 4, build, 0)

    base = step_base(idx, step, pieces, per_piece)

    def multiply(v_ref):
        for k in range(STEP_GROUPS):
            at = rows_at(base + k, CAP)
            left = s_ref[:, at, :].reshape(sources * CAP, NSUB).astype(bf16)
            got = dot(left, v_ref[NSUB * k : NSUB * (k + 1), :])
            partial[:, at, :] = got.reshape(sources, CAP, v_ref.shape[1])

    for n in range(pieces):
        pl.when(step // per_piece == n)(functools.partial(multiply, vs[n]))

    @pl.when(step == pl.num_programs(0) - 1)
    def _():
        s, t = idx[plan.si], idx[plan.ti]
        tokens = rows.shape[0]
        chunk = tokens // 4
        outs = (o0, o1, o2, o3)
        iota = (lax.broadcasted_iota(jnp.int32, (tokens, width), 0) + 1).astype(f32)
        for ds in range(4):
            hits, parts = [], []
            for m in range(4):
                src = plan.src(s ^ ds, m)
                token = names_ref[src].astype(f32)[8:9, :]
                hits.append(jnp.where(iota == token, 1.0, 0.0).astype(bf16))
                parts.append(partial[src].astype(bf16))
            rows[...] = dot(
                jnp.concatenate(hits, axis=1), jnp.concatenate(parts, axis=0)
            ).astype(bf16)
            for dt in range(4):
                dp, dz = plan.rel(ds, dt)
                outs[dp][chunk * dz : chunk * (dz + 1), :] = rows[rows_at(t ^ dt, chunk), :]


def value_specs(values, layer):
    d_model = values[0].shape[2]
    per_piece = values[0].shape[1] // (STEP_GROUPS * NSUB)
    specs = []
    for n in range(len(values)):
        def index(g, n=n):
            return (layer, jnp.clip(g - n * per_piece, 0, per_piece - 1), 0)

        specs.append(pl.BlockSpec((None, STEP_GROUPS * NSUB, d_model), index))
    return specs, per_piece


def read_call(idx, weights, names, layer, values, plan, tokens):
    sources, inner, width = weights.shape
    specs, per_piece = value_specs(values, layer)
    d_model = values[0].shape[2]
    out = shape((tokens, d_model), bf16)
    return pl.pallas_call(
        functools.partial(read_kernel, plan=plan, pieces=len(values), per_piece=per_piece),
        grid=(per_piece * len(values),),
        out_shape=[out, out, out, out, shape((sources, width, NSUB), f32)],
        in_specs=[
            pl.BlockSpec(memory_space=pltpu.SMEM),
            pl.BlockSpec((sources, inner, width), lambda g: (0, 0, 0)),
            pl.BlockSpec((sources, 16, width), lambda g: (0, layer, 0)),
        ]
        + specs,
        out_specs=[pl.BlockSpec((tokens, d_model), lambda g: (0, 0)) for _ in range(4)]
        + [pl.BlockSpec((sources, width, NSUB), lambda g: (0, 0, 0))],
        scratch_shapes=[
            pltpu.VMEM((sources, width, d_model), f32),
            pltpu.VMEM((tokens, d_model), bf16),
        ],
        compiler_params=pltpu.CompilerParams(vmem_limit_bytes=50 * MIB),
        cost_estimate=pl.CostEstimate(
            flops=4 * sources * width * NSUB * d_model, bytes_accessed=20 * MIB, transcendentals=0
        ),
        name="memory_read",
    )(idx, weights, names, *values)


def write_kernel(idx, g0, g1, g2, g3, names_ref, s_ref, *refs, plan, pieces, per_piece):
    vs, dvs = refs[:pieces], refs[pieces : 2 * pieces]
    gw_ref, grads, partial, cross = refs[2 * pieces :]
    step = pl.program_id(0)
    sources, width, _ = s_ref.shape
    d_model = vs[0].shape[1]

    @pl.when(step == 0)
    def _():
        s, t = idx[plan.si], idx[plan.ti]
        tokens = grads.shape[1]
        chunk = tokens // 4
        for dp, g in enumerate((g0, g1, g2, g3)):
            for dz in range(4):
                ds, dt = plan.rel(dp, dz)
                grads[s ^ ds, rows_at(t ^ dt, chunk), :] = g[chunk * dz : chunk * (dz + 1), :]
        iota = (lax.broadcasted_iota(jnp.int32, (tokens, width), 0) + 1).astype(f32)
        for sa in range(4):
            for m in range(4):
                src = plan.src(sa, m)
                token = names_ref[src].astype(f32)[8:9, :]
                hit = jnp.where(iota == token, 1.0, 0.0).astype(bf16)
                partial[src] = dot_tn(hit, grads[sa])

    base = step_base(idx, step, pieces, per_piece)

    def multiply(v_ref, dv_ref):
        for k in range(STEP_GROUPS):
            at = rows_at(base + k, CAP)
            cut = slice(NSUB * k, NSUB * (k + 1))
            inbox = partial[:, at, :].reshape(sources * CAP, d_model).astype(bf16)
            left = s_ref[:, at, :].reshape(sources * CAP, NSUB).astype(bf16)
            dv_ref[cut, :] = dot_tn(left, inbox).astype(bf16)
            cross[:, at, :] = dot_nt(inbox, v_ref[cut, :]).reshape(sources, CAP, NSUB)

    for n in range(pieces):
        pl.when(step // per_piece == n)(functools.partial(multiply, vs[n], dvs[n]))

    @pl.when(step == pl.num_programs(0) - 1)
    def _():
        iota = lax.broadcasted_iota(jnp.int32, (NSUB, width), 0).astype(f32)

        def select(sa, carry):
            picked = []
            for m in range(4):
                src = plan.src(sa, m)
                turned = cross[src].T
                names = names_ref[src].astype(f32)
                picked += [
                    jnp.sum(jnp.where(iota == names[b : b + 1, :], turned, 0.0), axis=0, keepdims=True)
                    for b in range(8)
                ]
            picked = jnp.concatenate(picked, axis=0).astype(bf16)
            for ta in range(4):
                gw_ref[plan.src(sa, ta)] = picked
            return carry

        lax.fori_loop(0, 4, select, 0)


def write_call(idx, grads, names, layer, dense, values, plan, tokens):
    sources, width, _ = dense.shape
    specs, per_piece = value_specs(values, layer)
    d_model = values[0].shape[2]
    pieces = len(values)

    def dv_spec(n):
        return pl.BlockSpec(
            (STEP_GROUPS * NSUB, d_model), lambda g: (jnp.clip(g - n * per_piece, 0, per_piece - 1), 0)
        )

    return pl.pallas_call(
        functools.partial(write_kernel, plan=plan, pieces=pieces, per_piece=per_piece),
        grid=(per_piece * pieces,),
        out_shape=[shape((v.shape[1], d_model), bf16) for v in values]
        + [shape((sources, 32, width), bf16)],
        in_specs=[pl.BlockSpec(memory_space=pltpu.SMEM)]
        + [pl.BlockSpec((tokens, d_model), lambda g: (0, 0)) for _ in range(4)]
        + [
            pl.BlockSpec((sources, 16, width), lambda g: (0, layer, 0)),
            pl.BlockSpec((sources, width, NSUB), lambda g: (0, 0, 0)),
        ]
        + specs,
        out_specs=[dv_spec(n) for n in range(pieces)]
        + [pl.BlockSpec((sources, 32, width), lambda g: (0, 0, 0))],
        scratch_shapes=[
            pltpu.VMEM((4, tokens, d_model), bf16),
            pltpu.VMEM((sources, width, d_model), f32),
            pltpu.VMEM((sources, width, NSUB), f32),
        ],
        compiler_params=pltpu.CompilerParams(vmem_limit_bytes=56 * MIB),
        cost_estimate=pl.CostEstimate(
            flops=6 * sources * width * NSUB * d_model, bytes_accessed=28 * MIB, transcendentals=0
        ),
        name="memory_write",
    )(idx, *grads, names, dense, *values)


def sum_kernel(idx, m0, r1, r2, r3, o0, o1, o2, o3):
    count = o0.shape[0]
    for dz, out in enumerate((o0, o1, o2, o3)):
        at = slice(count * dz, count * (dz + 1))
        out[...] = (
            (m0[at, :].astype(f32) + r1[at, :].astype(f32))
            + (r2[at, :].astype(f32) + r3[at, :].astype(f32))
        ).astype(bf16)


def table_grad_kernel(a_ref, b_ref, *refs):
    refs[-1][...] = a_ref[...].astype(f32) + b_ref[...].astype(f32)


def table_grad_call(mine, arrived, layer, layers, earlier):
    rows, d_model = mine.shape
    block = min(rows, 512)
    specs = [pl.BlockSpec((block, d_model), lambda g: (g, 0))] * 2
    args = [mine, arrived]
    if earlier is not None:
        specs = specs + [pl.BlockSpec(memory_space=pl.ANY)]
        args.append(earlier)
    return pl.pallas_call(
        table_grad_kernel,
        grid=(rows // block,),
        out_shape=shape((layers, rows, d_model), f32),
        in_specs=specs,
        out_specs=pl.BlockSpec((None, block, d_model), lambda g: (layer, g, 0)),
        input_output_aliases={} if earlier is None else {2: 0},
        compiler_params=pltpu.CompilerParams(vmem_limit_bytes=32 * MIB),
        cost_estimate=pl.CostEstimate(flops=0, bytes_accessed=16 * MIB, transcendentals=0),
        name="table_grad",
    )(*args)


def gather_shards(x, axis):
    if lax.axis_size("fsdp") != 2:
        return lax.all_gather(x, "fsdp", axis=axis, tiled=True)
    other = swap(x, "fsdp", 1)
    mine = lax.axis_index("fsdp") == 0
    return jnp.where(
        mine, jnp.concatenate([x, other], axis=axis), jnp.concatenate([other, x], axis=axis)
    )


def shard_pieces(x, axis):
    if lax.axis_size("fsdp") != 2:
        return [lax.all_gather(x, "fsdp", axis=axis, tiled=True)]
    return [x, swap(x, "fsdp", 1)]


def after(xs, *others):
    return lax.optimization_barrier((tuple(xs), tuple(others)))[0]


def body(
    inputs,
    query_weight,
    key_weight,
    value_weight,
    attention_weight,
    lookup_weight,
    gate_weight,
    memory_weight,
    first_table,
    second_table,
    attention_gain,
    memory_gain,
    memory_values,
    blocks,
    first_picks,
    second_picks,
    cotangent,
):
    plan = PLAN
    SA, TA = plan.SA, plan.TA
    layers = query_weight.shape[0]
    tokens = inputs.shape[1]
    d_model = inputs.shape[2]
    chunk = tokens // 4
    width = query_weight.shape[2]
    shards = lax.axis_size("fsdp")
    owners = lax.axis_size("ctx") * lax.axis_size("tp")
    groups = memory_values.shape[1] // NSUB
    lanes = shards * groups * CAP
    gbits = groups.bit_length() - 1
    dbits = owners.bit_length() - 1
    idx = jnp.stack(
        [lax.axis_index("fsdp"), lax.axis_index("ctx"), lax.axis_index("tp"), 0]
    ).astype(jnp.int32)

    w_qkv, w_o, w_look, w_gate, w_mem = [], [], [], [], []
    for l in range(layers):
        w_qkv.append(
            shard_pieces(
                jnp.concatenate([query_weight[l], key_weight[l], value_weight[l]], axis=1).astype(bf16), 0
            )
        )
        if l == 0:
            gains = gather_shards(
                jnp.concatenate([attention_gain, memory_gain], axis=0).astype(bf16), 1
            ).astype(f32)
        w_o.append(shard_pieces(attention_weight[l].astype(bf16), 1))
        look = jnp.concatenate(
            [lookup_weight[l], jnp.concatenate([first_table[l, 0], second_table[l, 0]], axis=1)], axis=0
        ).astype(bf16)
        w_look.append(lax.all_gather(look, ("fsdp", "tp"), axis=0, tiled=False))
        w_gate.append(lax.all_gather(gate_weight[l].astype(bf16), ("fsdp", "tp"), axis=0, tiled=False))
        w_mem.append(lax.all_gather(memory_weight[l].astype(bf16), ("fsdp", "tp"), axis=0, tiled=False))
    values = [memory_values]
    if shards == 2:
        values.append(swap(memory_values, "fsdp", 1))
    else:
        values = [lax.all_gather(memory_values, "fsdp", axis=1, tiled=True)]

    ids_row = blocks
    ids_col = blocks.reshape(-1, 1)
    heads_shape = shape((tokens * 3 // 2, 2 * HD), bf16)
    folded = shape((tokens // 2, 2 * HD), bf16)
    part_shape = shape((chunk, d_model), bf16)
    chunk_shape = shape((chunk, d_model), f32)
    full_shape = shape((tokens, d_model), bf16)
    gain_shape = shape((1, d_model), f32)
    forward_shape = shape((chunk, d_model + width), bf16)
    pack_scratch = pltpu.VMEM((4, tokens * 3 // 2, 2 * HD), bf16)
    part_scratch = pltpu.VMEM((tokens, d_model), bf16)
    kv_scratch = [
        pltpu.VMEM((4 * tokens, HD), bf16),
        pltpu.VMEM((4 * tokens, HD), bf16),
        pltpu.VMEM((4 * tokens, 1), jnp.int32),
    ]
    x = inputs[0]
    h_chunk = None
    names = table = None
    kept = []
    for l in range(layers):
        if l == 0:
            h1, *es = kernel_call(
                functools.partial(qkv_first_kernel, plan=plan, row=l),
                "qkv_first",
                [full_shape] + [heads_shape] * 4,
                idx,
                [x, gains, *w_qkv[l]],
                [pack_scratch],
            )
            firsts, seconds = after((first_picks, second_picks), es[0])
            firsts = jnp.swapaxes(firsts[:, 0, 0], 1, 2)
            seconds = jnp.swapaxes(seconds[:, 0, 0].reshape(layers, tokens, -1), 1, 2)
            height = layers * (8 + seconds.shape[1])
            outbox, *tables = kernel_call(
                functools.partial(slots_kernel, plan=plan, gbits=gbits, dbits=dbits),
                "pick_slots",
                [shape((owners, 16 * layers, lanes), bf16)] + [shape((height, chunk), jnp.int32)] * 4,
                idx,
                [firsts, seconds],
                [pltpu.VMEM((4, height, chunk), jnp.int32)],
            )
            (table,) = kernel_call(
                functools.partial(pick_table_kernel, plan=plan),
                "pick_table",
                [shape((layers, height // layers, tokens), jnp.int32)],
                idx,
                swaps(tables, TA),
                [pltpu.VMEM((4, height, chunk), jnp.int32)],
            )
        else:
            h1, *es = kernel_call(
                functools.partial(qkv_kernel, plan=plan),
                "qkv",
                [full_shape] + [heads_shape] * 4,
                idx,
                [*spread(h_chunk, TA), *w_qkv[l]],
                [pack_scratch],
            )
        es = swaps(es, SA)
        if l > 0:
            tied = after([*es, *kept[-1][-1]])
            es = list(tied[:4])
            kept[-1] = kept[-1][:-1] + (list(tied[4:]),)
        heads = kernel_call(
            functools.partial(attend_kernel, plan=plan),
            "attend",
            [folded] * 4,
            idx,
            [*es, ids_row, ids_col],
            kv_scratch,
        )
        attended, *parts = kernel_call(
            functools.partial(out_kernel, plan=plan),
            "attend_out",
            [shape((tokens, width), bf16)] + [part_shape] * 4,
            idx,
            [*swaps(heads, SA), *w_o[l]],
            [pltpu.VMEM((4, tokens, HD), bf16), part_scratch],
        )
        if l == 0:
            (outbox,) = after((outbox,), parts[0])
            names = lax.all_to_all(outbox, ("ctx", "tp"), 0, 0, tiled=True)
        middle, h2, u, w, outbox = kernel_call(
            functools.partial(lookup_kernel, plan=plan, row=layers + l, layer=l, shards=shards),
            "lookup",
            [
                chunk_shape,
                part_shape,
                shape((chunk, 8 * HD), bf16),
                shape((32, tokens), f32),
                shape((owners, 32, lanes), bf16),
            ],
            idx,
            [x, *swaps(parts, TA), gains, w_look[l], table],
        )
        weights = lax.all_to_all(outbox, ("ctx", "tp"), 0, 0, tiled=True)
        (gate,) = kernel_call(
            functools.partial(gate_values_kernel, shards=shards),
            "gate_values",
            [chunk_shape],
            idx,
            [h2, w_gate[l]],
        )
        *reads, dense = read_call(idx, weights, names, l, values, plan, tokens)
        sums = kernel_call(sum_kernel, "memory_sum", [part_shape] * 4, idx, swaps(reads, "ctx"))
        last = l + 1 == layers
        mem, z, x3, h_chunk, *messages = kernel_call(
            functools.partial(gate_kernel, plan=plan, row=None if last else l + 1, shards=shards),
            "gate",
            [chunk_shape, part_shape, chunk_shape, part_shape] + [forward_shape] * 4,
            idx,
            [*swaps(sums, "tp"), gate, w_mem[l], middle, h2, gains],
        )
        kept.append((x, h1, es, attended, middle, u, w, gate, dense, mem, swaps(messages, TA)))
        x = x3
    out_chunks = spread(h_chunk, TA)

    g = cotangent[0]
    packs = [None] * layers
    gain_rows = [None] * (2 * layers)
    table_grads = None
    table_list = [None] * layers
    gy = gn = gg = None
    output = None
    for l in reversed(range(layers)):
        x, h1, es, attended, middle, u, w, gate, dense, mem, messages = kept[l]
        top = l == layers - 1
        if top:
            gy, gn, gg = kernel_call(
                functools.partial(start_back_kernel, plan=plan, shards=shards),
                "start_back",
                [part_shape] * 3,
                idx,
                [g, w_mem[l], gate, mem],
            )
        line = jnp.concatenate(spread(gn, "tp"), axis=0)
        *dvs, gw = write_call(idx, spread(line, "ctx"), names, l, dense, values, plan, tokens)
        if top:
            gw, *out_chunks = after([gw, *out_chunks])
            (output,) = kernel_call(
                functools.partial(place_kernel, plan=plan), "output", [full_shape], idx, out_chunks
            )
        gw = lax.all_to_all(gw, ("ctx", "tp"), 0, 0, tiled=True)
        back_shape = shape((chunk, width + 10 * HD + (0 if top else d_model)), bf16)
        g_mid, go_chunk, gain_rows[layers + l], *back = kernel_call(
            functools.partial(lookup_back_kernel, plan=plan, row=layers + l, layer=l, shards=shards),
            "lookup_back",
            [chunk_shape, part_shape, gain_shape] + [back_shape] * 4,
            idx,
            [gw, table, w, w_look[l], u, gg, gy, w_gate[l], middle, g, gains],
            [
                pltpu.VMEM(w.shape, f32),
                pltpu.VMEM(u.shape, bf16),
                pltpu.VMEM((4, NSUB // 4, 8 * HD), bf16),
                pltpu.VMEM((chunk, d_model), f32),
            ],
        )
        go, *ups = kernel_call(
            functools.partial(out_back_kernel, plan=plan),
            "attend_out_back",
            [full_shape] + [folded] * 4,
            idx,
            [*spread(go_chunk, TA), *w_o[l]],
            [pltpu.VMEM((4, tokens // 2, 2 * HD), bf16)],
        )
        shard_size = d_model // shards
        (memory_pack,) = kernel_call(
            functools.partial(memory_grad_kernel, plan=plan, has_full=top),
            "memory_grad",
            [shape((shards, shard_size * 5 // 2 + NSUB // shards // 2, 256), bf16)],
            idx,
            [*messages, *swaps(back, TA)] + ([cotangent[0]] if top else []),
            [
                pltpu.VMEM((tokens, d_model), bf16),
                pltpu.VMEM((tokens, width), bf16),
                pltpu.VMEM((tokens, width), bf16),
                pltpu.VMEM((tokens, 2 * HD), bf16),
                pltpu.VMEM((tokens, d_model), bf16),
            ],
        )
        (out_pack,) = kernel_call(
            out_grad_kernel, "out_grad", [shape((shards, shard_size, 256), bf16)], idx, [attended, go]
        )
        head_grads = kernel_call(
            functools.partial(attend_back_kernel, plan=plan),
            "attend_back",
            [heads_shape] * 4,
            idx,
            [*es, *swaps(ups, SA), ids_row, ids_col],
            kv_scratch + [pltpu.VMEM((4 * tokens, HD), f32)] * 2,
        )
        g_qkv, *parts = kernel_call(
            functools.partial(qkv_back_kernel, plan=plan),
            "qkv_back",
            [shape((tokens, 3 * width), bf16)] + [part_shape] * 4,
            idx,
            [*swaps(head_grads, SA), *w_qkv[l]],
            [pack_scratch, part_scratch],
        )
        if l > 0:
            below = kept[l - 1]
            g, gy, gain_rows[l], gn, gg = kernel_call(
                functools.partial(norm_back_kernel, plan=plan, row=l, shards=shards),
                "norm_back",
                [chunk_shape, part_shape, gain_shape, part_shape, part_shape],
                idx,
                [*swaps(parts, TA), x, g_mid, gains, w_mem[l - 1], below[7], below[9]],
            )
        else:
            g, gain_rows[l] = kernel_call(
                functools.partial(norm_back_last_kernel, plan=plan, row=l),
                "norm_back_last",
                [part_shape, gain_shape],
                idx,
                [*swaps(parts, TA), x, g_mid, gains],
            )
        qkv_rows = 3 * shard_size
        if l == 0 and shards == 2:
            mine, other = kernel_call(
                qkv_grad_split_kernel,
                "qkv_grad",
                [shape((qkv_rows, 256), bf16)] * 2,
                idx,
                [h1, g_qkv],
                [pltpu.VMEM((d_model, 3 * width), f32)],
            )
            quarter = shape((qkv_rows // 4, 256), bf16)
            parts = kernel_call(
                add_two_kernel, "qkv_add", [quarter] * 4, idx, [mine, swap(other, "fsdp", 1)]
            )
            (part,) = kernel_call(add_four_kernel, "qkv_sum", [quarter], idx, swaps(parts, "ctx"))
            late = spread(part, "ctx")
            group = (memory_pack, out_pack)
        else:
            (pack,) = kernel_call(
                qkv_grad_kernel, "qkv_grad", [shape((shards, qkv_rows, 256), bf16)], idx, [h1, g_qkv]
            )
            late = []
            group = (memory_pack, out_pack, pack)
        if l + 1 < layers:
            group = after(group, *packs[l + 1])
        scattered = [lax.psum_scatter(p, "fsdp", scatter_dimension=0, tiled=False) for p in group]
        packs[l] = [lax.psum(p, "ctx") for p in scattered] + late
        if shards == 2:
            arrived = swap(dvs[1], "fsdp", 1)
            table_grads = table_grad_call(dvs[0], arrived, l, layers, table_grads)
        else:
            table_list[l] = lax.psum_scatter(dvs[0], "fsdp", scatter_dimension=0, tiled=True).astype(f32)
    (input_gradient,) = kernel_call(
        functools.partial(place_kernel, plan=plan),
        "input_gradient",
        [shape((tokens, d_model), f32)],
        idx,
        spread(g, TA),
    )
    if shards != 2:
        table_grads = jnp.stack(table_list)
    gain_all = jnp.concatenate(gain_rows, axis=0)
    for axis in ("tp", "ctx"):
        arrived = spread(gain_all, axis)
        gain_all = (arrived[0] + arrived[1]) + (arrived[2] + arrived[3])
    gain_all = lax.psum_scatter(gain_all, "fsdp", scatter_dimension=1, tiled=True) if shards != 2 else (
        lax.dynamic_slice_in_dim(gain_all + swap(gain_all, "fsdp", 1), idx[0] * (d_model // 2), d_model // 2, 1)
    )
    shard_size = d_model // shards
    tall = shape((layers, shard_size, width), f32)
    wide = shape((layers, width, shard_size), f32)
    sub = shape((layers, 1, NSUB // shards, HD), f32)
    flat = [p for l in range(layers) for p in packs[l]]
    grads = kernel_call(
        functools.partial(finalize_kernel, layers=layers, late=len(packs[0]) > 3),
        "finalize",
        [tall, tall, tall, wide, shape((layers, shard_size, 2 * HD), f32), tall, wide, sub, sub],
        idx,
        flat,
        [pltpu.VMEM((3 * shard_size, 256), bf16)],
        limit=48,
    )
    return (
        output[None],
        input_gradient[None],
        *grads,
        gain_all[:layers],
        gain_all[layers:],
        table_grads,
    )


def solution(mesh):
    placed = (
        P("fsdp", "ctx", None),
        P(None, "fsdp", "tp"),
        P(None, "fsdp", "tp"),
        P(None, "fsdp", "tp"),
        P(None, "tp", "fsdp"),
        P(None, "fsdp", "tp"),
        P(None, "fsdp", "tp"),
        P(None, "tp", "fsdp"),
        P(None, "tp", "fsdp", None),
        P(None, "tp", "fsdp", None),
        P(None, "fsdp"),
        P(None, "fsdp"),
        P(None, ("fsdp", "ctx", "tp"), None),
        P("fsdp", None),
        P(None, "fsdp", "tp", "ctx", None),
        P(None, "fsdp", "tp", "ctx", None, None),
        P("fsdp", "ctx", None),
    )
    return jax.shard_map(
        body,
        mesh=mesh,
        in_specs=placed,
        out_specs=(
            P("fsdp", "ctx", None),
            P("fsdp", "ctx", None),
            P(None, "fsdp", "tp"),
            P(None, "fsdp", "tp"),
            P(None, "fsdp", "tp"),
            P(None, "tp", "fsdp"),
            P(None, "fsdp", "tp"),
            P(None, "fsdp", "tp"),
            P(None, "tp", "fsdp"),
            P(None, "tp", "fsdp", None),
            P(None, "tp", "fsdp", None),
            P(None, "fsdp"),
            P(None, "fsdp"),
            P(None, ("fsdp", "ctx", "tp"), None),
        ),
        check_vma=False,
    )
```

```python
import functools

import jax
import jax.numpy as jnp
from jax import lax
from jax.experimental import pallas as pl
from jax.experimental.pallas import tpu as pltpu
from jax.sharding import PartitionSpec as P

HD = 64
NSUB = 256
CAP = 8
EPS = 1e-05
NEG = -1e30
f32 = jnp.float32
bf16 = jnp.bfloat16
MIB = 1 << 20


def dot(a, b):
    return jnp.dot(a, b, preferred_element_type=f32)


def dot_nt(a, b):
    return lax.dot_general(a, b, (((1,), (1,)), ((), ())), preferred_element_type=f32)


def dot_tn(a, b):
    return lax.dot_general(a, b, (((0,), (0,)), ((), ())), preferred_element_type=f32)


def swap(x, axis, step):
    size = lax.axis_size(axis)
    return lax.ppermute(x, axis, [(i, i ^ step) for i in range(size)])


def swaps(xs, axis):
    return [xs[0]] + [swap(xs[d], axis, d) for d in range(1, len(xs))]


def spread(x, axis):
    return [x] + [swap(x, axis, d) for d in range(1, lax.axis_size(axis))]


def shape(dims, dtype):
    return jax.ShapeDtypeStruct(dims, dtype)


def kernel_call(body, name, outs, idx, args, scratch=(), limit=50, flops=0):
    in_specs = [pl.BlockSpec(memory_space=pltpu.SMEM)]
    in_specs += [pl.BlockSpec(memory_space=pltpu.VMEM) for _ in args]
    moved = sum(a.size * a.dtype.itemsize for a in args)
    moved += sum(o.size * o.dtype.itemsize for o in outs)
    out = pl.pallas_call(
        body,
        out_shape=outs,
        in_specs=in_specs,
        out_specs=[pl.BlockSpec(memory_space=pltpu.VMEM) for _ in outs],
        scratch_shapes=list(scratch),
        compiler_params=pltpu.CompilerParams(vmem_limit_bytes=limit * MIB),
        cost_estimate=pl.CostEstimate(flops=flops, bytes_accessed=moved, transcendentals=0),
        name=name,
    )(idx, *args)
    return list(out)


def rows_at(index, count):
    return pl.ds(pl.multiple_of(index * count, count), count)


def rms(x, gain):
    factor = lax.rsqrt(jnp.mean(x * x, axis=1, keepdims=True) + EPS)
    return factor, x * factor * gain


def rms_back(x, factor, gain, upstream):
    scaled = upstream * gain
    return factor * scaled - x * factor**3 * jnp.mean(scaled * x, axis=1, keepdims=True)


def total4(refs):
    return (refs[0][...].astype(f32) + refs[1][...].astype(f32)) + (
        refs[2][...].astype(f32) + refs[3][...].astype(f32)
    )


def fold(x):
    half = x.shape[0] // 2
    return jnp.concatenate([x[:half], x[half:]], axis=1)


def unfold(x):
    half = x.shape[1] // 2
    return jnp.concatenate([x[:, :half], x[:, half:]], axis=0)


class Plan:
    def __init__(self, SA, TA):
        self.SA, self.TA = SA, TA
        self.si = 1 if SA == "ctx" else 2
        self.ti = 1 if TA == "ctx" else 2

    def src(self, sa, ta):
        return sa * 4 + ta if self.SA == "ctx" else ta * 4 + sa

    def rel(self, ds, dt):
        return (ds, dt) if self.SA == "ctx" else (dt, ds)


PLAN = Plan("ctx", "tp")


def slots_kernel(idx, first_ref, second_ref, out_ref, t0, t1, t2, t3, table, plan, gbits, dbits):
    layers, picks, tokens = first_ref.shape
    inner = second_ref.shape[1]
    owners, _, width = out_ref.shape
    lanes = owners * width
    chunk = tokens // 4
    iota = lax.broadcasted_iota(jnp.int32, (NSUB, tokens), 0)
    before = lax.broadcasted_iota(jnp.int32, (tokens, tokens), 0) < lax.broadcasted_iota(
        jnp.int32, (tokens, tokens), 1
    )
    before = jnp.where(before, 1.0, 0.0).astype(bf16)
    row = lax.broadcasted_iota(jnp.int32, (lanes, tokens), 0)
    token_row = (lax.broadcasted_iota(jnp.int32, (8, tokens), 1) + 1).astype(f32)
    token_row = jnp.where(
        lax.broadcasted_iota(jnp.int32, (8, tokens), 0) == 0, token_row, 0.0
    )
    for l in range(layers):
        onehot = jnp.zeros((NSUB, tokens), f32)
        for i in range(picks):
            onehot = jnp.where(iota == first_ref[l, i : i + 1, :], 1.0, onehot)
        counts = dot(onehot.astype(bf16), before)
        total = jnp.zeros((16, lanes), f32)
        slots = []
        for i in range(picks):
            first = first_ref[l, i : i + 1, :]
            rank = jnp.sum(jnp.where(iota == first, counts, 0.0), axis=0, keepdims=True)
            shard = lax.shift_right_logical(first, gbits)
            group = lax.shift_right_logical(shard, dbits) * (1 << gbits) + (first & ((1 << gbits) - 1))
            slot = (shard & ((1 << dbits) - 1)) * width + group * CAP + rank.astype(jnp.int32)
            slots.append(slot)
            names = jnp.concatenate(
                [second_ref[l, 8 * i : 8 * i + 8, :].astype(f32), token_row], axis=0
            )
            hit = jnp.where(row == slot, 1.0, 0.0).astype(bf16)
            total = total + dot_nt(names.astype(bf16), hit)
        for d in range(owners):
            out_ref[d, 16 * l : 16 * l + 16, :] = total[:, d * width : (d + 1) * width].astype(bf16)
        both = jnp.concatenate([first_ref[l], jnp.concatenate(slots, axis=0)], axis=0)
        for n in range(4):
            cut = slice(n * chunk, (n + 1) * chunk)
            at = l * (8 + inner)
            table[n, at : at + 8, :] = both[:, cut]
            table[n, at + 8 : at + 8 + inner, :] = second_ref[l, :, cut]
    for d, out in enumerate((t0, t1, t2, t3)):
        out[...] = table[idx[plan.ti] ^ d]


def pick_table_kernel(idx, t0, t1, t2, t3, out_ref, table, plan):
    for d, t in enumerate((t0, t1, t2, t3)):
        table[idx[plan.ti] ^ d] = t[...]
    rows = out_ref.shape[1]
    for l in range(out_ref.shape[0]):
        out_ref[l] = jnp.concatenate([table[n, rows * l : rows * (l + 1), :] for n in range(4)], axis=1)


def head_mask(shape_, lanes_each):
    return lax.broadcasted_iota(jnp.int32, shape_, 1) // lanes_each


def place_chunks(refs, full, t):
    count = refs[0].shape[0]
    for d in range(4):
        full[rows_at(t ^ d, count), :] = refs[d][...]


def emit_chunks(part, outs, t):
    count = outs[0].shape[0]
    for d in range(4):
        outs[d][...] = part[rows_at(t ^ d, count), :]


def piece_at(f, j, pieces, size):
    return rows_at(f ^ j, size) if len(pieces) > 1 else slice(0, size)


def emit_heads(h_ref, pieces, pack, outs, idx, plan):
    width = pieces[0].shape[1] // 3
    size = pieces[0].shape[0]
    qkv = sum(
        dot(h_ref[:, piece_at(idx[0], j, pieces, size)], w[...]) for j, w in enumerate(pieces)
    ).astype(bf16)
    for j in range(4):
        q = qkv[:, HD * j : HD * (j + 1)]
        k = qkv[:, width + HD * j : width + HD * (j + 1)]
        v = qkv[:, 2 * width + HD * j : 2 * width + HD * (j + 1)]
        pack[j] = jnp.concatenate([jnp.concatenate([q, k], axis=1), fold(v)], axis=0)
    for d in range(4):
        outs[d][...] = pack[idx[plan.si] ^ d]


def qkv_first_kernel(idx, x_ref, gain_ref, *refs, plan, row):
    *pieces, h_ref, e0, e1, e2, e3, pack = refs
    _, normed = rms(x_ref[...].astype(f32), gain_ref[row : row + 1, :])
    h_ref[...] = normed.astype(bf16)
    emit_heads(h_ref, pieces, pack, (e0, e1, e2, e3), idx, plan)


def qkv_kernel(idx, h0, h1, h2, h3, *refs, plan):
    *pieces, h_ref, e0, e1, e2, e3, pack = refs
    place_chunks((h0, h1, h2, h3), h_ref, idx[plan.ti])
    emit_heads(h_ref, pieces, pack, (e0, e1, e2, e3), idx, plan)


def load_heads(es, kk, vv):
    for d in range(4):
        rows = es[d].shape[0] * 2 // 3
        kk[rows * d : rows * (d + 1), :] = es[d][0:rows, HD : 2 * HD]
        vv[rows * d : rows * (d + 1), :] = unfold(es[d][rows:, :])


def load_ids(col_ref, ids_col, s):
    count = col_ref.shape[0] // 4
    for d in range(4):
        ids_col[count * d : count * (d + 1), :] = col_ref[rows_at(s ^ d, count), :]


def probabilities(kk, q, key_ids, query_ids):
    scores = dot_nt(kk, q) * (HD ** (-0.5))
    scores = jnp.where(key_ids <= query_ids, scores, NEG)
    top = jnp.max(scores, axis=0, keepdims=True)
    exponent = jnp.exp(scores - top)
    return exponent * (1.0 / jnp.sum(exponent, axis=0, keepdims=True))


def attend_kernel(idx, e0, e1, e2, e3, row_ref, col_ref, a0, a1, a2, a3, kk, vv, ids_col, plan):
    es, outs = (e0, e1, e2, e3), (a0, a1, a2, a3)
    s = idx[plan.si]
    load_heads(es, kk, vv)
    load_ids(col_ref, ids_col, s)
    count = kk.shape[0] // 4
    for d in range(4):
        query_ids = row_ref[:, rows_at(s ^ d, count)]
        p = probabilities(kk[...], es[d][0:count, 0:HD], ids_col[...], query_ids)
        blended = dot_tn(vv[...], p.astype(bf16))
        outs[d][...] = fold(blended.T.astype(bf16))


def attend_back_kernel(
    idx, e0, e1, e2, e3, u0, u1, u2, u3, row_ref, col_ref, g0, g1, g2, g3, kk, vv, ids_col, gk, gv, plan
):
    es, us, outs = (e0, e1, e2, e3), (u0, u1, u2, u3), (g0, g1, g2, g3)
    s = idx[plan.si]
    load_heads(es, kk, vv)
    load_ids(col_ref, ids_col, s)
    count = kk.shape[0] // 4
    scale = HD ** (-0.5)
    for d in range(4):
        query_ids = row_ref[:, rows_at(s ^ d, count)]
        q = es[d][0:count, 0:HD]
        up = unfold(us[d][...])
        p = probabilities(kk[...], q, ids_col[...], query_ids)
        gp = dot_nt(vv[...], up)
        centre = jnp.sum(p * gp, axis=0, keepdims=True)
        gs = (p * (gp - centre)).astype(bf16)
        gq = (dot_tn(kk[...], gs) * scale).T.astype(bf16)
        outs[d][0:count, 0:HD] = gq
        key_term = dot(gs, q)
        value_term = dot(p.astype(bf16), up)
        if d == 0:
            gk[...] = key_term
            gv[...] = value_term
        else:
            gk[...] += key_term
            gv[...] += value_term
    for d in range(4):
        outs[d][0:count, HD : 2 * HD] = (gk[count * d : count * (d + 1), :] * scale).astype(bf16)
        outs[d][count:, :] = fold(gv[count * d : count * (d + 1), :].astype(bf16))


def out_kernel(idx, a0, a1, a2, a3, *refs, plan):
    *pieces, a_ref, p0, p1, p2, p3, heads, part = refs
    for d, a in enumerate((a0, a1, a2, a3)):
        heads[idx[plan.si] ^ d] = unfold(a[...])
    a_ref[...] = jnp.concatenate([heads[j] for j in range(4)], axis=1)
    size = pieces[0].shape[1]
    for j, w in enumerate(pieces):
        part[:, piece_at(idx[0], j, pieces, size)] = dot(a_ref[...], w[...]).astype(bf16)
    emit_chunks(part, (p0, p1, p2, p3), idx[plan.ti])


def out_back_kernel(idx, g0, g1, g2, g3, *refs, plan):
    *pieces, go_ref, u0, u1, u2, u3, pack = refs
    place_chunks((g0, g1, g2, g3), go_ref, idx[plan.ti])
    size = pieces[0].shape[1]
    up = sum(
        dot_nt(go_ref[:, piece_at(idx[0], j, pieces, size)], w[...]) for j, w in enumerate(pieces)
    ).astype(bf16)
    for j in range(4):
        pack[j] = fold(up[:, HD * j : HD * (j + 1)])
    for d, u in enumerate((u0, u1, u2, u3)):
        u[...] = pack[idx[plan.si] ^ d]


def qkv_back_kernel(idx, g0, g1, g2, g3, *refs, plan):
    *pieces, g_ref, p0, p1, p2, p3, pack, part = refs
    for d, g in enumerate((g0, g1, g2, g3)):
        pack[idx[plan.si] ^ d] = g[...]
    rows = g_ref.shape[0]
    columns = [pack[j, 0:rows, 0:HD] for j in range(4)]
    columns += [pack[j, 0:rows, HD : 2 * HD] for j in range(4)]
    columns += [unfold(pack[j, rows:, :]) for j in range(4)]
    g_ref[...] = jnp.concatenate(columns, axis=1)
    size = pieces[0].shape[0]
    for j, w in enumerate(pieces):
        part[:, piece_at(idx[0], j, pieces, size)] = dot_nt(g_ref[...], w[...]).astype(bf16)
    emit_chunks(part, (p0, p1, p2, p3), idx[plan.ti])


def to_pack(x):
    rows, width = x.shape
    if width >= 256:
        return jnp.concatenate([x[:, 256 * i : 256 * (i + 1)] for i in range(width // 256)], axis=0)
    fold_by = 256 // width
    rows = rows // fold_by
    return jnp.concatenate([x[rows * i : rows * (i + 1)] for i in range(fold_by)], axis=1)


def from_pack(p, rows, width):
    if width >= 256:
        return jnp.concatenate([p[rows * i : rows * (i + 1)] for i in range(width // 256)], axis=1)
    return jnp.concatenate([p[:, width * i : width * (i + 1)] for i in range(256 // width)], axis=0)


def shard_rows(x, f, shards):
    size = x.shape[0] // shards
    return x[size * f : size * (f + 1)]


def shard_columns(x, f, shards):
    size = x.shape[1] // shards
    return x[:, size * f : size * (f + 1)]


def emit_shards(pack, outs, idx):
    if len(outs) == 1:
        outs[0][...] = pack[...]
    else:
        outs[0][...] = pack[idx[0]]
        outs[1][...] = pack[idx[0] ^ 1]


def qkv_grad_kernel(idx, h_ref, g_ref, *refs):
    *outs, pack = refs
    shards = pack.shape[0]
    change = dot_tn(h_ref[...], g_ref[...])
    for f in range(shards):
        pack[f] = to_pack(shard_rows(change, f, shards)).astype(bf16)
    emit_shards(pack, outs, idx)


def weight_grad_kernel(idx, *refs, plan, has_full):
    forward, back, near, (a_ref, go_ref) = refs[0], refs[1], refs[2:6], refs[6:8]
    full = refs[8] if has_full else None
    *outs, pack, h, z, gg, gu, gy = refs[8 + has_full :]
    chunk = forward.shape[1]
    d_model = h.shape[1]
    quarter = z.shape[1]
    shards = pack.shape[0]
    tables = jnp.zeros((NSUB, 2 * HD), f32)
    mine = rows_at(idx[plan.ti], quarter)
    for d in range(4):
        at = slice(chunk * d, chunk * (d + 1))
        h[at, :] = forward[d, :, 0:d_model]
        z[at, :] = forward.at[:, :, d_model:][d, :, mine]
        gg[at, :] = back.at[:, :, 0:d_model][d, :, mine]
        gu[rows_at(idx[plan.ti] ^ d, chunk), :] = near[d][:, 0 : 2 * HD]
        folded = near[d][:, 2 * HD :].astype(f32)
        tables = tables + jnp.concatenate(
            [folded[:, 2 * HD * i : 2 * HD * (i + 1)] for i in range(4)], axis=0
        )
        gy[at, :] = full[at, :] if has_full else back[d, :, d_model:]
    gate_change = dot_tn(h[...], gg[...])
    look_change = dot_tn(h[...], gu[...])
    mem_change = dot_tn(z[...], gy[...])
    out_change = dot_tn(a_ref[...], go_ref[...])
    for f in range(shards):
        pack[f] = jnp.concatenate(
            [
                to_pack(shard_rows(gate_change, f, shards)),
                to_pack(shard_columns(mem_change, f, shards)),
                to_pack(shard_rows(look_change, f, shards)),
                to_pack(shard_rows(tables, f, shards)),
                to_pack(shard_columns(out_change, f, shards)),
            ],
            axis=0,
        ).astype(bf16)
    emit_shards(pack, outs, idx)


def finalize_kernel(idx, *refs, layers, late):
    ins = refs[: 2 * layers + 3 * late]
    outs = refs[2 * layers + 3 * late :]
    q_ref, k_ref, v_ref, o_ref, look_ref, gate_ref, mem_ref, first_ref, second_ref = outs[:9]
    part = q_ref.shape[1]
    for l in range(layers):
        memory = ins[l]
        if l > 0 or not late:
            qkv = ins[layers + l - late]
        else:
            one_ref, two_ref, qkv = outs[9:]
            rows = qkv.shape[0] // 4
            total = 0.0
            for d in range(4):
                chunk = ins[2 * layers - 1 + d]
                qkv[rows_at(idx[1] ^ d, rows), :] = chunk[0:rows, :]
                total = total + chunk[rows:, :].astype(f32)
            total = jnp.concatenate([total[0:8], total[8:16]], axis=1)
            one_ref[...] = total[0:layers]
            two_ref[...] = total[layers : 2 * layers]
        for n, ref in enumerate((q_ref, k_ref, v_ref)):
            ref[l] = qkv[part * n : part * (n + 1), :].astype(f32)
        gate_ref[l] = memory[0:part, :].astype(f32)
        mem_ref[l] = from_pack(memory[part : 2 * part, :], mem_ref.shape[1], mem_ref.shape[2]).astype(f32)
        at = 2 * part + part // 2
        look_ref[l] = from_pack(memory[2 * part : at, :].astype(f32), part, look_ref.shape[2])
        rows = first_ref.shape[3]
        tables = from_pack(memory[at : at + rows // 2, :].astype(f32), rows, 2 * HD)
        first_ref[l, 0] = tables[:, :HD].T
        second_ref[l, 0] = tables[:, HD:].T
        at = at + rows // 2
        o_ref[l] = from_pack(memory[at : at + part, :], o_ref.shape[1], o_ref.shape[2]).astype(f32)


def add_pair_kernel(idx, a, b, out):
    out[...] = (a[...].astype(f32) + b[...].astype(f32)).astype(bf16)


def add_two_kernel(idx, a, b, o0, o1, o2, o3):
    chunk = o0.shape[0]
    for d, out in enumerate((o0, o1, o2, o3)):
        at = rows_at(idx[1] ^ d, chunk)
        out[...] = (a[at, :].astype(f32) + b[at, :].astype(f32)).astype(bf16)


def plane_sum_kernel(idx, a0, a1, a2, a3, g0, g1, out):
    rows = a0.shape[0]
    out[0:rows, :] = total4((a0, a1, a2, a3)).astype(bf16)
    out[rows:, :] = (g0[...].astype(f32) + g1[...].astype(f32)).astype(bf16)


def own_rows(ref, idx, plan, count):
    if ref.shape[0] == count:
        return ref[...].astype(f32)
    return ref[rows_at(idx[plan.ti], count), :].astype(f32)


def table_of(a_ref, m, shards):
    size = a_ref.shape[1] * 4 // 5
    both = [a_ref[f * 4 + m, size:, :] for f in range(shards)]
    both = both[0] if shards == 1 else jnp.concatenate(both, axis=0)
    return both[:, :HD], both[:, HD:]


def only_head(x, m, chunk):
    lane = lax.broadcasted_iota(jnp.int32, x.shape, 1)
    return jnp.where((lane >= m * chunk) & (lane < (m + 1) * chunk), x, 0.0)


def lookup_kernel(
    idx, x_ref, p0, r1, r2, r3, gain_ref, a_ref, pick_ref, *refs, plan, row, layer, shards
):
    *names_ref, x_out, h_ref, u_ref, w_ref, out_ref = refs
    chunk = p0.shape[0]
    x = own_rows(x_ref, idx, plan, chunk) + total4((p0, r1, r2, r3))
    x_out[...] = x
    _, normed = rms(x, gain_ref[row : row + 1, :])
    h_ref[...] = normed.astype(bf16)
    size = a_ref.shape[1] * 4 // 5
    c1, c2 = [], []
    for m in range(4):
        u = sum(
            dot(h_ref[:, size * f : size * (f + 1)], a_ref[f * 4 + m, 0:size, :]) for f in range(shards)
        ).astype(bf16)
        u_ref[:, 2 * HD * m : 2 * HD * (m + 1)] = u
        ka, kb = table_of(a_ref, m, shards)
        c1.append(dot_nt(ka, u[:, :HD]))
        c2.append(dot_nt(kb, u[:, HD:]))
    c1 = jnp.concatenate(c1, axis=1)
    c2 = jnp.concatenate(c2, axis=1)
    lanes = c1.shape[1]
    iota = lax.broadcasted_iota(jnp.int32, (NSUB, lanes), 0)
    for i in range(4):
        first = pick_ref[layer, i : i + 1, :]
        base = jnp.sum(jnp.where(iota == first, c1, 0.0), axis=0, keepdims=True)
        for b in range(8):
            r = i * 8 + b
            second = pick_ref[layer, 8 + r : 9 + r, :]
            picked = jnp.sum(jnp.where(iota == second, c2, 0.0), axis=0, keepdims=True)
            w_ref[r : r + 1, :] = base + picked
    logits = w_ref[...]
    exponent = jnp.exp(logits - jnp.max(logits, axis=0, keepdims=True))
    w = exponent * (1.0 / jnp.sum(exponent, axis=0, keepdims=True))
    w_ref[...] = w
    owners, _, width = out_ref.shape
    slots = lax.broadcasted_iota(jnp.int32, (owners * width, lanes), 0)
    total = jnp.zeros((32, owners * width), f32)
    for i in range(4):
        hit = jnp.where(slots == pick_ref[layer, 4 + i : 5 + i, :], 1.0, 0.0).astype(bf16)
        mine = w[8 * i : 8 * (i + 1), :]
        split = jnp.concatenate([only_head(mine, m, chunk) for m in range(4)], axis=0)
        total = total + dot_nt(split.astype(bf16), hit)
    for d in range(owners):
        out_ref[d, 0:32, :] = total[:, d * width : (d + 1) * width].astype(bf16)
        if names_ref:
            out_ref[d, 32:, :] = names_ref[0][d]


def gate_part(b_ref, n):
    return b_ref[n, 0 : b_ref.shape[1] // 2, :]


def memory_part(b_ref, n):
    size = b_ref.shape[1] // 2
    return from_pack(b_ref[n, size:, :], b_ref.shape[2], size)


def gate_values_kernel(idx, h_ref, b_ref, gate_ref, shards):
    size, quarter = b_ref.shape[1] // 2, b_ref.shape[2]
    for t in range(4):
        gate_ref[:, quarter * t : quarter * (t + 1)] = sum(
            dot(h_ref[:, size * f : size * (f + 1)], gate_part(b_ref, f * 4 + t)) for f in range(shards)
        )


def gate_sum(sums, gate_ref, b_ref, x_ref, mem_ref, z_ref, x_out, shards):
    mem = total4(sums)
    mem_ref[...] = mem
    gate = gate_ref[...]
    z_ref[...] = (mem * (gate * jax.nn.sigmoid(gate))).astype(bf16)
    size, quarter = b_ref.shape[1] // 2, b_ref.shape[2]
    for f in range(shards):
        at = slice(size * f, size * (f + 1))
        x_out[:, at] = x_ref[:, at] + sum(
            dot(z_ref[:, quarter * t : quarter * (t + 1)], memory_part(b_ref, f * 4 + t)) for t in range(4)
        )


def gate_kernel(
    idx, s0, s1, s2, s3, gate_ref, b_ref, x_ref, h_ref, gain_ref, mem_ref, box_ref, x_out, h_out, z, row, shards
):
    gate_sum((s0, s1, s2, s3), gate_ref, b_ref, x_ref, mem_ref, z, x_out, shards)
    h_out[...] = rms(x_out[...], gain_ref[row : row + 1, :])[1].astype(bf16)
    fill_box(box_ref, h_ref, z)


def fill_box(box_ref, left_ref, right_ref):
    width = left_ref.shape[1]
    box_ref[:, 0:width] = left_ref[...]
    box_ref[:, width:] = right_ref[...]


def gate_last_kernel(
    idx, s0, s1, s2, s3, gate_ref, b_ref, x_ref, h_ref, g_ref,
    n_ref, box_ref, back_ref, mem, z, x_out, gy, plan, shards,
):
    gate_sum((s0, s1, s2, s3), gate_ref, b_ref, x_ref, mem, z, x_out, shards)
    gy[...] = g_ref[rows_at(idx[plan.ti], gy.shape[0]), :]
    gate_back(gy, b_ref, gate_ref, mem, n_ref, back_ref, shards)
    back_ref[:, gy.shape[1] :] = x_out[...].astype(bf16)
    fill_box(box_ref, h_ref, z)


def gate_back(gy_ref, b_ref, gate_ref, mem_ref, gn_ref, gg_ref, shards):
    size, quarter = b_ref.shape[1] // 2, b_ref.shape[2]
    for t in range(4):
        at = slice(quarter * t, quarter * (t + 1))
        gz = sum(
            dot_nt(gy_ref[:, size * f : size * (f + 1)], memory_part(b_ref, f * 4 + t)) for f in range(shards)
        )
        gate = gate_ref[:, at]
        sigmoid = jax.nn.sigmoid(gate)
        gn_ref[:, at] = (gz * (gate * sigmoid)).astype(bf16)
        slope = sigmoid * (1.0 + gate * (1.0 - sigmoid))
        gg_ref[:, at] = (gz * mem_ref[:, at] * slope).astype(bf16)


def norm_back(idx, parts, x_ref, g_ref, gain_ref, dgain_ref, plan, row):
    count = parts[0].shape[0]
    upstream = total4(parts)
    x = own_rows(x_ref, idx, plan, count)
    gain = gain_ref[row : row + 1, :]
    factor, _ = rms(x, gain)
    dgain_ref[...] = jnp.sum(upstream * x * factor, axis=0, keepdims=True)
    return g_ref[...] + rms_back(x, factor, gain, upstream)


def norm_back_kernel(
    idx, p0, r1, r2, r3, x_ref, g_ref, gain_ref, b_ref, gate_ref, mem_ref,
    gx_ref, dgain_ref, gn_ref, back_ref, gy, plan, row, shards,
):
    gx = norm_back(idx, (p0, r1, r2, r3), x_ref, g_ref, gain_ref, dgain_ref, plan, row)
    gx_ref[...] = gx
    gy[...] = gx.astype(bf16)
    gate_back(gy, b_ref, gate_ref, mem_ref, gn_ref, back_ref, shards)
    back_ref[:, gy.shape[1] :] = gy[...]


def norm_back_last_kernel(idx, p0, r1, r2, r3, x_ref, g_ref, gain_ref, *refs, plan, row):
    *rows, out_ref, dgain = refs
    gx = norm_back(idx, (p0, r1, r2, r3), x_ref, g_ref, gain_ref, dgain, plan, row)
    count = gx.shape[0]
    out_ref[0:count, :] = gx.astype(bf16)
    both = [dgain[...]] + [r[...] for r in rows]
    blank = jnp.zeros((out_ref.shape[0] - count - len(both), gx.shape[1]), f32)
    out_ref[count:, :] = jnp.concatenate(both + [blank], axis=0).astype(bf16)


def input_grad_kernel(idx, c0, c1, c2, c3, out_ref, gain_ref, mine_ref, other_ref, plan):
    chunk = out_ref.shape[0] // 4
    total = 0.0
    for d, c in enumerate((c0, c1, c2, c3)):
        out_ref[rows_at(idx[plan.ti] ^ d, chunk), :] = c[0:chunk, :].astype(f32)
        total = total + c[chunk:, :].astype(f32)
    gain_ref[...] = total
    size = gain_ref.shape[1] // 2
    for j, out in enumerate((mine_ref, other_ref)):
        half = gain_ref[:, rows_at(idx[0] ^ j, size)]
        out[...] = jnp.concatenate([half[:8, 0:256], half[:8, 256:]], axis=0).astype(bf16)


def lookup_back_kernel(
    idx, gw_ref, pick_ref, w_ref, a_ref, u_ref, gg_ref, b_ref, x_ref, g_ref, gain_ref,
    gx_ref, go_ref, dgain_ref, b0, b1, b2, b3, gl, gu_all, tables, gh, plan, row, layer, shards,
):
    chunk = u_ref.shape[0]
    owners, _, width = gw_ref.shape
    lanes = w_ref.shape[1]
    slots = lax.broadcasted_iota(jnp.int32, (owners * width, lanes), 0)
    arrived = jnp.concatenate([gw_ref[d] for d in range(owners)], axis=1)
    for i in range(4):
        hit = jnp.where(slots == pick_ref[layer, 4 + i : 5 + i, :], 1.0, 0.0).astype(bf16)
        mixed = dot(arrived, hit)
        gl[8 * i : 8 * (i + 1), :] = sum(
            only_head(mixed[8 * m : 8 * (m + 1), :], m, chunk) for m in range(4)
        )
    w = w_ref[...]
    gw = gl[...]
    gl[...] = w * (gw - jnp.sum(w * gw, axis=0, keepdims=True))
    iota = lax.broadcasted_iota(jnp.int32, (NSUB, lanes), 0)
    gc1 = jnp.zeros((NSUB, lanes), f32)
    gc2 = jnp.zeros((NSUB, lanes), f32)
    for i in range(4):
        both = jnp.sum(gl[8 * i : 8 * (i + 1), :], axis=0, keepdims=True)
        gc1 = jnp.where(iota == pick_ref[layer, i : i + 1, :], both, gc1)
        for b in range(8):
            r = i * 8 + b
            gc2 = gc2 + jnp.where(iota == pick_ref[layer, 8 + r : 9 + r, :], gl[r : r + 1, :], 0.0)
    gc1 = gc1.astype(bf16)
    gc2 = gc2.astype(bf16)
    for m in range(4):
        ka, kb = table_of(a_ref, m, shards)
        one = gc1[:, chunk * m : chunk * (m + 1)]
        two = gc2[:, chunk * m : chunk * (m + 1)]
        gu_all[:, 2 * HD * m : 2 * HD * (m + 1)] = jnp.concatenate(
            [dot_tn(one, ka), dot_tn(two, kb)], axis=1
        ).astype(bf16)
        change = jnp.concatenate(
            [
                dot(one, u_ref[:, 2 * HD * m : 2 * HD * m + HD]),
                dot(two, u_ref[:, 2 * HD * m + HD : 2 * HD * (m + 1)]),
            ],
            axis=1,
        ).astype(bf16)
        tables[m] = jnp.concatenate(
            [change[NSUB // 4 * n : NSUB // 4 * (n + 1), :] for n in range(4)], axis=1
        )
    size, quarter = b_ref.shape[1] // 2, b_ref.shape[2]
    for f in range(shards):
        gh[:, size * f : size * (f + 1)] = sum(
            dot_nt(gg_ref[:, quarter * t : quarter * (t + 1)], gate_part(b_ref, f * 4 + t))
            + dot_nt(gu_all[:, 2 * HD * t : 2 * HD * (t + 1)], a_ref[f * 4 + t, 0:size, :])
            for t in range(4)
        )
    upstream = gh[...]
    x = x_ref[...]
    gain = gain_ref[row : row + 1, :]
    factor, _ = rms(x, gain)
    dgain_ref[...] = jnp.sum(upstream * x * factor, axis=0, keepdims=True)
    gx = own_rows(g_ref, idx, plan, chunk) + rms_back(x, factor, gain, upstream)
    gx_ref[...] = gx
    go_ref[...] = gx.astype(bf16)
    for d, out in enumerate((b0, b1, b2, b3)):
        n = idx[plan.ti] ^ d
        out[:, 0 : 2 * HD] = gu_all[:, rows_at(n, 2 * HD)]
        out[:, 2 * HD : 10 * HD] = tables[n]


STEP_GROUPS = 4


def step_base(idx, step, pieces, per_piece):
    if pieces == 1:
        return step * STEP_GROUPS
    piece = step // per_piece
    return ((idx[0] ^ piece) * per_piece + step % per_piece) * STEP_GROUPS


def read_kernel(idx, w_ref, names_ref, *refs, plan, pieces, per_piece):
    vs = refs[:pieces]
    o0, o1, o2, o3, s_ref, partial, rows = refs[pieces:]
    step = pl.program_id(0)
    sources, _, width = w_ref.shape

    @pl.when(step == 0)
    def _():
        iota = lax.broadcasted_iota(jnp.int32, (NSUB, width), 0).astype(f32)

        def build(sa, carry):
            weights = sum(w_ref[plan.src(sa, ta)].astype(f32) for ta in range(4))
            for m in range(4):
                src = plan.src(sa, m)
                names = names_ref[src].astype(f32)
                dense = jnp.zeros((NSUB, width), f32)
                for b in range(8):
                    r = 8 * m + b
                    dense = jnp.where(iota == names[b : b + 1, :], weights[r : r + 1, :], dense)
                s_ref[src] = dense.T
            return carry

        lax.fori_loop(0, 4, build, 0)

    base = step_base(idx, step, pieces, per_piece)

    def multiply(v_ref):
        for k in range(STEP_GROUPS):
            at = rows_at(base + k, CAP)
            left = s_ref[:, at, :].reshape(sources * CAP, NSUB).astype(bf16)
            got = dot(left, v_ref[NSUB * k : NSUB * (k + 1), :])
            partial[:, at, :] = got.reshape(sources, CAP, v_ref.shape[1])

    for n in range(pieces):
        pl.when(step // per_piece == n)(functools.partial(multiply, vs[n]))

    @pl.when(step == pl.num_programs(0) - 1)
    def _():
        s, t = idx[plan.si], idx[plan.ti]
        tokens = rows.shape[0]
        chunk = tokens // 4
        outs = (o0, o1, o2, o3)
        iota = (lax.broadcasted_iota(jnp.int32, (tokens, width), 0) + 1).astype(f32)
        for ds in range(4):
            hits, parts = [], []
            for m in range(4):
                src = plan.src(s ^ ds, m)
                token = names_ref[src].astype(f32)[8:9, :]
                hits.append(jnp.where(iota == token, 1.0, 0.0).astype(bf16))
                parts.append(partial[src].astype(bf16))
            rows[...] = dot(
                jnp.concatenate(hits, axis=1), jnp.concatenate(parts, axis=0)
            ).astype(bf16)
            for dt in range(4):
                dp, dz = plan.rel(ds, dt)
                outs[dp][chunk * dz : chunk * (dz + 1), :] = rows[rows_at(t ^ dt, chunk), :]


def value_specs(values, layer):
    d_model = values[0].shape[2]
    per_piece = values[0].shape[1] // (STEP_GROUPS * NSUB)
    specs = []
    for n in range(len(values)):
        def index(g, n=n):
            return (layer, jnp.clip(g - n * per_piece, 0, per_piece - 1), 0)

        specs.append(pl.BlockSpec((None, STEP_GROUPS * NSUB, d_model), index))
    return specs, per_piece


def read_call(idx, weights, names, layer, values, plan, tokens):
    sources, _, width = weights.shape
    specs, per_piece = value_specs(values, layer)
    d_model = values[0].shape[2]
    out = shape((tokens, d_model), bf16)
    return pl.pallas_call(
        functools.partial(read_kernel, plan=plan, pieces=len(values), per_piece=per_piece),
        grid=(per_piece * len(values),),
        out_shape=[out, out, out, out, shape((sources, width, NSUB), f32)],
        in_specs=[
            pl.BlockSpec(memory_space=pltpu.SMEM),
            pl.BlockSpec((sources, 32, width), lambda g: (0, 0, 0)),
            pl.BlockSpec((sources, 16, width), lambda g: (0, 2 + layer, 0)),
        ]
        + specs,
        out_specs=[pl.BlockSpec((tokens, d_model), lambda g: (0, 0)) for _ in range(4)]
        + [pl.BlockSpec((sources, width, NSUB), lambda g: (0, 0, 0))],
        scratch_shapes=[
            pltpu.VMEM((sources, width, d_model), f32),
            pltpu.VMEM((tokens, d_model), bf16),
        ],
        compiler_params=pltpu.CompilerParams(vmem_limit_bytes=50 * MIB),
        cost_estimate=pl.CostEstimate(
            flops=4 * sources * width * NSUB * d_model, bytes_accessed=20 * MIB, transcendentals=0
        ),
        name="memory_read",
    )(idx, weights, names, *values)


def write_kernel(idx, g0, g1, g2, g3, names_ref, s_ref, *refs, plan, pieces, per_piece):
    vs, dvs = refs[:pieces], refs[pieces : 2 * pieces]
    gw_ref, grads, partial, cross = refs[2 * pieces :]
    step = pl.program_id(0)
    sources, width, _ = s_ref.shape
    d_model = vs[0].shape[1]

    @pl.when(step == 0)
    def _():
        s, t = idx[plan.si], idx[plan.ti]
        tokens = grads.shape[1]
        chunk = tokens // 4
        for dp, g in enumerate((g0, g1, g2, g3)):
            for dz in range(4):
                ds, dt = plan.rel(dp, dz)
                grads[s ^ ds, rows_at(t ^ dt, chunk), :] = g[chunk * dz : chunk * (dz + 1), :]
        iota = (lax.broadcasted_iota(jnp.int32, (tokens, width), 0) + 1).astype(f32)
        for sa in range(4):
            hits = []
            for m in range(4):
                token = names_ref[plan.src(sa, m)].astype(f32)[8:9, :]
                hits.append(jnp.where(iota == token, 1.0, 0.0).astype(bf16))
            got = dot_tn(jnp.concatenate(hits, axis=1), grads[sa])
            for m in range(4):
                partial[plan.src(sa, m)] = got[width * m : width * (m + 1), :]

    base = step_base(idx, step, pieces, per_piece)

    def multiply(v_ref, dv_ref):
        for k in range(STEP_GROUPS):
            at = rows_at(base + k, CAP)
            cut = slice(NSUB * k, NSUB * (k + 1))
            inbox = partial[:, at, :].reshape(sources * CAP, d_model).astype(bf16)
            left = s_ref[:, at, :].reshape(sources * CAP, NSUB).astype(bf16)
            dv_ref[cut, :] = dot_tn(left, inbox).astype(bf16)
            cross[:, at, :] = dot_nt(inbox, v_ref[cut, :]).reshape(sources, CAP, NSUB)

    for n in range(pieces):
        pl.when(step // per_piece == n)(functools.partial(multiply, vs[n], dvs[n]))

    @pl.when(step == pl.num_programs(0) - 1)
    def _():
        iota = lax.broadcasted_iota(jnp.int32, (NSUB, width), 0).astype(f32)

        def select(sa, carry):
            picked = []
            for m in range(4):
                src = plan.src(sa, m)
                turned = cross[src].T
                names = names_ref[src].astype(f32)
                picked += [
                    jnp.sum(jnp.where(iota == names[b : b + 1, :], turned, 0.0), axis=0, keepdims=True)
                    for b in range(8)
                ]
            picked = jnp.concatenate(picked, axis=0).astype(bf16)
            for ta in range(4):
                gw_ref[plan.src(sa, ta)] = picked
            return carry

        lax.fori_loop(0, 4, select, 0)


def write_call(idx, grads, names, layer, dense, values, plan, tokens):
    sources, width, _ = dense.shape
    specs, per_piece = value_specs(values, layer)
    d_model = values[0].shape[2]
    pieces = len(values)

    def dv_spec(n):
        return pl.BlockSpec(
            (STEP_GROUPS * NSUB, d_model), lambda g: (jnp.clip(g - n * per_piece, 0, per_piece - 1), 0)
        )

    return pl.pallas_call(
        functools.partial(write_kernel, plan=plan, pieces=pieces, per_piece=per_piece),
        grid=(per_piece * pieces,),
        out_shape=[shape((v.shape[1], d_model), bf16) for v in values]
        + [shape((sources, 32, width), bf16)],
        in_specs=[pl.BlockSpec(memory_space=pltpu.SMEM)]
        + [
            pl.BlockSpec((tokens, d_model), lambda g: (0, 0), pipeline_mode=pl.Buffered(1))
            for _ in range(4)
        ]
        + [
            pl.BlockSpec((sources, 16, width), lambda g: (0, 2 + layer, 0)),
            pl.BlockSpec((sources, width, NSUB), lambda g: (0, 0, 0), pipeline_mode=pl.Buffered(1)),
        ]
        + specs,
        out_specs=[dv_spec(n) for n in range(pieces)]
        + [pl.BlockSpec((sources, 32, width), lambda g: (0, 0, 0))],
        scratch_shapes=[
            pltpu.VMEM((4, tokens, d_model), bf16),
            pltpu.VMEM((sources, width, d_model), f32),
            pltpu.VMEM((sources, width, NSUB), f32),
        ],
        compiler_params=pltpu.CompilerParams(vmem_limit_bytes=50 * MIB),
        cost_estimate=pl.CostEstimate(
            flops=6 * sources * width * NSUB * d_model, bytes_accessed=28 * MIB, transcendentals=0
        ),
        name="memory_write",
    )(idx, *grads, names, dense, *values)


def sum_kernel(idx, m0, r1, r2, r3, o0, o1, o2, o3):
    count = o0.shape[0]
    for dz, out in enumerate((o0, o1, o2, o3)):
        at = slice(count * dz, count * (dz + 1))
        out[...] = (
            (m0[at, :].astype(f32) + r1[at, :].astype(f32))
            + (r2[at, :].astype(f32) + r3[at, :].astype(f32))
        ).astype(bf16)


def table_grad_kernel(a_ref, b_ref, *refs):
    refs[-1][...] = a_ref[...].astype(f32) + b_ref[...].astype(f32)


def table_grad_call(mine, arrived, layer, layers, earlier):
    rows, d_model = mine.shape
    block = min(rows, 512)
    specs = [pl.BlockSpec((block, d_model), lambda g: (g, 0))] * 2
    args = [mine, arrived]
    if earlier is not None:
        specs = specs + [pl.BlockSpec(memory_space=pl.ANY)]
        args.append(earlier)
    return pl.pallas_call(
        table_grad_kernel,
        grid=(rows // block,),
        out_shape=shape((layers, rows, d_model), f32),
        in_specs=specs,
        out_specs=pl.BlockSpec((None, block, d_model), lambda g: (layer, g, 0)),
        input_output_aliases={} if earlier is None else {2: 0},
        compiler_params=pltpu.CompilerParams(vmem_limit_bytes=32 * MIB),
        cost_estimate=pl.CostEstimate(flops=0, bytes_accessed=16 * MIB, transcendentals=0),
        name="table_grad",
    )(*args)


def gather_shards(x, axis):
    if lax.axis_size("fsdp") != 2:
        return lax.all_gather(x, "fsdp", axis=axis, tiled=True)
    other = swap(x, "fsdp", 1)
    mine = lax.axis_index("fsdp") == 0
    return jnp.where(
        mine, jnp.concatenate([x, other], axis=axis), jnp.concatenate([other, x], axis=axis)
    )


def shard_pieces(x, axis):
    if lax.axis_size("fsdp") != 2:
        return [lax.all_gather(x, "fsdp", axis=axis, tiled=True)]
    return [x, swap(x, "fsdp", 1)]


def reduce_packs(group):
    scattered = [lax.psum_scatter(p, "fsdp", scatter_dimension=0, tiled=False) for p in group]
    return [lax.psum(p, "ctx") for p in scattered]


def after(xs, *others):
    return list(lax.optimization_barrier((tuple(xs), tuple(others)))[0])


def body(
    inputs,
    query_weight,
    key_weight,
    value_weight,
    attention_weight,
    lookup_weight,
    gate_weight,
    memory_weight,
    first_table,
    second_table,
    attention_gain,
    memory_gain,
    memory_values,
    blocks,
    first_picks,
    second_picks,
    cotangent,
):
    plan = PLAN
    SA, TA = plan.SA, plan.TA
    layers = query_weight.shape[0]
    tokens = inputs.shape[1]
    d_model = inputs.shape[2]
    chunk = tokens // 4
    width = query_weight.shape[2]
    shards = lax.axis_size("fsdp")
    owners = lax.axis_size("ctx") * lax.axis_size("tp")
    groups = memory_values.shape[1] // NSUB
    lanes = shards * groups * CAP
    gbits = groups.bit_length() - 1
    dbits = owners.bit_length() - 1
    idx = jnp.stack(
        [lax.axis_index("fsdp"), lax.axis_index("ctx"), lax.axis_index("tp"), 0]
    ).astype(jnp.int32)

    gains = gather_shards(
        jnp.concatenate([attention_gain, memory_gain], axis=0).astype(bf16), 1
    ).astype(f32)

    def qkv_weight(l, queries, keys, values_):
        joined = jnp.concatenate([queries[l], keys[l], values_[l]], axis=1).astype(bf16)
        return shard_pieces(joined, 0)

    def gather_all(x):
        return lax.all_gather(x, ("fsdp", "tp"), axis=0, tiled=False)

    w_qkv = [qkv_weight(0, query_weight, key_weight, value_weight)]
    w_o, w_a, w_b = [], [], []

    firsts = jnp.swapaxes(first_picks[:, 0, 0], 1, 2)
    seconds = jnp.swapaxes(second_picks[:, 0, 0].reshape(layers, tokens, -1), 1, 2)
    height = layers * (8 + seconds.shape[1])
    name_box, *tables = kernel_call(
        functools.partial(slots_kernel, plan=plan, gbits=gbits, dbits=dbits),
        "pick_slots",
        [shape((owners, 16 * layers, lanes), bf16)] + [shape((height, chunk), jnp.int32)] * 4,
        idx,
        [firsts, seconds],
        [pltpu.VMEM((4, height, chunk), jnp.int32)],
    )
    w_qkv[0][-1], name_box, *tables = after([w_qkv[0][-1], name_box, *tables])
    ids_row = blocks
    ids_col = blocks.reshape(-1, 1)
    heads_shape = shape((tokens * 3 // 2, 2 * HD), bf16)
    folded = shape((tokens // 2, 2 * HD), bf16)
    part_shape = shape((chunk, d_model), bf16)
    chunk_shape = shape((chunk, d_model), f32)
    full_shape = shape((tokens, d_model), bf16)
    gain_shape = shape((1, d_model), f32)
    box_shape = shape((chunk, 2 * d_model), bf16)
    chunk_scratch = pltpu.VMEM((chunk, d_model), bf16)
    pack_scratch = pltpu.VMEM((4, tokens * 3 // 2, 2 * HD), bf16)
    part_scratch = pltpu.VMEM((tokens, d_model), bf16)
    kv_scratch = [
        pltpu.VMEM((4 * tokens, HD), bf16),
        pltpu.VMEM((4 * tokens, HD), bf16),
        pltpu.VMEM((4 * tokens, 1), jnp.int32),
    ]
    x = inputs[0]
    h_chunk = names = table = None
    h_chunks = []
    kept = []
    for l in range(layers):
        if l == 0:
            h1, *es = kernel_call(
                functools.partial(qkv_first_kernel, plan=plan, row=l),
                "qkv_first",
                [full_shape] + [heads_shape] * 4,
                idx,
                [x, gains, *w_qkv[l]],
                [pack_scratch],
            )
            qw, kw, vw, ow, lw, gw_, pw, ta_, tb_, mv = after(
                (
                    query_weight, key_weight, value_weight, attention_weight, lookup_weight,
                    gate_weight, memory_weight, first_table, second_table, memory_values,
                ),
                es[0],
            )
            a_boxes, b_boxes = [], []
            for n in range(layers):
                w_o.append(shard_pieces(ow[n].astype(bf16), 1))
                a_boxes.append(
                    jnp.concatenate(
                        [lw[n], jnp.concatenate([ta_[n, 0], tb_[n, 0]], axis=1)], axis=0
                    ).astype(bf16)
                )
                b_boxes.append(jnp.concatenate([gw_[n], to_pack(pw[n])], axis=0).astype(bf16))
                if n > 0:
                    w_qkv.append(qkv_weight(n, qw, kw, vw))
            w_a.append(gather_all(a_boxes[0]))
        else:
            h1, *es = kernel_call(
                functools.partial(qkv_kernel, plan=plan),
                "qkv",
                [full_shape] + [heads_shape] * 4,
                idx,
                [*h_chunks, *w_qkv[l]],
                [pack_scratch],
            )
        es = swaps(es, SA)
        if l == 0:
            (table,) = kernel_call(
                functools.partial(pick_table_kernel, plan=plan),
                "pick_table",
                [shape((layers, height // layers, tokens), jnp.int32)],
                idx,
                swaps(tables, TA),
                [pltpu.VMEM((4, height, chunk), jnp.int32)],
            )
            if shards == 2:
                values = [memory_values, swap(mv, "fsdp", 1)]
            else:
                values = [lax.all_gather(mv, "fsdp", axis=1, tiled=True)]
        else:
            w_a.append(gather_all(after([a_boxes[l]], h1)[0]))
        heads = kernel_call(
            functools.partial(attend_kernel, plan=plan),
            "attend",
            [folded] * 4,
            idx,
            [*es, ids_row, ids_col],
            kv_scratch,
        )
        heads = swaps(heads, SA)
        if l == 0:
            heads[3], table = after([heads[3], table])
        attended, *parts = kernel_call(
            functools.partial(out_kernel, plan=plan),
            "attend_out",
            [shape((tokens, width), bf16)] + [part_shape] * 4,
            idx,
            [*heads, *w_o[l]],
            [pltpu.VMEM((4, tokens, HD), bf16), part_scratch],
        )
        parts = swaps(parts, TA)
        middle, h2, u, w, outbox = kernel_call(
            functools.partial(lookup_kernel, plan=plan, row=layers + l, layer=l, shards=shards),
            "lookup",
            [
                chunk_shape,
                part_shape,
                shape((chunk, 8 * HD), bf16),
                shape((32, tokens), f32),
                shape((owners, 32 if l else 32 + name_box.shape[1], lanes), bf16),
            ],
            idx,
            [x, *parts, gains, w_a[l], table] + ([] if l else [name_box]),
        )
        weights = lax.all_to_all(outbox, ("ctx", "tp"), 0, 0, tiled=True)
        if l == 0:
            names = weights
        w_b.append(gather_all(after([b_boxes[l]], h2)[0]))
        (gate,) = kernel_call(
            functools.partial(gate_values_kernel, shards=shards),
            "gate_values",
            [chunk_shape],
            idx,
            [h2, w_b[l]],
        )
        *reads, dense = read_call(idx, weights, names, l, values, plan, tokens)
        reads = swaps(reads, "ctx")
        sums = kernel_call(sum_kernel, "memory_sum", [part_shape] * 4, idx, reads)
        sums = swaps(sums, "tp")
        if l + 1 < layers:
            mem, box, x3, h_chunk = kernel_call(
                functools.partial(gate_kernel, row=l + 1, shards=shards),
                "gate",
                [chunk_shape, box_shape, chunk_shape, part_shape],
                idx,
                [*sums, gate, w_b[l], middle, h2, gains],
                [chunk_scratch],
            )
            h_chunks = spread(h_chunk, TA)
        else:
            mem = x3 = None
            gn, box, back_box = kernel_call(
                functools.partial(gate_last_kernel, plan=plan, shards=shards),
                "gate_last",
                [part_shape, box_shape, box_shape],
                idx,
                [*sums, gate, w_b[l], middle, h2, cotangent[0]],
                [
                    pltpu.VMEM((chunk, d_model), f32),
                    chunk_scratch,
                    pltpu.VMEM((chunk, d_model), f32),
                    chunk_scratch,
                ],
            )
        kept.append((x, h1, es, attended, middle, u, w, gate, dense, mem, box))
        x = x3

    g = cotangent[0]
    packs = [None] * layers
    gain_rows = [None] * (2 * layers)
    table_grads = None
    table_list = [None] * layers
    output = dvs_above = None
    for l in reversed(range(layers)):
        x, h1, es, attended, middle, u, w, gate, dense, mem, box = kept[l]
        top = l == layers - 1
        line = jnp.concatenate(spread(gn, "tp"), axis=0)
        planes = spread(line, "ctx")
        if not top and shards == 2:
            table_grads = table_grad_call(*dvs_above, l + 1, layers, table_grads)
            planes[3], table_grads = after([planes[3], table_grads])
        *dvs, gw = write_call(idx, planes, names, l, dense, values, plan, tokens)
        if shards == 2:
            dvs_above = [dvs[0], swap(dvs[1], "fsdp", 1)]
        else:
            table_list[l] = lax.psum_scatter(dvs[0], "fsdp", scatter_dimension=0, tiled=True).astype(f32)
        gw = lax.all_to_all(gw, ("ctx", "tp"), 0, 0, tiled=True)
        back_shape = shape((chunk, 10 * HD), bf16)
        g_mid, go_chunk, gain_rows[layers + l], *back = kernel_call(
            functools.partial(lookup_back_kernel, plan=plan, row=layers + l, layer=l, shards=shards),
            "lookup_back",
            [chunk_shape, part_shape, gain_shape] + [back_shape] * 4,
            idx,
            [gw, table, w, w_a[l], u, back_box, w_b[l], middle, g, gains],
            [
                pltpu.VMEM(w.shape, f32),
                pltpu.VMEM(u.shape, bf16),
                pltpu.VMEM((4, NSUB // 4, 8 * HD), bf16),
                pltpu.VMEM((chunk, d_model), f32),
            ],
        )
        go_chunks = spread(go_chunk, TA)
        if l == 0 and shards == 2:
            table_grads = table_grad_call(*dvs_above, l, layers, table_grads)
            go_chunks[3], table_grads = after([go_chunks[3], table_grads])
        go, *ups = kernel_call(
            functools.partial(out_back_kernel, plan=plan),
            "attend_out_back",
            [full_shape] + [folded] * 4,
            idx,
            [*go_chunks, *w_o[l]],
            [pltpu.VMEM((4, tokens // 2, 2 * HD), bf16)],
        )
        ups = swaps(ups, SA)
        back = swaps(back, TA)
        ups[3], *back = after([ups[3], *back])
        shard_size = d_model // shards
        head_grads = kernel_call(
            functools.partial(attend_back_kernel, plan=plan),
            "attend_back",
            [heads_shape] * 4,
            idx,
            [*es, *ups, ids_row, ids_col],
            kv_scratch + [pltpu.VMEM((4 * tokens, HD), f32)] * 2,
        )
        head_grads = swaps(head_grads, SA)
        if top:
            forward_all = lax.all_gather(after([box], line)[0], TA, axis=0, tiled=False)
            below_all = lax.all_gather(after([kept[l - 1][10]], line)[0], TA, axis=0, tiled=False)
        else:
            forward_all = below_all
        back_all = lax.all_gather(after([back_box], line)[0], TA, axis=0, tiled=False)
        if top:
            output = back_all[:, :, d_model:].reshape(tokens, d_model)
        g_qkv, *parts = kernel_call(
            functools.partial(qkv_back_kernel, plan=plan),
            "qkv_back",
            [shape((tokens, 3 * width), bf16)] + [part_shape] * 4,
            idx,
            [*head_grads, *w_qkv[l]],
            [pack_scratch, part_scratch],
        )
        parts = swaps(parts, TA)
        qkv_rows = 3 * shard_size
        weight_rows = shard_size * 7 // 2 + NSUB // shards // 2
        weight_scratch = [
            pltpu.VMEM((shards, weight_rows, 256), bf16),
            pltpu.VMEM((tokens, d_model), bf16),
            pltpu.VMEM((tokens, width), bf16),
            pltpu.VMEM((tokens, width), bf16),
            pltpu.VMEM((tokens, 2 * HD), bf16),
            pltpu.VMEM((tokens, d_model), bf16),
        ]
        qkv_scratch = [pltpu.VMEM((shards, qkv_rows, 256), bf16)]
        split = l == 0 and shards == 2
        weight_outs = [shape((weight_rows, 256), bf16)] * 2 if split else [shape((shards, weight_rows, 256), bf16)]
        qkv_outs = [shape((qkv_rows, 256), bf16)] * 2 if split else [shape((shards, qkv_rows, 256), bf16)]
        qkv_packs = kernel_call(
            qkv_grad_kernel, "qkv_grad", qkv_outs, idx, [h1, g_qkv], qkv_scratch
        )
        weight_packs = kernel_call(
            functools.partial(weight_grad_kernel, plan=plan, has_full=top),
            "weight_grad",
            weight_outs,
            idx,
            [forward_all, back_all, *back, attended, go] + ([cotangent[0]] if top else []),
            weight_scratch,
        )
        if split:
            quarter = shape((qkv_rows // 4, 256), bf16)
            qkv_quarters = kernel_call(
                add_two_kernel, "qkv_add", [quarter] * 4, idx, [qkv_packs[0], swap(qkv_packs[1], "fsdp", 1)]
            )
            (pack,) = kernel_call(
                add_pair_kernel,
                "weight_add",
                [shape((weight_rows, 256), bf16)],
                idx,
                [weight_packs[0], swap(weight_packs[1], "fsdp", 1)],
            )
            packs[l] = [lax.psum(pack, "ctx")]
        else:
            parts[3], weight_packs[0], qkv_packs[0], below_all = after(
                [parts[3], weight_packs[0], qkv_packs[0], below_all]
            )
            packs[l] = reduce_packs([weight_packs[0], qkv_packs[0]])
        if l > 0:
            below = kept[l - 1]
            g, gain_rows[l], gn, back_box = kernel_call(
                functools.partial(norm_back_kernel, plan=plan, row=l, shards=shards),
                "norm_back",
                [chunk_shape, gain_shape, part_shape, box_shape],
                idx,
                [*parts, x, g_mid, gains, w_b[l - 1], below[7], below[9]],
                [chunk_scratch],
            )
        else:
            (g,) = kernel_call(
                functools.partial(norm_back_last_kernel, plan=plan, row=l),
                "norm_back_last",
                [shape((chunk + 16, d_model), bf16)],
                idx,
                [*parts, x, g_mid, gains, *gain_rows[1:]],
                [pltpu.VMEM((1, d_model), f32)],
            )
    g_chunks = spread(g, TA)
    input_gradient, gain_all, *gain_halves = kernel_call(
        functools.partial(input_grad_kernel, plan=plan),
        "input_gradient",
        [
            shape((tokens, d_model), f32),
            shape((16, d_model), f32),
            shape((16, 256), bf16),
            shape((16, 256), bf16),
        ],
        idx,
        g_chunks,
    )
    if shards != 2:
        table_grads = jnp.stack(table_list)
    gain_shapes = []
    if shards == 2:
        rows = qkv_rows // 4
        (part,) = kernel_call(
            plane_sum_kernel,
            "plane_sum",
            [shape((rows + 16, 256), bf16)],
            idx,
            [*swaps(qkv_quarters, "ctx"), gain_halves[0], swap(gain_halves[1], "fsdp", 1)],
        )
        late = spread(part, "ctx")
        gain_shapes = [shape((layers, d_model // 2), f32)] * 2
        flat = [packs[l][0] for l in range(layers)] + [packs[l][1] for l in range(1, layers)] + late
    else:
        gain_all = lax.psum(
            lax.psum_scatter(gain_all[: 2 * layers], "fsdp", scatter_dimension=1, tiled=True), "ctx"
        )
        flat = [packs[l][n] for n in range(2) for l in range(layers)]
    shard_size = d_model // shards
    tall = shape((layers, shard_size, width), f32)
    wide = shape((layers, width, shard_size), f32)
    sub = shape((layers, 1, HD, NSUB // shards), f32)
    grads = kernel_call(
        functools.partial(finalize_kernel, layers=layers, late=shards == 2),
        "finalize",
        [tall, tall, tall, wide, shape((layers, shard_size, 2 * HD), f32), tall, wide, sub, sub]
        + gain_shapes,
        idx,
        flat,
        [pltpu.VMEM((qkv_rows, 256), bf16)] if shards == 2 else [],
    )
    gain_grads = grads[9:] if shards == 2 else [gain_all[:layers], gain_all[layers:]]
    return (
        output[None],
        input_gradient[None],
        *grads[:7],
        *[jnp.swapaxes(t, 2, 3) for t in grads[7:9]],
        *gain_grads,
        table_grads,
    )


def solution(mesh):
    placed = (
        P("fsdp", "ctx", None),
        P(None, "fsdp", "tp"),
        P(None, "fsdp", "tp"),
        P(None, "fsdp", "tp"),
        P(None, "tp", "fsdp"),
        P(None, "fsdp", "tp"),
        P(None, "fsdp", "tp"),
        P(None, "tp", "fsdp"),
        P(None, "tp", "fsdp", None),
        P(None, "tp", "fsdp", None),
        P(None, "fsdp"),
        P(None, "fsdp"),
        P(None, ("fsdp", "ctx", "tp"), None),
        P("fsdp", None),
        P(None, "fsdp", "tp", "ctx", None),
        P(None, "fsdp", "tp", "ctx", None, None),
        P("fsdp", "ctx", None),
    )
    return jax.shard_map(
        body,
        mesh=mesh,
        in_specs=placed,
        out_specs=(
            P("fsdp", "ctx", None),
            P("fsdp", "ctx", None),
            P(None, "fsdp", "tp"),
            P(None, "fsdp", "tp"),
            P(None, "fsdp", "tp"),
            P(None, "tp", "fsdp"),
            P(None, "fsdp", "tp"),
            P(None, "fsdp", "tp"),
            P(None, "tp", "fsdp"),
            P(None, "tp", "fsdp", None),
            P(None, "tp", "fsdp", None),
            P(None, "fsdp"),
            P(None, "fsdp"),
            P(None, ("fsdp", "ctx", "tp"), None),
        ),
        check_vma=False,
    )
```

```python
import functools

import jax
import jax.numpy as jnp
from jax import lax
from jax.experimental import pallas as pl
from jax.experimental.pallas import tpu as pltpu
from jax.sharding import PartitionSpec as P

HD = 64
NSUB = 256
CAP = 8
EPS = 1e-05
NEG = -1e30
f32 = jnp.float32
bf16 = jnp.bfloat16
MIB = 1 << 20


def dot(a, b):
    return jnp.dot(a, b, preferred_element_type=f32)


def dot_nt(a, b):
    return lax.dot_general(a, b, (((1,), (1,)), ((), ())), preferred_element_type=f32)


def dot_tn(a, b):
    return lax.dot_general(a, b, (((0,), (0,)), ((), ())), preferred_element_type=f32)


def swap(x, axis, step):
    size = lax.axis_size(axis)
    return lax.ppermute(x, axis, [(i, i ^ step) for i in range(size)])


def swaps(xs, axis):
    return [xs[0]] + [swap(xs[d], axis, d) for d in range(1, len(xs))]


def spread(x, axis):
    return [x] + [swap(x, axis, d) for d in range(1, lax.axis_size(axis))]


def shape(dims, dtype):
    return jax.ShapeDtypeStruct(dims, dtype)


def kernel_call(body, name, outs, idx, args, scratch=(), limit=50, flops=0):
    in_specs = [pl.BlockSpec(memory_space=pltpu.SMEM)]
    in_specs += [pl.BlockSpec(memory_space=pltpu.VMEM) for _ in args]
    moved = sum(a.size * a.dtype.itemsize for a in args)
    moved += sum(o.size * o.dtype.itemsize for o in outs)
    out = pl.pallas_call(
        body,
        out_shape=outs,
        in_specs=in_specs,
        out_specs=[pl.BlockSpec(memory_space=pltpu.VMEM) for _ in outs],
        scratch_shapes=list(scratch),
        compiler_params=pltpu.CompilerParams(vmem_limit_bytes=limit * MIB),
        cost_estimate=pl.CostEstimate(flops=flops, bytes_accessed=moved, transcendentals=0),
        name=name,
    )(idx, *args)
    return list(out)


def rows_at(index, count):
    return pl.ds(pl.multiple_of(index * count, count), count)


def rms(x, gain):
    factor = lax.rsqrt(jnp.mean(x * x, axis=1, keepdims=True) + EPS)
    return factor, x * factor * gain


def rms_back(x, factor, gain, upstream):
    scaled = upstream * gain
    return factor * scaled - x * factor**3 * jnp.mean(scaled * x, axis=1, keepdims=True)


def total4(refs):
    return (refs[0][...].astype(f32) + refs[1][...].astype(f32)) + (
        refs[2][...].astype(f32) + refs[3][...].astype(f32)
    )


def fold(x):
    half = x.shape[0] // 2
    return jnp.concatenate([x[:half], x[half:]], axis=1)


def unfold(x):
    half = x.shape[1] // 2
    return jnp.concatenate([x[:, :half], x[:, half:]], axis=0)


class Plan:
    def __init__(self, SA, TA):
        self.SA, self.TA = SA, TA
        self.si = 1 if SA == "ctx" else 2
        self.ti = 1 if TA == "ctx" else 2

    def src(self, sa, ta):
        return sa * 4 + ta if self.SA == "ctx" else ta * 4 + sa

    def rel(self, ds, dt):
        return (ds, dt) if self.SA == "ctx" else (dt, ds)


PLAN = Plan("ctx", "tp")


def slots_kernel(idx, first_ref, second_ref, out_ref, t0, t1, t2, t3, table, plan, gbits, dbits):
    layers, picks, tokens = first_ref.shape
    inner = second_ref.shape[1]
    owners, _, width = out_ref.shape
    lanes = owners * width
    chunk = tokens // 4
    iota = lax.broadcasted_iota(jnp.int32, (NSUB, tokens), 0)
    before = lax.broadcasted_iota(jnp.int32, (tokens, tokens), 0) < lax.broadcasted_iota(
        jnp.int32, (tokens, tokens), 1
    )
    before = jnp.where(before, 1.0, 0.0).astype(bf16)
    row = lax.broadcasted_iota(jnp.int32, (lanes, tokens), 0)
    token_row = (lax.broadcasted_iota(jnp.int32, (8, tokens), 1) + 1).astype(f32)
    token_row = jnp.where(
        lax.broadcasted_iota(jnp.int32, (8, tokens), 0) == 0, token_row, 0.0
    )
    for l in range(layers):
        onehot = jnp.zeros((NSUB, tokens), f32)
        for i in range(picks):
            onehot = jnp.where(iota == first_ref[l, i : i + 1, :], 1.0, onehot)
        counts = dot(onehot.astype(bf16), before)
        total = jnp.zeros((16, lanes), f32)
        slots = []
        for i in range(picks):
            first = first_ref[l, i : i + 1, :]
            rank = jnp.sum(jnp.where(iota == first, counts, 0.0), axis=0, keepdims=True)
            shard = lax.shift_right_logical(first, gbits)
            group = lax.shift_right_logical(shard, dbits) * (1 << gbits) + (first & ((1 << gbits) - 1))
            slot = (shard & ((1 << dbits) - 1)) * width + group * CAP + rank.astype(jnp.int32)
            slots.append(slot)
            names = jnp.concatenate(
                [second_ref[l, 8 * i : 8 * i + 8, :].astype(f32), token_row], axis=0
            )
            hit = jnp.where(row == slot, 1.0, 0.0).astype(bf16)
            total = total + dot_nt(names.astype(bf16), hit)
        for d in range(owners):
            out_ref[d, 16 * l : 16 * l + 16, :] = total[:, d * width : (d + 1) * width].astype(bf16)
        both = jnp.concatenate([first_ref[l], jnp.concatenate(slots, axis=0)], axis=0)
        for n in range(4):
            cut = slice(n * chunk, (n + 1) * chunk)
            at = l * (8 + inner)
            table[n, at : at + 8, :] = both[:, cut]
            table[n, at + 8 : at + 8 + inner, :] = second_ref[l, :, cut]
    for d, out in enumerate((t0, t1, t2, t3)):
        out[...] = table[idx[plan.ti] ^ d]


def pick_table_kernel(idx, t0, t1, t2, t3, out_ref, table, plan):
    for d, t in enumerate((t0, t1, t2, t3)):
        table[idx[plan.ti] ^ d] = t[...]
    rows = out_ref.shape[1]
    for l in range(out_ref.shape[0]):
        out_ref[l] = jnp.concatenate([table[n, rows * l : rows * (l + 1), :] for n in range(4)], axis=1)


def head_mask(shape_, lanes_each):
    return lax.broadcasted_iota(jnp.int32, shape_, 1) // lanes_each


def place_chunks(refs, full, t):
    count = refs[0].shape[0]
    for d in range(4):
        full[rows_at(t ^ d, count), :] = refs[d][...]


def emit_chunks(part, outs, t):
    count = outs[0].shape[0]
    for d in range(4):
        outs[d][...] = part[rows_at(t ^ d, count), :]


def piece_at(f, j, pieces, size):
    return rows_at(f ^ j, size) if len(pieces) > 1 else slice(0, size)


def emit_heads(h_ref, pieces, pack, outs, idx, plan):
    width = pieces[0].shape[1] // 3
    size = pieces[0].shape[0]
    qkv = sum(
        dot(h_ref[:, piece_at(idx[0], j, pieces, size)], w[...]) for j, w in enumerate(pieces)
    ).astype(bf16)
    for j in range(4):
        q = qkv[:, HD * j : HD * (j + 1)]
        k = qkv[:, width + HD * j : width + HD * (j + 1)]
        v = qkv[:, 2 * width + HD * j : 2 * width + HD * (j + 1)]
        pack[j] = jnp.concatenate([jnp.concatenate([q, k], axis=1), fold(v)], axis=0)
    for d in range(4):
        outs[d][...] = pack[idx[plan.si] ^ d]


def qkv_first_kernel(idx, x_ref, gain_ref, *refs, plan, row):
    *pieces, h_ref, e0, e1, e2, e3, pack = refs
    _, normed = rms(x_ref[...].astype(f32), gain_ref[row : row + 1, :])
    h_ref[...] = normed.astype(bf16)
    emit_heads(h_ref, pieces, pack, (e0, e1, e2, e3), idx, plan)


def qkv_kernel(idx, h0, h1, h2, h3, *refs, plan):
    *pieces, h_ref, e0, e1, e2, e3, pack = refs
    place_chunks((h0, h1, h2, h3), h_ref, idx[plan.ti])
    emit_heads(h_ref, pieces, pack, (e0, e1, e2, e3), idx, plan)


def load_heads(es, kk, vv):
    for d in range(4):
        rows = es[d].shape[0] * 2 // 3
        kk[rows * d : rows * (d + 1), :] = es[d][0:rows, HD : 2 * HD]
        vv[rows * d : rows * (d + 1), :] = unfold(es[d][rows:, :])


def load_ids(col_ref, ids_col, s):
    count = col_ref.shape[0] // 4
    for d in range(4):
        ids_col[count * d : count * (d + 1), :] = col_ref[rows_at(s ^ d, count), :]


def probabilities(kk, q, key_ids, query_ids):
    scores = dot_nt(kk, q) * (HD ** (-0.5))
    scores = jnp.where(key_ids <= query_ids, scores, NEG)
    top = jnp.max(scores, axis=0, keepdims=True)
    exponent = jnp.exp(scores - top)
    return exponent * (1.0 / jnp.sum(exponent, axis=0, keepdims=True))


def attend_kernel(idx, e0, e1, e2, e3, row_ref, col_ref, a0, a1, a2, a3, kk, vv, ids_col, plan):
    es, outs = (e0, e1, e2, e3), (a0, a1, a2, a3)
    s = idx[plan.si]
    load_heads(es, kk, vv)
    load_ids(col_ref, ids_col, s)
    count = kk.shape[0] // 4
    for d in range(4):
        query_ids = row_ref[:, rows_at(s ^ d, count)]
        p = probabilities(kk[...], es[d][0:count, 0:HD], ids_col[...], query_ids)
        blended = dot_tn(vv[...], p.astype(bf16))
        outs[d][...] = fold(blended.T.astype(bf16))


def attend_back_kernel(
    idx, e0, e1, e2, e3, u0, u1, u2, u3, row_ref, col_ref, g0, g1, g2, g3, kk, vv, ids_col, gk, gv, plan
):
    es, us, outs = (e0, e1, e2, e3), (u0, u1, u2, u3), (g0, g1, g2, g3)
    s = idx[plan.si]
    load_heads(es, kk, vv)
    load_ids(col_ref, ids_col, s)
    count = kk.shape[0] // 4
    scale = HD ** (-0.5)
    for d in range(4):
        query_ids = row_ref[:, rows_at(s ^ d, count)]
        q = es[d][0:count, 0:HD]
        up = unfold(us[d][...])
        p = probabilities(kk[...], q, ids_col[...], query_ids)
        gp = dot_nt(vv[...], up)
        centre = jnp.sum(p * gp, axis=0, keepdims=True)
        gs = (p * (gp - centre)).astype(bf16)
        gq = (dot_tn(kk[...], gs) * scale).T.astype(bf16)
        outs[d][0:count, 0:HD] = gq
        key_term = dot(gs, q)
        value_term = dot(p.astype(bf16), up)
        if d == 0:
            gk[...] = key_term
            gv[...] = value_term
        else:
            gk[...] += key_term
            gv[...] += value_term
    for d in range(4):
        outs[d][0:count, HD : 2 * HD] = (gk[count * d : count * (d + 1), :] * scale).astype(bf16)
        outs[d][count:, :] = fold(gv[count * d : count * (d + 1), :].astype(bf16))


def out_kernel(idx, a0, a1, a2, a3, *refs, plan):
    *pieces, a_ref, p0, p1, p2, p3, heads, part = refs
    for d, a in enumerate((a0, a1, a2, a3)):
        heads[idx[plan.si] ^ d] = unfold(a[...])
    a_ref[...] = jnp.concatenate([heads[j] for j in range(4)], axis=1)
    size = pieces[0].shape[1]
    for j, w in enumerate(pieces):
        part[:, piece_at(idx[0], j, pieces, size)] = dot(a_ref[...], w[...]).astype(bf16)
    emit_chunks(part, (p0, p1, p2, p3), idx[plan.ti])


def out_back_kernel(idx, g0, g1, g2, g3, *refs, plan):
    *pieces, go_ref, u0, u1, u2, u3, pack = refs
    place_chunks((g0, g1, g2, g3), go_ref, idx[plan.ti])
    size = pieces[0].shape[1]
    up = sum(
        dot_nt(go_ref[:, piece_at(idx[0], j, pieces, size)], w[...]) for j, w in enumerate(pieces)
    ).astype(bf16)
    for j in range(4):
        pack[j] = fold(up[:, HD * j : HD * (j + 1)])
    for d, u in enumerate((u0, u1, u2, u3)):
        u[...] = pack[idx[plan.si] ^ d]


def qkv_back_kernel(idx, g0, g1, g2, g3, *refs, plan, row=None, gain_rows=0):
    *ins, g_ref, p0, p1, p2, p3, pack, part = refs
    x_ref, *rows_refs = ins[len(ins) - gain_rows :] if gain_rows else [None]
    pieces = ins[: len(ins) - gain_rows]
    for d, g in enumerate((g0, g1, g2, g3)):
        pack[idx[plan.si] ^ d] = g[...]
    rows = g_ref.shape[0]
    columns = [pack[j, 0:rows, 0:HD] for j in range(4)]
    columns += [pack[j, 0:rows, HD : 2 * HD] for j in range(4)]
    columns += [unfold(pack[j, rows:, :]) for j in range(4)]
    g_ref[...] = jnp.concatenate(columns, axis=1)
    size = pieces[0].shape[0]
    if not gain_rows:
        for j, w in enumerate(pieces):
            part[:, piece_at(idx[0], j, pieces, size)] = dot_nt(g_ref[...], w[...]).astype(bf16)
        emit_chunks(part, (p0, p1, p2, p3), idx[plan.ti])
        return
    x = x_ref[...].astype(f32)
    factor = lax.rsqrt(jnp.mean(x * x, axis=1, keepdims=True) + EPS)
    count = part.shape[0] // 4
    for j, w in enumerate(pieces):
        at = piece_at(idx[0], j, pieces, size)
        term = dot_nt(g_ref[...], w[...])
        part[:, at] = term.astype(bf16)
        change = jnp.sum(term * (x_ref[:, at].astype(f32) * factor), axis=0, keepdims=True)
        p0[count : count + 1, at] = change.astype(bf16)
    blank = jnp.zeros((p0.shape[0] - count - gain_rows, p0.shape[1]), f32)
    tail = [p0[count : count + 1, :].astype(f32)] + [r[...] for r in rows_refs] + [blank]
    tail = jnp.concatenate(tail, axis=0).astype(bf16)
    for d, out in enumerate((p0, p1, p2, p3)):
        out[0:count, :] = part[rows_at(idx[plan.ti] ^ d, count), :]
        out[count:, :] = tail


def to_pack(x):
    rows, width = x.shape
    if width >= 256:
        return jnp.concatenate([x[:, 256 * i : 256 * (i + 1)] for i in range(width // 256)], axis=0)
    fold_by = 256 // width
    rows = rows // fold_by
    return jnp.concatenate([x[rows * i : rows * (i + 1)] for i in range(fold_by)], axis=1)


def from_pack(p, rows, width):
    if width >= 256:
        return jnp.concatenate([p[rows * i : rows * (i + 1)] for i in range(width // 256)], axis=1)
    return jnp.concatenate([p[:, width * i : width * (i + 1)] for i in range(256 // width)], axis=0)


def shard_rows(x, f, shards):
    size = x.shape[0] // shards
    return x[size * f : size * (f + 1)]


def shard_columns(x, f, shards):
    size = x.shape[1] // shards
    return x[:, size * f : size * (f + 1)]


def emit_shards(pack, outs, idx):
    if len(outs) == 1:
        outs[0][...] = pack[...]
    else:
        outs[0][...] = pack[idx[0]]
        outs[1][...] = pack[idx[0] ^ 1]


def qkv_grad_kernel(idx, h_ref, g_ref, *refs):
    *outs, pack = refs
    shards = pack.shape[0]
    change = dot_tn(h_ref[...], g_ref[...])
    for f in range(shards):
        pack[f] = to_pack(shard_rows(change, f, shards)).astype(bf16)
    emit_shards(pack, outs, idx)


def weight_grad_kernel(idx, *refs, plan, has_full):
    forward, back, near, (a_ref, go_ref) = refs[0], refs[1], refs[2:6], refs[6:8]
    full = refs[8] if has_full else None
    *outs, pack, h, z, gg, gu, gy = refs[8 + has_full :]
    chunk = forward.shape[1]
    d_model = h.shape[1]
    quarter = z.shape[1]
    shards = pack.shape[0]
    tables = jnp.zeros((NSUB, 2 * HD), f32)
    mine = rows_at(idx[plan.ti], quarter)
    for d in range(4):
        at = slice(chunk * d, chunk * (d + 1))
        h[at, :] = forward[d, :, 0:d_model]
        z[at, :] = forward.at[:, :, d_model:][d, :, mine]
        gg[at, :] = back.at[:, :, 0:d_model][d, :, mine]
        gu[rows_at(idx[plan.ti] ^ d, chunk), :] = near[d][:, 0 : 2 * HD]
        folded = near[d][:, 2 * HD :].astype(f32)
        tables = tables + jnp.concatenate(
            [folded[:, 2 * HD * i : 2 * HD * (i + 1)] for i in range(4)], axis=0
        )
        gy[at, :] = full[at, :] if has_full else back[d, :, d_model:]
    gate_change = dot_tn(h[...], gg[...])
    look_change = dot_tn(h[...], gu[...])
    mem_change = dot_tn(z[...], gy[...])
    out_change = dot_tn(a_ref[...], go_ref[...])
    for f in range(shards):
        pack[f] = jnp.concatenate(
            [
                to_pack(shard_rows(gate_change, f, shards)),
                to_pack(shard_columns(mem_change, f, shards)),
                to_pack(shard_rows(look_change, f, shards)),
                to_pack(shard_rows(tables, f, shards)),
                to_pack(shard_columns(out_change, f, shards)),
            ],
            axis=0,
        ).astype(bf16)
    emit_shards(pack, outs, idx)


def finalize_kernel(idx, *refs, layers, late):
    count = 2 * layers + 2 * late
    ins, outs = refs[:count], refs[count:]
    q_ref, k_ref, v_ref, o_ref, look_ref, gate_ref, mem_ref, first_ref, second_ref = outs[:9]
    part = q_ref.shape[1]
    for l in range(layers):
        if l > 0 or not late:
            memory, qkv = ins[2 * l + 2 * late], ins[2 * l + 2 * late + 1]
        else:
            one_ref, two_ref, memory, qkv = outs[9:]
            rows, more = memory.shape[0] // 4, qkv.shape[0] // 4
            total = 0.0
            for d in range(4):
                memory[rows_at(idx[1] ^ d, rows), :] = ins[d][0:rows, :]
                qkv[rows_at(idx[1] ^ d, more), :] = ins[d][rows : rows + more, :]
                total = total + ins[d][rows + more :, :].astype(f32)
            total = jnp.concatenate([total[0:8], total[8:16]], axis=1)
            one_ref[...] = total[0:layers]
            two_ref[...] = total[layers : 2 * layers]
        for n, ref in enumerate((q_ref, k_ref, v_ref)):
            ref[l] = qkv[part * n : part * (n + 1), :].astype(f32)
        gate_ref[l] = memory[0:part, :].astype(f32)
        mem_ref[l] = from_pack(memory[part : 2 * part, :], mem_ref.shape[1], mem_ref.shape[2]).astype(f32)
        at = 2 * part + part // 2
        look_ref[l] = from_pack(memory[2 * part : at, :].astype(f32), part, look_ref.shape[2])
        rows = first_ref.shape[3]
        tables = from_pack(memory[at : at + rows // 2, :].astype(f32), rows, 2 * HD)
        first_ref[l, 0] = tables[:, :HD].T
        second_ref[l, 0] = tables[:, HD:].T
        at = at + rows // 2
        o_ref[l] = from_pack(memory[at : at + part, :], o_ref.shape[1], o_ref.shape[2]).astype(f32)


def add_two_kernel(idx, a, b, o0, o1, o2, o3):
    chunk = o0.shape[0]
    for d, out in enumerate((o0, o1, o2, o3)):
        at = rows_at(idx[1] ^ d, chunk)
        out[...] = (a[at, :].astype(f32) + b[at, :].astype(f32)).astype(bf16)


def plane_sum_kernel(idx, *refs):
    a, b, (g0, g1, out) = refs[0:4], refs[4:8], refs[8:]
    rows = a[0].shape[0]
    more = rows + b[0].shape[0]
    out[0:rows, :] = total4(a).astype(bf16)
    out[rows:more, :] = total4(b).astype(bf16)
    out[more:, :] = (g0[...].astype(f32) + g1[...].astype(f32)).astype(bf16)


def own_rows(ref, idx, plan, count):
    if ref.shape[0] == count:
        return ref[...].astype(f32)
    return ref[rows_at(idx[plan.ti], count), :].astype(f32)


def table_of(a_ref, m, shards):
    size = a_ref.shape[1] * 4 // 5
    both = [a_ref[f * 4 + m, size:, :] for f in range(shards)]
    both = both[0] if shards == 1 else jnp.concatenate(both, axis=0)
    return both[:, :HD], both[:, HD:]


def only_head(x, m, chunk):
    lane = lax.broadcasted_iota(jnp.int32, x.shape, 1)
    return jnp.where((lane >= m * chunk) & (lane < (m + 1) * chunk), x, 0.0)


def lookup_kernel(
    idx, x_ref, p0, r1, r2, r3, gain_ref, a_ref, pick_ref, *refs, plan, row, layer, shards
):
    *names_ref, x_out, h_ref, u_ref, w_ref, out_ref = refs
    chunk = p0.shape[0]
    x = own_rows(x_ref, idx, plan, chunk) + total4((p0, r1, r2, r3))
    x_out[...] = x
    _, normed = rms(x, gain_ref[row : row + 1, :])
    h_ref[...] = normed.astype(bf16)
    size = a_ref.shape[1] * 4 // 5
    c1, c2 = [], []
    for m in range(4):
        u = sum(
            dot(h_ref[:, size * f : size * (f + 1)], a_ref[f * 4 + m, 0:size, :]) for f in range(shards)
        ).astype(bf16)
        u_ref[:, 2 * HD * m : 2 * HD * (m + 1)] = u
        ka, kb = table_of(a_ref, m, shards)
        c1.append(dot_nt(ka, u[:, :HD]))
        c2.append(dot_nt(kb, u[:, HD:]))
    c1 = jnp.concatenate(c1, axis=1)
    c2 = jnp.concatenate(c2, axis=1)
    lanes = c1.shape[1]
    iota = lax.broadcasted_iota(jnp.int32, (NSUB, lanes), 0)
    for i in range(4):
        first = pick_ref[layer, i : i + 1, :]
        base = jnp.sum(jnp.where(iota == first, c1, 0.0), axis=0, keepdims=True)
        for b in range(8):
            r = i * 8 + b
            second = pick_ref[layer, 8 + r : 9 + r, :]
            picked = jnp.sum(jnp.where(iota == second, c2, 0.0), axis=0, keepdims=True)
            w_ref[r : r + 1, :] = base + picked
    logits = w_ref[...]
    exponent = jnp.exp(logits - jnp.max(logits, axis=0, keepdims=True))
    w = exponent * (1.0 / jnp.sum(exponent, axis=0, keepdims=True))
    w_ref[...] = w
    owners, _, width = out_ref.shape
    slots = lax.broadcasted_iota(jnp.int32, (owners * width, lanes), 0)
    total = jnp.zeros((32, owners * width), f32)
    for i in range(4):
        hit = jnp.where(slots == pick_ref[layer, 4 + i : 5 + i, :], 1.0, 0.0).astype(bf16)
        mine = w[8 * i : 8 * (i + 1), :]
        split = jnp.concatenate([only_head(mine, m, chunk) for m in range(4)], axis=0)
        total = total + dot_nt(split.astype(bf16), hit)
    for d in range(owners):
        out_ref[d, 0:32, :] = total[:, d * width : (d + 1) * width].astype(bf16)
        if names_ref:
            out_ref[d, 32:, :] = names_ref[0][d]


def gate_part(b_ref, n):
    return b_ref[n, 0 : b_ref.shape[1] // 2, :]


def memory_part(b_ref, n):
    size = b_ref.shape[1] // 2
    return from_pack(b_ref[n, size:, :], b_ref.shape[2], size)


def gate_values_kernel(idx, h_ref, b_ref, gate_ref, shards):
    size, quarter = b_ref.shape[1] // 2, b_ref.shape[2]
    for t in range(4):
        gate_ref[:, quarter * t : quarter * (t + 1)] = sum(
            dot(h_ref[:, size * f : size * (f + 1)], gate_part(b_ref, f * 4 + t)) for f in range(shards)
        )


def gate_sum(sums, gate_ref, b_ref, x_ref, mem_ref, z_ref, x_out, shards):
    mem = total4(sums)
    mem_ref[...] = mem
    gate = gate_ref[...]
    z_ref[...] = (mem * (gate * jax.nn.sigmoid(gate))).astype(bf16)
    size, quarter = b_ref.shape[1] // 2, b_ref.shape[2]
    for f in range(shards):
        at = slice(size * f, size * (f + 1))
        x_out[:, at] = x_ref[:, at] + sum(
            dot(z_ref[:, quarter * t : quarter * (t + 1)], memory_part(b_ref, f * 4 + t)) for t in range(4)
        )


def gate_kernel(
    idx, s0, s1, s2, s3, gate_ref, b_ref, x_ref, h_ref, gain_ref, mem_ref, box_ref, x_out, h_out, z, row, shards
):
    gate_sum((s0, s1, s2, s3), gate_ref, b_ref, x_ref, mem_ref, z, x_out, shards)
    h_out[...] = rms(x_out[...], gain_ref[row : row + 1, :])[1].astype(bf16)
    fill_box(box_ref, h_ref, z)


def fill_box(box_ref, left_ref, right_ref):
    width = left_ref.shape[1]
    box_ref[:, 0:width] = left_ref[...]
    box_ref[:, width:] = right_ref[...]


def gate_last_kernel(
    idx, s0, s1, s2, s3, gate_ref, b_ref, x_ref, h_ref, g_ref,
    n_ref, box_ref, back_ref, mem, z, x_out, gy, plan, shards,
):
    gate_sum((s0, s1, s2, s3), gate_ref, b_ref, x_ref, mem, z, x_out, shards)
    gy[...] = g_ref[rows_at(idx[plan.ti], gy.shape[0]), :]
    gate_back(gy, b_ref, gate_ref, mem, n_ref, back_ref, shards)
    back_ref[:, gy.shape[1] :] = x_out[...].astype(bf16)
    fill_box(box_ref, h_ref, z)


def gate_back(gy_ref, b_ref, gate_ref, mem_ref, gn_ref, gg_ref, shards):
    size, quarter = b_ref.shape[1] // 2, b_ref.shape[2]
    for t in range(4):
        at = slice(quarter * t, quarter * (t + 1))
        gz = sum(
            dot_nt(gy_ref[:, size * f : size * (f + 1)], memory_part(b_ref, f * 4 + t)) for f in range(shards)
        )
        gate = gate_ref[:, at]
        sigmoid = jax.nn.sigmoid(gate)
        gn_ref[:, at] = (gz * (gate * sigmoid)).astype(bf16)
        slope = sigmoid * (1.0 + gate * (1.0 - sigmoid))
        gg_ref[:, at] = (gz * mem_ref[:, at] * slope).astype(bf16)


def norm_back(idx, parts, x_ref, g_ref, gain_ref, dgain_ref, plan, row):
    count = parts[0].shape[0]
    upstream = total4(parts)
    x = own_rows(x_ref, idx, plan, count)
    gain = gain_ref[row : row + 1, :]
    factor, _ = rms(x, gain)
    dgain_ref[...] = jnp.sum(upstream * x * factor, axis=0, keepdims=True)
    return g_ref[...] + rms_back(x, factor, gain, upstream)


def norm_back_kernel(
    idx, p0, r1, r2, r3, x_ref, g_ref, gain_ref, b_ref, gate_ref, mem_ref,
    gx_ref, dgain_ref, gn_ref, back_ref, gy, plan, row, shards,
):
    gx = norm_back(idx, (p0, r1, r2, r3), x_ref, g_ref, gain_ref, dgain_ref, plan, row)
    gx_ref[...] = gx
    gy[...] = gx.astype(bf16)
    gate_back(gy, b_ref, gate_ref, mem_ref, gn_ref, back_ref, shards)
    back_ref[:, gy.shape[1] :] = gy[...]


def norm_back_last_kernel(
    idx, p0, r1, r2, r3, x_ref, g_ref, gain_ref, out_ref, all_ref, mine_ref, other_ref, plan, row
):
    count = out_ref.shape[0]
    refs = (p0, r1, r2, r3)
    upstream = total4([r.at[0:count] for r in refs])
    x = own_rows(x_ref, idx, plan, count)
    factor, _ = rms(x, gain_ref[row : row + 1, :])
    gx = g_ref[...] + rms_back(x, factor, gain_ref[row : row + 1, :], upstream)
    out_ref[...] = gx.astype(bf16)
    all_ref[...] = total4([r.at[count:] for r in refs])
    size = all_ref.shape[1] // 2
    for j, out in enumerate((mine_ref, other_ref)):
        half = all_ref[:, rows_at(idx[0] ^ j, size)]
        out[...] = jnp.concatenate([half[:8, 0:256], half[:8, 256:]], axis=0).astype(bf16)


def place_kernel(idx, c0, c1, c2, c3, out_ref, plan):
    chunk = c0.shape[0]
    for d, c in enumerate((c0, c1, c2, c3)):
        out_ref[rows_at(idx[plan.ti] ^ d, chunk), :] = c[...].astype(out_ref.dtype)


def lookup_back_kernel(
    idx, gw_ref, pick_ref, w_ref, a_ref, u_ref, gg_ref, b_ref, x_ref, g_ref, gain_ref,
    gx_ref, go_ref, dgain_ref, b0, b1, b2, b3, gl, gu_all, tables, gh, plan, row, layer, shards,
):
    chunk = u_ref.shape[0]
    owners, _, width = gw_ref.shape
    lanes = w_ref.shape[1]
    slots = lax.broadcasted_iota(jnp.int32, (owners * width, lanes), 0)
    arrived = jnp.concatenate([gw_ref[d] for d in range(owners)], axis=1)
    for i in range(4):
        hit = jnp.where(slots == pick_ref[layer, 4 + i : 5 + i, :], 1.0, 0.0).astype(bf16)
        mixed = dot(arrived, hit)
        gl[8 * i : 8 * (i + 1), :] = sum(
            only_head(mixed[8 * m : 8 * (m + 1), :], m, chunk) for m in range(4)
        )
    w = w_ref[...]
    gw = gl[...]
    gl[...] = w * (gw - jnp.sum(w * gw, axis=0, keepdims=True))
    iota = lax.broadcasted_iota(jnp.int32, (NSUB, lanes), 0)
    gc1 = jnp.zeros((NSUB, lanes), f32)
    gc2 = jnp.zeros((NSUB, lanes), f32)
    for i in range(4):
        both = jnp.sum(gl[8 * i : 8 * (i + 1), :], axis=0, keepdims=True)
        gc1 = jnp.where(iota == pick_ref[layer, i : i + 1, :], both, gc1)
        for b in range(8):
            r = i * 8 + b
            gc2 = gc2 + jnp.where(iota == pick_ref[layer, 8 + r : 9 + r, :], gl[r : r + 1, :], 0.0)
    gc1 = gc1.astype(bf16)
    gc2 = gc2.astype(bf16)
    for m in range(4):
        ka, kb = table_of(a_ref, m, shards)
        one = gc1[:, chunk * m : chunk * (m + 1)]
        two = gc2[:, chunk * m : chunk * (m + 1)]
        gu_all[:, 2 * HD * m : 2 * HD * (m + 1)] = jnp.concatenate(
            [dot_tn(one, ka), dot_tn(two, kb)], axis=1
        ).astype(bf16)
        change = jnp.concatenate(
            [
                dot(one, u_ref[:, 2 * HD * m : 2 * HD * m + HD]),
                dot(two, u_ref[:, 2 * HD * m + HD : 2 * HD * (m + 1)]),
            ],
            axis=1,
        ).astype(bf16)
        tables[m] = jnp.concatenate(
            [change[NSUB // 4 * n : NSUB // 4 * (n + 1), :] for n in range(4)], axis=1
        )
    size, quarter = b_ref.shape[1] // 2, b_ref.shape[2]
    for f in range(shards):
        gh[:, size * f : size * (f + 1)] = sum(
            dot_nt(gg_ref[:, quarter * t : quarter * (t + 1)], gate_part(b_ref, f * 4 + t))
            + dot_nt(gu_all[:, 2 * HD * t : 2 * HD * (t + 1)], a_ref[f * 4 + t, 0:size, :])
            for t in range(4)
        )
    upstream = gh[...]
    x = x_ref[...]
    gain = gain_ref[row : row + 1, :]
    factor, _ = rms(x, gain)
    dgain_ref[...] = jnp.sum(upstream * x * factor, axis=0, keepdims=True)
    gx = own_rows(g_ref, idx, plan, chunk) + rms_back(x, factor, gain, upstream)
    gx_ref[...] = gx
    go_ref[...] = gx.astype(bf16)
    for d, out in enumerate((b0, b1, b2, b3)):
        n = idx[plan.ti] ^ d
        out[:, 0 : 2 * HD] = gu_all[:, rows_at(n, 2 * HD)]
        out[:, 2 * HD : 10 * HD] = tables[n]


STEP_GROUPS = 4


def step_base(idx, step, pieces, per_piece):
    if pieces == 1:
        return step * STEP_GROUPS
    piece = step // per_piece
    return ((idx[0] ^ piece) * per_piece + step % per_piece) * STEP_GROUPS


def read_kernel(idx, w_ref, names_ref, *refs, plan, pieces, per_piece):
    vs = refs[:pieces]
    o0, o1, o2, o3, s_ref, partial, rows = refs[pieces:]
    step = pl.program_id(0)
    sources, _, width = w_ref.shape

    @pl.when(step == 0)
    def _():
        iota = lax.broadcasted_iota(jnp.int32, (NSUB, width), 0).astype(f32)

        def build(sa, carry):
            weights = sum(w_ref[plan.src(sa, ta)].astype(f32) for ta in range(4))
            for m in range(4):
                src = plan.src(sa, m)
                names = names_ref[src].astype(f32)
                dense = jnp.zeros((NSUB, width), f32)
                for b in range(8):
                    r = 8 * m + b
                    dense = jnp.where(iota == names[b : b + 1, :], weights[r : r + 1, :], dense)
                s_ref[src] = dense.T
            return carry

        lax.fori_loop(0, 4, build, 0)

    base = step_base(idx, step, pieces, per_piece)

    def multiply(v_ref):
        for k in range(STEP_GROUPS):
            at = rows_at(base + k, CAP)
            left = s_ref[:, at, :].reshape(sources * CAP, NSUB).astype(bf16)
            got = dot(left, v_ref[NSUB * k : NSUB * (k + 1), :])
            partial[:, at, :] = got.reshape(sources, CAP, v_ref.shape[1])

    for n in range(pieces):
        pl.when(step // per_piece == n)(functools.partial(multiply, vs[n]))

    @pl.when(step == pl.num_programs(0) - 1)
    def _():
        s, t = idx[plan.si], idx[plan.ti]
        tokens = rows.shape[0]
        chunk = tokens // 4
        outs = (o0, o1, o2, o3)
        iota = (lax.broadcasted_iota(jnp.int32, (tokens, width), 0) + 1).astype(f32)
        for ds in range(4):
            hits, parts = [], []
            for m in range(4):
                src = plan.src(s ^ ds, m)
                token = names_ref[src].astype(f32)[8:9, :]
                hits.append(jnp.where(iota == token, 1.0, 0.0).astype(bf16))
                parts.append(partial[src].astype(bf16))
            rows[...] = dot(
                jnp.concatenate(hits, axis=1), jnp.concatenate(parts, axis=0)
            ).astype(bf16)
            for dt in range(4):
                dp, dz = plan.rel(ds, dt)
                outs[dp][chunk * dz : chunk * (dz + 1), :] = rows[rows_at(t ^ dt, chunk), :]


def value_specs(values, layer):
    d_model = values[0].shape[2]
    per_piece = values[0].shape[1] // (STEP_GROUPS * NSUB)
    specs = []
    for n in range(len(values)):
        def index(g, n=n):
            return (layer, jnp.clip(g - n * per_piece, 0, per_piece - 1), 0)

        specs.append(pl.BlockSpec((None, STEP_GROUPS * NSUB, d_model), index))
    return specs, per_piece


def read_call(idx, weights, names, layer, values, plan, tokens):
    sources, _, width = weights.shape
    specs, per_piece = value_specs(values, layer)
    d_model = values[0].shape[2]
    out = shape((tokens, d_model), bf16)
    return pl.pallas_call(
        functools.partial(read_kernel, plan=plan, pieces=len(values), per_piece=per_piece),
        grid=(per_piece * len(values),),
        out_shape=[out, out, out, out, shape((sources, width, NSUB), f32)],
        in_specs=[
            pl.BlockSpec(memory_space=pltpu.SMEM),
            pl.BlockSpec((sources, 32, width), lambda g: (0, 0, 0)),
            pl.BlockSpec((sources, 16, width), lambda g: (0, 2 + layer, 0)),
        ]
        + specs,
        out_specs=[pl.BlockSpec((tokens, d_model), lambda g: (0, 0)) for _ in range(4)]
        + [pl.BlockSpec((sources, width, NSUB), lambda g: (0, 0, 0))],
        scratch_shapes=[
            pltpu.VMEM((sources, width, d_model), f32),
            pltpu.VMEM((tokens, d_model), bf16),
        ],
        compiler_params=pltpu.CompilerParams(vmem_limit_bytes=50 * MIB),
        cost_estimate=pl.CostEstimate(
            flops=4 * sources * width * NSUB * d_model, bytes_accessed=20 * MIB, transcendentals=0
        ),
        name="memory_read",
    )(idx, weights, names, *values)


def write_kernel(idx, g0, g1, g2, g3, names_ref, s_ref, *refs, plan, pieces, per_piece):
    vs, dvs = refs[:pieces], refs[pieces : 2 * pieces]
    gw_ref, grads, partial, cross = refs[2 * pieces :]
    step = pl.program_id(0)
    sources, width, _ = s_ref.shape
    d_model = vs[0].shape[1]

    @pl.when(step == 0)
    def _():
        s, t = idx[plan.si], idx[plan.ti]
        tokens = grads.shape[1]
        chunk = tokens // 4
        for dp, g in enumerate((g0, g1, g2, g3)):
            for dz in range(4):
                ds, dt = plan.rel(dp, dz)
                grads[s ^ ds, rows_at(t ^ dt, chunk), :] = g[chunk * dz : chunk * (dz + 1), :]
        iota = (lax.broadcasted_iota(jnp.int32, (tokens, width), 0) + 1).astype(f32)
        for sa in range(4):
            hits = []
            for m in range(4):
                token = names_ref[plan.src(sa, m)].astype(f32)[8:9, :]
                hits.append(jnp.where(iota == token, 1.0, 0.0).astype(bf16))
            got = dot_tn(jnp.concatenate(hits, axis=1), grads[sa])
            for m in range(4):
                partial[plan.src(sa, m)] = got[width * m : width * (m + 1), :]

    base = step_base(idx, step, pieces, per_piece)

    def multiply(v_ref, dv_ref):
        for k in range(STEP_GROUPS):
            at = rows_at(base + k, CAP)
            cut = slice(NSUB * k, NSUB * (k + 1))
            inbox = partial[:, at, :].reshape(sources * CAP, d_model).astype(bf16)
            left = s_ref[:, at, :].reshape(sources * CAP, NSUB).astype(bf16)
            dv_ref[cut, :] = dot_tn(left, inbox).astype(bf16)
            cross[:, at, :] = dot_nt(inbox, v_ref[cut, :]).reshape(sources, CAP, NSUB)

    for n in range(pieces):
        pl.when(step // per_piece == n)(functools.partial(multiply, vs[n], dvs[n]))

    @pl.when(step == pl.num_programs(0) - 1)
    def _():
        iota = lax.broadcasted_iota(jnp.int32, (NSUB, width), 0).astype(f32)

        def select(sa, carry):
            picked = []
            for m in range(4):
                src = plan.src(sa, m)
                turned = cross[src].T
                names = names_ref[src].astype(f32)
                picked += [
                    jnp.sum(jnp.where(iota == names[b : b + 1, :], turned, 0.0), axis=0, keepdims=True)
                    for b in range(8)
                ]
            picked = jnp.concatenate(picked, axis=0).astype(bf16)
            for ta in range(4):
                gw_ref[plan.src(sa, ta)] = picked
            return carry

        lax.fori_loop(0, 4, select, 0)


def write_call(idx, grads, names, layer, dense, values, plan, tokens):
    sources, width, _ = dense.shape
    specs, per_piece = value_specs(values, layer)
    d_model = values[0].shape[2]
    pieces = len(values)

    def dv_spec(n):
        return pl.BlockSpec(
            (STEP_GROUPS * NSUB, d_model), lambda g: (jnp.clip(g - n * per_piece, 0, per_piece - 1), 0)
        )

    return pl.pallas_call(
        functools.partial(write_kernel, plan=plan, pieces=pieces, per_piece=per_piece),
        grid=(per_piece * pieces,),
        out_shape=[shape((v.shape[1], d_model), bf16) for v in values]
        + [shape((sources, 32, width), bf16)],
        in_specs=[pl.BlockSpec(memory_space=pltpu.SMEM)]
        + [
            pl.BlockSpec((tokens, d_model), lambda g: (0, 0), pipeline_mode=pl.Buffered(1))
            for _ in range(4)
        ]
        + [
            pl.BlockSpec((sources, 16, width), lambda g: (0, 2 + layer, 0)),
            pl.BlockSpec((sources, width, NSUB), lambda g: (0, 0, 0), pipeline_mode=pl.Buffered(1)),
        ]
        + specs,
        out_specs=[dv_spec(n) for n in range(pieces)]
        + [pl.BlockSpec((sources, 32, width), lambda g: (0, 0, 0))],
        scratch_shapes=[
            pltpu.VMEM((4, tokens, d_model), bf16),
            pltpu.VMEM((sources, width, d_model), f32),
            pltpu.VMEM((sources, width, NSUB), f32),
        ],
        compiler_params=pltpu.CompilerParams(vmem_limit_bytes=50 * MIB),
        cost_estimate=pl.CostEstimate(
            flops=6 * sources * width * NSUB * d_model, bytes_accessed=28 * MIB, transcendentals=0
        ),
        name="memory_write",
    )(idx, *grads, names, dense, *values)


def sum_kernel(idx, m0, r1, r2, r3, o0, o1, o2, o3):
    count = o0.shape[0]
    for dz, out in enumerate((o0, o1, o2, o3)):
        at = slice(count * dz, count * (dz + 1))
        out[...] = (
            (m0[at, :].astype(f32) + r1[at, :].astype(f32))
            + (r2[at, :].astype(f32) + r3[at, :].astype(f32))
        ).astype(bf16)


def table_grad_kernel(a_ref, b_ref, *refs):
    refs[-1][...] = a_ref[...].astype(f32) + b_ref[...].astype(f32)


def table_grad_call(mine, arrived, layer, layers, earlier):
    rows, d_model = mine.shape
    block = min(rows, 512)
    specs = [pl.BlockSpec((block, d_model), lambda g: (g, 0))] * 2
    args = [mine, arrived]
    if earlier is not None:
        specs = specs + [pl.BlockSpec(memory_space=pl.ANY)]
        args.append(earlier)
    return pl.pallas_call(
        table_grad_kernel,
        grid=(rows // block,),
        out_shape=shape((layers, rows, d_model), f32),
        in_specs=specs,
        out_specs=pl.BlockSpec((None, block, d_model), lambda g: (layer, g, 0)),
        input_output_aliases={} if earlier is None else {2: 0},
        compiler_params=pltpu.CompilerParams(vmem_limit_bytes=32 * MIB),
        cost_estimate=pl.CostEstimate(flops=0, bytes_accessed=16 * MIB, transcendentals=0),
        name="table_grad",
    )(*args)


def gather_shards(x, axis):
    if lax.axis_size("fsdp") != 2:
        return lax.all_gather(x, "fsdp", axis=axis, tiled=True)
    other = swap(x, "fsdp", 1)
    mine = lax.axis_index("fsdp") == 0
    return jnp.where(
        mine, jnp.concatenate([x, other], axis=axis), jnp.concatenate([other, x], axis=axis)
    )


def shard_pieces(x, axis):
    if lax.axis_size("fsdp") != 2:
        return [lax.all_gather(x, "fsdp", axis=axis, tiled=True)]
    return [x, swap(x, "fsdp", 1)]


def reduce_packs(group):
    scattered = [lax.psum_scatter(p, "fsdp", scatter_dimension=0, tiled=False) for p in group]
    return [lax.psum(p, "ctx") for p in scattered]


def after(xs, *others):
    return list(lax.optimization_barrier((tuple(xs), tuple(others)))[0])


def body(
    inputs,
    query_weight,
    key_weight,
    value_weight,
    attention_weight,
    lookup_weight,
    gate_weight,
    memory_weight,
    first_table,
    second_table,
    attention_gain,
    memory_gain,
    memory_values,
    blocks,
    first_picks,
    second_picks,
    cotangent,
):
    plan = PLAN
    SA, TA = plan.SA, plan.TA
    layers = query_weight.shape[0]
    tokens = inputs.shape[1]
    d_model = inputs.shape[2]
    chunk = tokens // 4
    width = query_weight.shape[2]
    shards = lax.axis_size("fsdp")
    owners = lax.axis_size("ctx") * lax.axis_size("tp")
    groups = memory_values.shape[1] // NSUB
    lanes = shards * groups * CAP
    gbits = groups.bit_length() - 1
    dbits = owners.bit_length() - 1
    idx = jnp.stack(
        [lax.axis_index("fsdp"), lax.axis_index("ctx"), lax.axis_index("tp"), 0]
    ).astype(jnp.int32)

    gains = gather_shards(
        jnp.concatenate([attention_gain, memory_gain], axis=0).astype(bf16), 1
    ).astype(f32)

    def qkv_weight(l, queries, keys, values_):
        joined = jnp.concatenate([queries[l], keys[l], values_[l]], axis=1).astype(bf16)
        return shard_pieces(joined, 0)

    def gather_all(x):
        return lax.all_gather(x, ("fsdp", "tp"), axis=0, tiled=False)

    w_qkv = [qkv_weight(0, query_weight, key_weight, value_weight)]
    w_o, w_a, w_b = [], [], []

    firsts = jnp.swapaxes(first_picks[:, 0, 0], 1, 2)
    seconds = jnp.swapaxes(second_picks[:, 0, 0].reshape(layers, tokens, -1), 1, 2)
    height = layers * (8 + seconds.shape[1])
    name_box, *tables = kernel_call(
        functools.partial(slots_kernel, plan=plan, gbits=gbits, dbits=dbits),
        "pick_slots",
        [shape((owners, 16 * layers, lanes), bf16)] + [shape((height, chunk), jnp.int32)] * 4,
        idx,
        [firsts, seconds],
        [pltpu.VMEM((4, height, chunk), jnp.int32)],
    )
    w_qkv[0][-1], name_box, *tables = after([w_qkv[0][-1], name_box, *tables])
    ids_row = blocks
    ids_col = blocks.reshape(-1, 1)
    heads_shape = shape((tokens * 3 // 2, 2 * HD), bf16)
    folded = shape((tokens // 2, 2 * HD), bf16)
    part_shape = shape((chunk, d_model), bf16)
    chunk_shape = shape((chunk, d_model), f32)
    full_shape = shape((tokens, d_model), bf16)
    gain_shape = shape((1, d_model), f32)
    box_shape = shape((chunk, 2 * d_model), bf16)
    chunk_scratch = pltpu.VMEM((chunk, d_model), bf16)
    pack_scratch = pltpu.VMEM((4, tokens * 3 // 2, 2 * HD), bf16)
    part_scratch = pltpu.VMEM((tokens, d_model), bf16)
    kv_scratch = [
        pltpu.VMEM((4 * tokens, HD), bf16),
        pltpu.VMEM((4 * tokens, HD), bf16),
        pltpu.VMEM((4 * tokens, 1), jnp.int32),
    ]
    x = inputs[0]
    h_chunk = names = table = None
    h_chunks = []
    kept = []
    for l in range(layers):
        if l == 0:
            h1, *es = kernel_call(
                functools.partial(qkv_first_kernel, plan=plan, row=l),
                "qkv_first",
                [full_shape] + [heads_shape] * 4,
                idx,
                [x, gains, *w_qkv[l]],
                [pack_scratch],
            )
            qw, kw, vw, ow, lw, gw_, pw, ta_, tb_, mv = after(
                (
                    query_weight, key_weight, value_weight, attention_weight, lookup_weight,
                    gate_weight, memory_weight, first_table, second_table, memory_values,
                ),
                es[0],
            )
            a_boxes, b_boxes = [], []
            for n in range(layers):
                w_o.append(shard_pieces(ow[n].astype(bf16), 1))
                a_boxes.append(
                    jnp.concatenate(
                        [lw[n], jnp.concatenate([ta_[n, 0], tb_[n, 0]], axis=1)], axis=0
                    ).astype(bf16)
                )
                b_boxes.append(jnp.concatenate([gw_[n], to_pack(pw[n])], axis=0).astype(bf16))
                if n > 0:
                    w_qkv.append(qkv_weight(n, qw, kw, vw))
            w_a.append(gather_all(a_boxes[0]))
        else:
            h1, *es = kernel_call(
                functools.partial(qkv_kernel, plan=plan),
                "qkv",
                [full_shape] + [heads_shape] * 4,
                idx,
                [*h_chunks, *w_qkv[l]],
                [pack_scratch],
            )
        es = swaps(es, SA)
        if l == 0:
            (table,) = kernel_call(
                functools.partial(pick_table_kernel, plan=plan),
                "pick_table",
                [shape((layers, height // layers, tokens), jnp.int32)],
                idx,
                swaps(tables, TA),
                [pltpu.VMEM((4, height, chunk), jnp.int32)],
            )
            if shards == 2:
                values = [memory_values, swap(mv, "fsdp", 1)]
            else:
                values = [lax.all_gather(mv, "fsdp", axis=1, tiled=True)]
        else:
            w_a.append(gather_all(after([a_boxes[l]], h1)[0]))
        heads = kernel_call(
            functools.partial(attend_kernel, plan=plan),
            "attend",
            [folded] * 4,
            idx,
            [*es, ids_row, ids_col],
            kv_scratch,
        )
        heads = swaps(heads, SA)
        if l == 0:
            heads[3], table = after([heads[3], table])
        attended, *parts = kernel_call(
            functools.partial(out_kernel, plan=plan),
            "attend_out",
            [shape((tokens, width), bf16)] + [part_shape] * 4,
            idx,
            [*heads, *w_o[l]],
            [pltpu.VMEM((4, tokens, HD), bf16), part_scratch],
        )
        parts = swaps(parts, TA)
        middle, h2, u, w, outbox = kernel_call(
            functools.partial(lookup_kernel, plan=plan, row=layers + l, layer=l, shards=shards),
            "lookup",
            [
                chunk_shape,
                part_shape,
                shape((chunk, 8 * HD), bf16),
                shape((32, tokens), f32),
                shape((owners, 32 if l else 32 + name_box.shape[1], lanes), bf16),
            ],
            idx,
            [x, *parts, gains, w_a[l], table] + ([] if l else [name_box]),
        )
        weights = lax.all_to_all(outbox, ("ctx", "tp"), 0, 0, tiled=True)
        if l == 0:
            names = weights
        w_b.append(gather_all(after([b_boxes[l]], h2)[0]))
        (gate,) = kernel_call(
            functools.partial(gate_values_kernel, shards=shards),
            "gate_values",
            [chunk_shape],
            idx,
            [h2, w_b[l]],
        )
        *reads, dense = read_call(idx, weights, names, l, values, plan, tokens)
        reads = swaps(reads, "ctx")
        sums = kernel_call(sum_kernel, "memory_sum", [part_shape] * 4, idx, reads)
        sums = swaps(sums, "tp")
        if l + 1 < layers:
            mem, box, x3, h_chunk = kernel_call(
                functools.partial(gate_kernel, row=l + 1, shards=shards),
                "gate",
                [chunk_shape, box_shape, chunk_shape, part_shape],
                idx,
                [*sums, gate, w_b[l], middle, h2, gains],
                [chunk_scratch],
            )
            h_chunks = spread(h_chunk, TA)
        else:
            mem = x3 = None
            gn, box, back_box = kernel_call(
                functools.partial(gate_last_kernel, plan=plan, shards=shards),
                "gate_last",
                [part_shape, box_shape, box_shape],
                idx,
                [*sums, gate, w_b[l], middle, h2, cotangent[0]],
                [
                    pltpu.VMEM((chunk, d_model), f32),
                    chunk_scratch,
                    pltpu.VMEM((chunk, d_model), f32),
                    chunk_scratch,
                ],
            )
        kept.append((x, h1, es, attended, middle, u, w, gate, dense, mem, box))
        x = x3

    g = cotangent[0]
    packs = [None] * layers
    gain_rows = [None] * (2 * layers)
    table_grads = None
    table_list = [None] * layers
    output = dvs_above = None
    for l in reversed(range(layers)):
        x, h1, es, attended, middle, u, w, gate, dense, mem, box = kept[l]
        top = l == layers - 1
        line = jnp.concatenate(spread(gn, "tp"), axis=0)
        planes = spread(line, "ctx")
        if not top and shards == 2:
            table_grads = table_grad_call(*dvs_above, l + 1, layers, table_grads)
            planes[3], table_grads = after([planes[3], table_grads])
        *dvs, gw = write_call(idx, planes, names, l, dense, values, plan, tokens)
        if shards == 2:
            dvs_above = [dvs[0], swap(dvs[1], "fsdp", 1)]
        else:
            table_list[l] = lax.psum_scatter(dvs[0], "fsdp", scatter_dimension=0, tiled=True).astype(f32)
        if not top:
            back_all = lax.all_gather(after([back_box], line)[0], TA, axis=0, tiled=False)
            gw, back_all = after([gw, back_all])
        gw = lax.all_to_all(gw, ("ctx", "tp"), 0, 0, tiled=True)
        back_shape = shape((chunk, 10 * HD), bf16)
        g_mid, go_chunk, gain_rows[layers + l], *back = kernel_call(
            functools.partial(lookup_back_kernel, plan=plan, row=layers + l, layer=l, shards=shards),
            "lookup_back",
            [chunk_shape, part_shape, gain_shape] + [back_shape] * 4,
            idx,
            [gw, table, w, w_a[l], u, back_box, w_b[l], middle, g, gains],
            [
                pltpu.VMEM(w.shape, f32),
                pltpu.VMEM(u.shape, bf16),
                pltpu.VMEM((4, NSUB // 4, 8 * HD), bf16),
                pltpu.VMEM((chunk, d_model), f32),
            ],
        )
        go_chunks = spread(go_chunk, TA)
        if l == 0 and shards == 2:
            table_grads = table_grad_call(*dvs_above, l, layers, table_grads)
            go_chunks[3], table_grads = after([go_chunks[3], table_grads])
        go, *ups = kernel_call(
            functools.partial(out_back_kernel, plan=plan),
            "attend_out_back",
            [full_shape] + [folded] * 4,
            idx,
            [*go_chunks, *w_o[l]],
            [pltpu.VMEM((4, tokens // 2, 2 * HD), bf16)],
        )
        ups = swaps(ups, SA)
        back = swaps(back, TA)
        ups[3], *back = after([ups[3], *back])
        shard_size = d_model // shards
        head_grads = kernel_call(
            functools.partial(attend_back_kernel, plan=plan),
            "attend_back",
            [heads_shape] * 4,
            idx,
            [*es, *ups, ids_row, ids_col],
            kv_scratch + [pltpu.VMEM((4 * tokens, HD), f32)] * 2,
        )
        head_grads = swaps(head_grads, SA)
        if top:
            forward_all = lax.all_gather(after([box], line)[0], TA, axis=0, tiled=False)
            below_all = lax.all_gather(after([kept[l - 1][10]], line)[0], TA, axis=0, tiled=False)
        else:
            forward_all = below_all
        if top:
            back_all = lax.all_gather(after([back_box], line)[0], TA, axis=0, tiled=False)
        if top:
            output = back_all[:, :, d_model:].reshape(tokens, d_model)
        riders = [] if l else [inputs[0], *gain_rows[1:]]
        g_qkv, *parts = kernel_call(
            functools.partial(qkv_back_kernel, plan=plan, row=l, gain_rows=len(riders)),
            "qkv_back",
            [shape((tokens, 3 * width), bf16)] + [part_shape if l else shape((chunk + 16, d_model), bf16)] * 4,
            idx,
            [*head_grads, *w_qkv[l], *riders],
            [pack_scratch, part_scratch],
        )
        parts = swaps(parts, TA)
        qkv_rows = 3 * shard_size
        weight_rows = shard_size * 7 // 2 + NSUB // shards // 2
        weight_scratch = [
            pltpu.VMEM((shards, weight_rows, 256), bf16),
            pltpu.VMEM((tokens, d_model), bf16),
            pltpu.VMEM((tokens, width), bf16),
            pltpu.VMEM((tokens, width), bf16),
            pltpu.VMEM((tokens, 2 * HD), bf16),
            pltpu.VMEM((tokens, d_model), bf16),
        ]
        qkv_scratch = [pltpu.VMEM((shards, qkv_rows, 256), bf16)]
        split = l == 0 and shards == 2
        weight_outs = [shape((weight_rows, 256), bf16)] * 2 if split else [shape((shards, weight_rows, 256), bf16)]
        qkv_outs = [shape((qkv_rows, 256), bf16)] * 2 if split else [shape((shards, qkv_rows, 256), bf16)]
        qkv_packs = kernel_call(
            qkv_grad_kernel, "qkv_grad", qkv_outs, idx, [h1, g_qkv], qkv_scratch
        )
        weight_packs = kernel_call(
            functools.partial(weight_grad_kernel, plan=plan, has_full=top),
            "weight_grad",
            weight_outs,
            idx,
            [forward_all, back_all, *back, attended, go] + ([cotangent[0]] if top else []),
            weight_scratch,
        )
        if split:
            quarter = shape((qkv_rows // 4, 256), bf16)
            qkv_quarters = kernel_call(
                add_two_kernel, "qkv_add", [quarter] * 4, idx, [qkv_packs[0], swap(qkv_packs[1], "fsdp", 1)]
            )
            quarter = shape((weight_rows // 4, 256), bf16)
            weight_quarters = kernel_call(
                add_two_kernel,
                "weight_add",
                [quarter] * 4,
                idx,
                [weight_packs[0], swap(weight_packs[1], "fsdp", 1)],
            )
            weight_quarters = swaps(weight_quarters, "ctx")
            parts[3], *weight_quarters = after([parts[3], *weight_quarters])
        else:
            parts[3], weight_packs[0], qkv_packs[0], below_all = after(
                [parts[3], weight_packs[0], qkv_packs[0], below_all]
            )
            packs[l] = reduce_packs([weight_packs[0], qkv_packs[0]])
        if l > 0:
            below = kept[l - 1]
            g, gain_rows[l], gn, back_box = kernel_call(
                functools.partial(norm_back_kernel, plan=plan, row=l, shards=shards),
                "norm_back",
                [chunk_shape, gain_shape, part_shape, box_shape],
                idx,
                [*parts, x, g_mid, gains, w_b[l - 1], below[7], below[9]],
                [chunk_scratch],
            )
        else:
            g, gain_all, *gain_halves = kernel_call(
                functools.partial(norm_back_last_kernel, plan=plan, row=l),
                "norm_back_last",
                [part_shape, shape((16, d_model), f32), shape((16, 256), bf16), shape((16, 256), bf16)],
                idx,
                [*parts, x, g_mid, gains],
            )
    (input_gradient,) = kernel_call(
        functools.partial(place_kernel, plan=plan),
        "input_gradient",
        [shape((tokens, d_model), f32)],
        idx,
        spread(g, TA),
    )
    if shards != 2:
        table_grads = jnp.stack(table_list)
    gain_shapes = []
    if shards == 2:
        rows = (weight_rows + qkv_rows) // 4
        (part,) = kernel_call(
            plane_sum_kernel,
            "plane_sum",
            [shape((rows + 16, 256), bf16)],
            idx,
            [*weight_quarters, *swaps(qkv_quarters, "ctx"), gain_halves[0], swap(gain_halves[1], "fsdp", 1)],
        )
        part, *packs[1] = after([part, *packs[1]])
        late = spread(part, "ctx")
        gain_shapes = [shape((layers, d_model // 2), f32)] * 2
        flat = late + [p for l in range(1, layers) for p in packs[l]]
    else:
        gain_all = lax.psum(
            lax.psum_scatter(gain_all[: 2 * layers], "fsdp", scatter_dimension=1, tiled=True), "ctx"
        )
        flat = [p for l in range(layers) for p in packs[l]]
    shard_size = d_model // shards
    tall = shape((layers, shard_size, width), f32)
    wide = shape((layers, width, shard_size), f32)
    sub = shape((layers, 1, HD, NSUB // shards), f32)
    grads = kernel_call(
        functools.partial(finalize_kernel, layers=layers, late=shards == 2),
        "finalize",
        [tall, tall, tall, wide, shape((layers, shard_size, 2 * HD), f32), tall, wide, sub, sub]
        + gain_shapes,
        idx,
        flat,
        [pltpu.VMEM((weight_rows, 256), bf16), pltpu.VMEM((qkv_rows, 256), bf16)] if shards == 2 else [],
    )
    gain_grads = grads[9:] if shards == 2 else [gain_all[:layers], gain_all[layers:]]
    return (
        output[None],
        input_gradient[None],
        *grads[:7],
        *[jnp.swapaxes(t, 2, 3) for t in grads[7:9]],
        *gain_grads,
        table_grads,
    )


def solution(mesh):
    placed = (
        P("fsdp", "ctx", None),
        P(None, "fsdp", "tp"),
        P(None, "fsdp", "tp"),
        P(None, "fsdp", "tp"),
        P(None, "tp", "fsdp"),
        P(None, "fsdp", "tp"),
        P(None, "fsdp", "tp"),
        P(None, "tp", "fsdp"),
        P(None, "tp", "fsdp", None),
        P(None, "tp", "fsdp", None),
        P(None, "fsdp"),
        P(None, "fsdp"),
        P(None, ("fsdp", "ctx", "tp"), None),
        P("fsdp", None),
        P(None, "fsdp", "tp", "ctx", None),
        P(None, "fsdp", "tp", "ctx", None, None),
        P("fsdp", "ctx", None),
    )
    return jax.shard_map(
        body,
        mesh=mesh,
        in_specs=placed,
        out_specs=(
            P("fsdp", "ctx", None),
            P("fsdp", "ctx", None),
            P(None, "fsdp", "tp"),
            P(None, "fsdp", "tp"),
            P(None, "fsdp", "tp"),
            P(None, "tp", "fsdp"),
            P(None, "fsdp", "tp"),
            P(None, "fsdp", "tp"),
            P(None, "tp", "fsdp"),
            P(None, "tp", "fsdp", None),
            P(None, "tp", "fsdp", None),
            P(None, "fsdp"),
            P(None, "fsdp"),
            P(None, ("fsdp", "ctx", "tp"), None),
        ),
        check_vma=False,
    )
```

```python
import functools

import jax
import jax.numpy as jnp
from jax import lax
from jax.experimental import pallas as pl
from jax.experimental.pallas import tpu as pltpu
from jax.sharding import PartitionSpec as P

HD = 64
NSUB = 256
CAP = 8
EPS = 1e-05
NEG = -1e30
f32 = jnp.float32
bf16 = jnp.bfloat16
MIB = 1 << 20


def dot(a, b):
    return jnp.dot(a, b, preferred_element_type=f32)


def dot_nt(a, b):
    return lax.dot_general(a, b, (((1,), (1,)), ((), ())), preferred_element_type=f32)


def dot_tn(a, b):
    return lax.dot_general(a, b, (((0,), (0,)), ((), ())), preferred_element_type=f32)


def swap(x, axis, step):
    size = lax.axis_size(axis)
    return lax.ppermute(x, axis, [(i, i ^ step) for i in range(size)])


def swaps(xs, axis):
    return [xs[0]] + [swap(xs[d], axis, d) for d in range(1, len(xs))]


def spread(x, axis):
    return [x] + [swap(x, axis, d) for d in range(1, lax.axis_size(axis))]


def shape(dims, dtype):
    return jax.ShapeDtypeStruct(dims, dtype)


def kernel_call(body, name, outs, idx, args, scratch=(), limit=50, flops=0):
    limit = {'norm_back_last': 16, 'plane_sum': 16, 'input_gradient': 16, 'finalize': 24, 'weight_add': 16, 'qkv_add': 16}.get(name, limit)
    in_specs = [pl.BlockSpec(memory_space=pltpu.SMEM)]
    in_specs += [pl.BlockSpec(memory_space=pltpu.VMEM) for _ in args]
    moved = sum(a.size * a.dtype.itemsize for a in args)
    moved += sum(o.size * o.dtype.itemsize for o in outs)
    out = pl.pallas_call(
        body,
        out_shape=outs,
        in_specs=in_specs,
        out_specs=[pl.BlockSpec(memory_space=pltpu.VMEM) for _ in outs],
        scratch_shapes=list(scratch),
        compiler_params=pltpu.CompilerParams(vmem_limit_bytes=limit * MIB),
        cost_estimate=pl.CostEstimate(flops=flops, bytes_accessed=moved, transcendentals=0),
        name=name,
    )(idx, *args)
    return list(out)


def rows_at(index, count):
    return pl.ds(pl.multiple_of(index * count, count), count)


def rms(x, gain):
    factor = lax.rsqrt(jnp.mean(x * x, axis=1, keepdims=True) + EPS)
    return factor, x * factor * gain


def rms_back(x, factor, gain, upstream):
    scaled = upstream * gain
    return factor * scaled - x * factor**3 * jnp.mean(scaled * x, axis=1, keepdims=True)


def total4(refs):
    return (refs[0][...].astype(f32) + refs[1][...].astype(f32)) + (
        refs[2][...].astype(f32) + refs[3][...].astype(f32)
    )


def fold(x):
    half = x.shape[0] // 2
    return jnp.concatenate([x[:half], x[half:]], axis=1)


def unfold(x):
    half = x.shape[1] // 2
    return jnp.concatenate([x[:, :half], x[:, half:]], axis=0)


class Plan:
    def __init__(self, SA, TA):
        self.SA, self.TA = SA, TA
        self.si = 1 if SA == "ctx" else 2
        self.ti = 1 if TA == "ctx" else 2

    def src(self, sa, ta):
        return sa * 4 + ta if self.SA == "ctx" else ta * 4 + sa

    def rel(self, ds, dt):
        return (ds, dt) if self.SA == "ctx" else (dt, ds)


PLAN = Plan("ctx", "tp")


def slots_kernel(idx, first_ref, second_ref, out_ref, t0, t1, t2, t3, table, plan, gbits, dbits):
    layers, picks, tokens = first_ref.shape
    inner = second_ref.shape[1]
    owners, _, width = out_ref.shape
    lanes = owners * width
    chunk = tokens // 4
    iota = lax.broadcasted_iota(jnp.int32, (NSUB, tokens), 0)
    before = lax.broadcasted_iota(jnp.int32, (tokens, tokens), 0) < lax.broadcasted_iota(
        jnp.int32, (tokens, tokens), 1
    )
    before = jnp.where(before, 1.0, 0.0).astype(bf16)
    row = lax.broadcasted_iota(jnp.int32, (lanes, tokens), 0)
    token_row = (lax.broadcasted_iota(jnp.int32, (8, tokens), 1) + 1).astype(f32)
    token_row = jnp.where(
        lax.broadcasted_iota(jnp.int32, (8, tokens), 0) == 0, token_row, 0.0
    )
    for l in range(layers):
        onehot = jnp.zeros((NSUB, tokens), f32)
        for i in range(picks):
            onehot = jnp.where(iota == first_ref[l, i : i + 1, :], 1.0, onehot)
        counts = dot(onehot.astype(bf16), before)
        total = jnp.zeros((16, lanes), f32)
        slots = []
        for i in range(picks):
            first = first_ref[l, i : i + 1, :]
            rank = jnp.sum(jnp.where(iota == first, counts, 0.0), axis=0, keepdims=True)
            shard = lax.shift_right_logical(first, gbits)
            group = lax.shift_right_logical(shard, dbits) * (1 << gbits) + (first & ((1 << gbits) - 1))
            slot = (shard & ((1 << dbits) - 1)) * width + group * CAP + rank.astype(jnp.int32)
            slots.append(slot)
            names = jnp.concatenate(
                [second_ref[l, 8 * i : 8 * i + 8, :].astype(f32), token_row], axis=0
            )
            hit = jnp.where(row == slot, 1.0, 0.0).astype(bf16)
            total = total + dot_nt(names.astype(bf16), hit)
        for d in range(owners):
            out_ref[d, 16 * l : 16 * l + 16, :] = total[:, d * width : (d + 1) * width].astype(bf16)
        both = jnp.concatenate([first_ref[l], jnp.concatenate(slots, axis=0)], axis=0)
        for n in range(4):
            cut = slice(n * chunk, (n + 1) * chunk)
            at = l * (8 + inner)
            table[n, at : at + 8, :] = both[:, cut]
            table[n, at + 8 : at + 8 + inner, :] = second_ref[l, :, cut]
    for d, out in enumerate((t0, t1, t2, t3)):
        out[...] = table[idx[plan.ti] ^ d]


def pick_table_kernel(idx, t0, t1, t2, t3, out_ref, table, plan):
    for d, t in enumerate((t0, t1, t2, t3)):
        table[idx[plan.ti] ^ d] = t[...]
    rows = out_ref.shape[1]
    for l in range(out_ref.shape[0]):
        out_ref[l] = jnp.concatenate([table[n, rows * l : rows * (l + 1), :] for n in range(4)], axis=1)


def head_mask(shape_, lanes_each):
    return lax.broadcasted_iota(jnp.int32, shape_, 1) // lanes_each


def place_chunks(refs, full, t):
    count = refs[0].shape[0]
    for d in range(4):
        full[rows_at(t ^ d, count), :] = refs[d][...]


def emit_chunks(part, outs, t):
    count = outs[0].shape[0]
    for d in range(4):
        outs[d][...] = part[rows_at(t ^ d, count), :]


def piece_at(f, j, pieces, size):
    return rows_at(f ^ j, size) if len(pieces) > 1 else slice(0, size)


def emit_heads(h_ref, pieces, pack, outs, idx, plan):
    width = pieces[0].shape[1] // 3
    size = pieces[0].shape[0]
    qkv = sum(
        dot(h_ref[:, piece_at(idx[0], j, pieces, size)], w[...]) for j, w in enumerate(pieces)
    ).astype(bf16)
    for j in range(4):
        q = qkv[:, HD * j : HD * (j + 1)]
        k = qkv[:, width + HD * j : width + HD * (j + 1)]
        v = qkv[:, 2 * width + HD * j : 2 * width + HD * (j + 1)]
        pack[j] = jnp.concatenate([jnp.concatenate([q, k], axis=1), fold(v)], axis=0)
    for d in range(4):
        outs[d][...] = pack[idx[plan.si] ^ d]


def qkv_first_kernel(idx, x_ref, gain_ref, *refs, plan, row):
    *pieces, h_ref, e0, e1, e2, e3, pack = refs
    _, normed = rms(x_ref[...].astype(f32), gain_ref[row : row + 1, :])
    h_ref[...] = normed.astype(bf16)
    emit_heads(h_ref, pieces, pack, (e0, e1, e2, e3), idx, plan)


def qkv_kernel(idx, h0, h1, h2, h3, *refs, plan):
    *pieces, h_ref, e0, e1, e2, e3, pack = refs
    place_chunks((h0, h1, h2, h3), h_ref, idx[plan.ti])
    emit_heads(h_ref, pieces, pack, (e0, e1, e2, e3), idx, plan)


def load_heads(es, kk, vv):
    for d in range(4):
        rows = es[d].shape[0] * 2 // 3
        kk[rows * d : rows * (d + 1), :] = es[d][0:rows, HD : 2 * HD]
        vv[rows * d : rows * (d + 1), :] = unfold(es[d][rows:, :])


def load_ids(col_ref, ids_col, s):
    count = col_ref.shape[0] // 4
    for d in range(4):
        ids_col[count * d : count * (d + 1), :] = col_ref[rows_at(s ^ d, count), :]


def probabilities(kk, q, key_ids, query_ids):
    scores = dot_nt(kk, q) * (HD ** (-0.5))
    scores = jnp.where(key_ids <= query_ids, scores, NEG)
    top = jnp.max(scores, axis=0, keepdims=True)
    exponent = jnp.exp(scores - top)
    return exponent * (1.0 / jnp.sum(exponent, axis=0, keepdims=True))


def attend_kernel(idx, e0, e1, e2, e3, row_ref, col_ref, a0, a1, a2, a3, kk, vv, ids_col, plan):
    es, outs = (e0, e1, e2, e3), (a0, a1, a2, a3)
    s = idx[plan.si]
    load_heads(es, kk, vv)
    load_ids(col_ref, ids_col, s)
    count = kk.shape[0] // 4
    for d in range(4):
        query_ids = row_ref[:, rows_at(s ^ d, count)]
        p = probabilities(kk[...], es[d][0:count, 0:HD], ids_col[...], query_ids)
        blended = dot_tn(vv[...], p.astype(bf16))
        outs[d][...] = fold(blended.T.astype(bf16))


def attend_back_kernel(
    idx, e0, e1, e2, e3, u0, u1, u2, u3, row_ref, col_ref, g0, g1, g2, g3, kk, vv, ids_col, gk, gv, plan
):
    es, us, outs = (e0, e1, e2, e3), (u0, u1, u2, u3), (g0, g1, g2, g3)
    s = idx[plan.si]
    load_heads(es, kk, vv)
    load_ids(col_ref, ids_col, s)
    count = kk.shape[0] // 4
    scale = HD ** (-0.5)
    for d in range(4):
        query_ids = row_ref[:, rows_at(s ^ d, count)]
        q = es[d][0:count, 0:HD]
        up = unfold(us[d][...])
        p = probabilities(kk[...], q, ids_col[...], query_ids)
        gp = dot_nt(vv[...], up)
        centre = jnp.sum(p * gp, axis=0, keepdims=True)
        gs = (p * (gp - centre)).astype(bf16)
        gq = (dot_tn(kk[...], gs) * scale).T.astype(bf16)
        outs[d][0:count, 0:HD] = gq
        key_term = dot(gs, q)
        value_term = dot(p.astype(bf16), up)
        if d == 0:
            gk[...] = key_term
            gv[...] = value_term
        else:
            gk[...] += key_term
            gv[...] += value_term
    for d in range(4):
        outs[d][0:count, HD : 2 * HD] = (gk[count * d : count * (d + 1), :] * scale).astype(bf16)
        outs[d][count:, :] = fold(gv[count * d : count * (d + 1), :].astype(bf16))


def out_kernel(idx, a0, a1, a2, a3, *refs, plan):
    *pieces, a_ref, p0, p1, p2, p3, heads, part = refs
    for d, a in enumerate((a0, a1, a2, a3)):
        heads[idx[plan.si] ^ d] = unfold(a[...])
    a_ref[...] = jnp.concatenate([heads[j] for j in range(4)], axis=1)
    size = pieces[0].shape[1]
    for j, w in enumerate(pieces):
        part[:, piece_at(idx[0], j, pieces, size)] = dot(a_ref[...], w[...]).astype(bf16)
    emit_chunks(part, (p0, p1, p2, p3), idx[plan.ti])


def out_back_kernel(idx, g0, g1, g2, g3, *refs, plan):
    *pieces, go_ref, u0, u1, u2, u3, pack = refs
    place_chunks((g0, g1, g2, g3), go_ref, idx[plan.ti])
    size = pieces[0].shape[1]
    up = sum(
        dot_nt(go_ref[:, piece_at(idx[0], j, pieces, size)], w[...]) for j, w in enumerate(pieces)
    ).astype(bf16)
    for j in range(4):
        pack[j] = fold(up[:, HD * j : HD * (j + 1)])
    for d, u in enumerate((u0, u1, u2, u3)):
        u[...] = pack[idx[plan.si] ^ d]


def qkv_back_kernel(idx, g0, g1, g2, g3, *refs, plan, row=None, gain_rows=0):
    *ins, g_ref, p0, p1, p2, p3, pack, part = refs
    x_ref, *rows_refs = ins[len(ins) - gain_rows :] if gain_rows else [None]
    pieces = ins[: len(ins) - gain_rows]
    for d, g in enumerate((g0, g1, g2, g3)):
        pack[idx[plan.si] ^ d] = g[...]
    rows = g_ref.shape[0]
    columns = [pack[j, 0:rows, 0:HD] for j in range(4)]
    columns += [pack[j, 0:rows, HD : 2 * HD] for j in range(4)]
    columns += [unfold(pack[j, rows:, :]) for j in range(4)]
    g_ref[...] = jnp.concatenate(columns, axis=1)
    size = pieces[0].shape[0]
    if not gain_rows:
        for j, w in enumerate(pieces):
            part[:, piece_at(idx[0], j, pieces, size)] = dot_nt(g_ref[...], w[...]).astype(bf16)
        emit_chunks(part, (p0, p1, p2, p3), idx[plan.ti])
        return
    x = x_ref[...].astype(f32)
    factor = lax.rsqrt(jnp.mean(x * x, axis=1, keepdims=True) + EPS)
    count = part.shape[0] // 4
    for j, w in enumerate(pieces):
        at = piece_at(idx[0], j, pieces, size)
        term = dot_nt(g_ref[...], w[...])
        part[:, at] = term.astype(bf16)
        change = jnp.sum(term * (x_ref[:, at].astype(f32) * factor), axis=0, keepdims=True)
        p0[count : count + 1, at] = change.astype(bf16)
    blank = jnp.zeros((p0.shape[0] - count - gain_rows, p0.shape[1]), f32)
    tail = [p0[count : count + 1, :].astype(f32)] + [r[...] for r in rows_refs] + [blank]
    tail = jnp.concatenate(tail, axis=0).astype(bf16)
    for d, out in enumerate((p0, p1, p2, p3)):
        out[0:count, :] = part[rows_at(idx[plan.ti] ^ d, count), :]
        out[count:, :] = tail


def to_pack(x):
    rows, width = x.shape
    if width >= 256:
        return jnp.concatenate([x[:, 256 * i : 256 * (i + 1)] for i in range(width // 256)], axis=0)
    fold_by = 256 // width
    rows = rows // fold_by
    return jnp.concatenate([x[rows * i : rows * (i + 1)] for i in range(fold_by)], axis=1)


def from_pack(p, rows, width):
    if width >= 256:
        return jnp.concatenate([p[rows * i : rows * (i + 1)] for i in range(width // 256)], axis=1)
    return jnp.concatenate([p[:, width * i : width * (i + 1)] for i in range(256 // width)], axis=0)


def shard_rows(x, f, shards):
    size = x.shape[0] // shards
    return x[size * f : size * (f + 1)]


def shard_columns(x, f, shards):
    size = x.shape[1] // shards
    return x[:, size * f : size * (f + 1)]


def emit_shards(pack, outs, idx):
    if len(outs) == 1:
        outs[0][...] = pack[...]
    else:
        outs[0][...] = pack[idx[0]]
        outs[1][...] = pack[idx[0] ^ 1]


def qkv_grad_kernel(idx, h_ref, g_ref, *refs):
    *outs, pack = refs
    shards = pack.shape[0]
    change = dot_tn(h_ref[...], g_ref[...])
    for f in range(shards):
        pack[f] = to_pack(shard_rows(change, f, shards)).astype(bf16)
    emit_shards(pack, outs, idx)


def weight_grad_kernel(idx, *refs, plan, has_full):
    forward, back, near, (a_ref, go_ref) = refs[0], refs[1], refs[2:6], refs[6:8]
    full = refs[8] if has_full else None
    *outs, pack, h, z, gg, gu, gy = refs[8 + has_full :]
    chunk = forward.shape[1]
    d_model = h.shape[1]
    quarter = z.shape[1]
    shards = pack.shape[0]
    tables = jnp.zeros((NSUB, 2 * HD), f32)
    mine = rows_at(idx[plan.ti], quarter)
    for d in range(4):
        at = slice(chunk * d, chunk * (d + 1))
        h[at, :] = forward[d, :, 0:d_model]
        z[at, :] = forward.at[:, :, d_model:][d, :, mine]
        gg[at, :] = back.at[:, :, 0:d_model][d, :, mine]
        gu[rows_at(idx[plan.ti] ^ d, chunk), :] = near[d][:, 0 : 2 * HD]
        folded = near[d][:, 2 * HD :].astype(f32)
        tables = tables + jnp.concatenate(
            [folded[:, 2 * HD * i : 2 * HD * (i + 1)] for i in range(4)], axis=0
        )
        gy[at, :] = full[at, :] if has_full else back[d, :, d_model:]
    gate_change = dot_tn(h[...], gg[...])
    look_change = dot_tn(h[...], gu[...])
    mem_change = dot_tn(z[...], gy[...])
    out_change = dot_tn(a_ref[...], go_ref[...])
    for f in range(shards):
        pack[f] = jnp.concatenate(
            [
                to_pack(shard_rows(gate_change, f, shards)),
                to_pack(shard_columns(mem_change, f, shards)),
                to_pack(shard_rows(look_change, f, shards)),
                to_pack(shard_rows(tables, f, shards)),
                to_pack(shard_columns(out_change, f, shards)),
            ],
            axis=0,
        ).astype(bf16)
    emit_shards(pack, outs, idx)


def finalize_kernel(idx, *refs, layers, late):
    count = 2 * layers + 2 * late
    ins, outs = refs[:count], refs[count:]
    q_ref, k_ref, v_ref, o_ref, look_ref, gate_ref, mem_ref, first_ref, second_ref = outs[:9]
    part = q_ref.shape[1]
    for l in range(layers):
        if l > 0 or not late:
            memory, qkv = ins[2 * l + 2 * late], ins[2 * l + 2 * late + 1]
        else:
            one_ref, two_ref, memory, qkv = outs[9:]
            rows, more = memory.shape[0] // 4, qkv.shape[0] // 4
            total = 0.0
            for d in range(4):
                memory[rows_at(idx[1] ^ d, rows), :] = ins[d][0:rows, :]
                qkv[rows_at(idx[1] ^ d, more), :] = ins[d][rows : rows + more, :]
                total = total + ins[d][rows + more :, :].astype(f32)
            total = jnp.concatenate([total[0:8], total[8:16]], axis=1)
            one_ref[...] = total[0:layers]
            two_ref[...] = total[layers : 2 * layers]
        for n, ref in enumerate((q_ref, k_ref, v_ref)):
            ref[l] = qkv[part * n : part * (n + 1), :].astype(f32)
        gate_ref[l] = memory[0:part, :].astype(f32)
        mem_ref[l] = from_pack(memory[part : 2 * part, :], mem_ref.shape[1], mem_ref.shape[2]).astype(f32)
        at = 2 * part + part // 2
        look_ref[l] = from_pack(memory[2 * part : at, :].astype(f32), part, look_ref.shape[2])
        rows = first_ref.shape[3]
        tables = from_pack(memory[at : at + rows // 2, :].astype(f32), rows, 2 * HD)
        first_ref[l, 0] = tables[:, :HD].T
        second_ref[l, 0] = tables[:, HD:].T
        at = at + rows // 2
        o_ref[l] = from_pack(memory[at : at + part, :], o_ref.shape[1], o_ref.shape[2]).astype(f32)


def add_two_kernel(idx, a, b, o0, o1, o2, o3):
    chunk = o0.shape[0]
    for d, out in enumerate((o0, o1, o2, o3)):
        at = rows_at(idx[1] ^ d, chunk)
        out[...] = (a[at, :].astype(f32) + b[at, :].astype(f32)).astype(bf16)


def plane_sum_kernel(idx, *refs):
    a, b, (g0, g1, out) = refs[0:4], refs[4:8], refs[8:]
    rows = a[0].shape[0]
    more = rows + b[0].shape[0]
    out[0:rows, :] = total4(a).astype(bf16)
    out[rows:more, :] = total4(b).astype(bf16)
    out[more:, :] = (g0[...].astype(f32) + g1[...].astype(f32)).astype(bf16)


def own_rows(ref, idx, plan, count):
    if ref.shape[0] == count:
        return ref[...].astype(f32)
    return ref[rows_at(idx[plan.ti], count), :].astype(f32)


def table_of(a_ref, m, shards):
    size = a_ref.shape[1] * 4 // 5
    both = [a_ref[f * 4 + m, size:, :] for f in range(shards)]
    both = both[0] if shards == 1 else jnp.concatenate(both, axis=0)
    return both[:, :HD], both[:, HD:]


def only_head(x, m, chunk):
    lane = lax.broadcasted_iota(jnp.int32, x.shape, 1)
    return jnp.where((lane >= m * chunk) & (lane < (m + 1) * chunk), x, 0.0)


def lookup_kernel(
    idx, x_ref, p0, r1, r2, r3, gain_ref, a_ref, pick_ref, *refs, plan, row, layer, shards
):
    *names_ref, x_out, h_ref, u_ref, w_ref, out_ref = refs
    chunk = p0.shape[0]
    x = own_rows(x_ref, idx, plan, chunk) + total4((p0, r1, r2, r3))
    x_out[...] = x
    _, normed = rms(x, gain_ref[row : row + 1, :])
    h_ref[...] = normed.astype(bf16)
    size = a_ref.shape[1] * 4 // 5
    c1, c2 = [], []
    for m in range(4):
        u = sum(
            dot(h_ref[:, size * f : size * (f + 1)], a_ref[f * 4 + m, 0:size, :]) for f in range(shards)
        ).astype(bf16)
        u_ref[:, 2 * HD * m : 2 * HD * (m + 1)] = u
        ka, kb = table_of(a_ref, m, shards)
        c1.append(dot_nt(ka, u[:, :HD]))
        c2.append(dot_nt(kb, u[:, HD:]))
    c1 = jnp.concatenate(c1, axis=1)
    c2 = jnp.concatenate(c2, axis=1)
    lanes = c1.shape[1]
    iota = lax.broadcasted_iota(jnp.int32, (NSUB, lanes), 0)
    for i in range(4):
        first = pick_ref[layer, i : i + 1, :]
        base = jnp.sum(jnp.where(iota == first, c1, 0.0), axis=0, keepdims=True)
        for b in range(8):
            r = i * 8 + b
            second = pick_ref[layer, 8 + r : 9 + r, :]
            picked = jnp.sum(jnp.where(iota == second, c2, 0.0), axis=0, keepdims=True)
            w_ref[r : r + 1, :] = base + picked
    logits = w_ref[...]
    exponent = jnp.exp(logits - jnp.max(logits, axis=0, keepdims=True))
    w = exponent * (1.0 / jnp.sum(exponent, axis=0, keepdims=True))
    w_ref[...] = w
    owners, _, width = out_ref.shape
    slots = lax.broadcasted_iota(jnp.int32, (owners * width, lanes), 0)
    total = jnp.zeros((32, owners * width), f32)
    for i in range(4):
        hit = jnp.where(slots == pick_ref[layer, 4 + i : 5 + i, :], 1.0, 0.0).astype(bf16)
        mine = w[8 * i : 8 * (i + 1), :]
        split = jnp.concatenate([only_head(mine, m, chunk) for m in range(4)], axis=0)
        total = total + dot_nt(split.astype(bf16), hit)
    for d in range(owners):
        out_ref[d, 0:32, :] = total[:, d * width : (d + 1) * width].astype(bf16)
        if names_ref:
            out_ref[d, 32:, :] = names_ref[0][d]


def gate_part(b_ref, n):
    return b_ref[n, 0 : b_ref.shape[1] // 2, :]


def memory_part(b_ref, n):
    size = b_ref.shape[1] // 2
    return from_pack(b_ref[n, size:, :], b_ref.shape[2], size)


def gate_values_kernel(idx, h_ref, b_ref, gate_ref, shards):
    size, quarter = b_ref.shape[1] // 2, b_ref.shape[2]
    for t in range(4):
        gate_ref[:, quarter * t : quarter * (t + 1)] = sum(
            dot(h_ref[:, size * f : size * (f + 1)], gate_part(b_ref, f * 4 + t)) for f in range(shards)
        )


def gate_sum(sums, gate_ref, b_ref, x_ref, mem_ref, z_ref, x_out, shards):
    mem = total4(sums)
    mem_ref[...] = mem
    gate = gate_ref[...]
    z_ref[...] = (mem * (gate * jax.nn.sigmoid(gate))).astype(bf16)
    size, quarter = b_ref.shape[1] // 2, b_ref.shape[2]
    for f in range(shards):
        at = slice(size * f, size * (f + 1))
        x_out[:, at] = x_ref[:, at] + sum(
            dot(z_ref[:, quarter * t : quarter * (t + 1)], memory_part(b_ref, f * 4 + t)) for t in range(4)
        )


def gate_kernel(
    idx, s0, s1, s2, s3, gate_ref, b_ref, x_ref, h_ref, gain_ref, mem_ref, box_ref, x_out, h_out, z, row, shards
):
    gate_sum((s0, s1, s2, s3), gate_ref, b_ref, x_ref, mem_ref, z, x_out, shards)
    h_out[...] = rms(x_out[...], gain_ref[row : row + 1, :])[1].astype(bf16)
    fill_box(box_ref, h_ref, z)


def fill_box(box_ref, left_ref, right_ref):
    width = left_ref.shape[1]
    box_ref[:, 0:width] = left_ref[...]
    box_ref[:, width:] = right_ref[...]


def gate_last_kernel(
    idx, s0, s1, s2, s3, gate_ref, b_ref, x_ref, h_ref, g_ref,
    n_ref, box_ref, back_ref, mem, z, x_out, gy, plan, shards,
):
    gate_sum((s0, s1, s2, s3), gate_ref, b_ref, x_ref, mem, z, x_out, shards)
    gy[...] = g_ref[rows_at(idx[plan.ti], gy.shape[0]), :]
    gate_back(gy, b_ref, gate_ref, mem, n_ref, back_ref, shards)
    back_ref[:, gy.shape[1] :] = x_out[...].astype(bf16)
    fill_box(box_ref, h_ref, z)


def gate_back(gy_ref, b_ref, gate_ref, mem_ref, gn_ref, gg_ref, shards):
    size, quarter = b_ref.shape[1] // 2, b_ref.shape[2]
    for t in range(4):
        at = slice(quarter * t, quarter * (t + 1))
        gz = sum(
            dot_nt(gy_ref[:, size * f : size * (f + 1)], memory_part(b_ref, f * 4 + t)) for f in range(shards)
        )
        gate = gate_ref[:, at]
        sigmoid = jax.nn.sigmoid(gate)
        gn_ref[:, at] = (gz * (gate * sigmoid)).astype(bf16)
        slope = sigmoid * (1.0 + gate * (1.0 - sigmoid))
        gg_ref[:, at] = (gz * mem_ref[:, at] * slope).astype(bf16)


def norm_back(idx, parts, x_ref, g_ref, gain_ref, dgain_ref, plan, row):
    count = parts[0].shape[0]
    upstream = total4(parts)
    x = own_rows(x_ref, idx, plan, count)
    gain = gain_ref[row : row + 1, :]
    factor, _ = rms(x, gain)
    dgain_ref[...] = jnp.sum(upstream * x * factor, axis=0, keepdims=True)
    return g_ref[...] + rms_back(x, factor, gain, upstream)


def norm_back_kernel(
    idx, p0, r1, r2, r3, x_ref, g_ref, gain_ref, b_ref, gate_ref, mem_ref,
    gx_ref, dgain_ref, gn_ref, back_ref, gy, plan, row, shards,
):
    gx = norm_back(idx, (p0, r1, r2, r3), x_ref, g_ref, gain_ref, dgain_ref, plan, row)
    gx_ref[...] = gx
    gy[...] = gx.astype(bf16)
    gate_back(gy, b_ref, gate_ref, mem_ref, gn_ref, back_ref, shards)
    back_ref[:, gy.shape[1] :] = gy[...]


def norm_back_last_kernel(
    idx, p0, r1, r2, r3, x_ref, g_ref, gain_ref, out_ref, all_ref, mine_ref, other_ref, plan, row
):
    count = out_ref.shape[0]
    refs = (p0, r1, r2, r3)
    upstream = total4([r.at[0:count] for r in refs])
    x = own_rows(x_ref, idx, plan, count)
    factor, _ = rms(x, gain_ref[row : row + 1, :])
    gx = g_ref[...] + rms_back(x, factor, gain_ref[row : row + 1, :], upstream)
    out_ref[...] = gx.astype(bf16)
    all_ref[...] = total4([r.at[count:] for r in refs])
    size = all_ref.shape[1] // 2
    for j, out in enumerate((mine_ref, other_ref)):
        half = all_ref[:, rows_at(idx[0] ^ j, size)]
        out[...] = jnp.concatenate([half[:8, 0:256], half[:8, 256:]], axis=0).astype(bf16)


def place_kernel(idx, c0, c1, c2, c3, out_ref, plan):
    chunk = c0.shape[0]
    for d, c in enumerate((c0, c1, c2, c3)):
        out_ref[rows_at(idx[plan.ti] ^ d, chunk), :] = c[...].astype(out_ref.dtype)


def lookup_back_kernel(
    idx, gw_ref, pick_ref, w_ref, a_ref, u_ref, gg_ref, b_ref, x_ref, g_ref, gain_ref,
    gx_ref, go_ref, dgain_ref, b0, b1, b2, b3, gl, gu_all, tables, gh, plan, row, layer, shards,
):
    chunk = u_ref.shape[0]
    owners, _, width = gw_ref.shape
    lanes = w_ref.shape[1]
    slots = lax.broadcasted_iota(jnp.int32, (owners * width, lanes), 0)
    arrived = jnp.concatenate([gw_ref[d] for d in range(owners)], axis=1)
    for i in range(4):
        hit = jnp.where(slots == pick_ref[layer, 4 + i : 5 + i, :], 1.0, 0.0).astype(bf16)
        mixed = dot(arrived, hit)
        gl[8 * i : 8 * (i + 1), :] = sum(
            only_head(mixed[8 * m : 8 * (m + 1), :], m, chunk) for m in range(4)
        )
    w = w_ref[...]
    gw = gl[...]
    gl[...] = w * (gw - jnp.sum(w * gw, axis=0, keepdims=True))
    iota = lax.broadcasted_iota(jnp.int32, (NSUB, lanes), 0)
    gc1 = jnp.zeros((NSUB, lanes), f32)
    gc2 = jnp.zeros((NSUB, lanes), f32)
    for i in range(4):
        both = jnp.sum(gl[8 * i : 8 * (i + 1), :], axis=0, keepdims=True)
        gc1 = jnp.where(iota == pick_ref[layer, i : i + 1, :], both, gc1)
        for b in range(8):
            r = i * 8 + b
            gc2 = gc2 + jnp.where(iota == pick_ref[layer, 8 + r : 9 + r, :], gl[r : r + 1, :], 0.0)
    gc1 = gc1.astype(bf16)
    gc2 = gc2.astype(bf16)
    for m in range(4):
        ka, kb = table_of(a_ref, m, shards)
        one = gc1[:, chunk * m : chunk * (m + 1)]
        two = gc2[:, chunk * m : chunk * (m + 1)]
        gu_all[:, 2 * HD * m : 2 * HD * (m + 1)] = jnp.concatenate(
            [dot_tn(one, ka), dot_tn(two, kb)], axis=1
        ).astype(bf16)
        change = jnp.concatenate(
            [
                dot(one, u_ref[:, 2 * HD * m : 2 * HD * m + HD]),
                dot(two, u_ref[:, 2 * HD * m + HD : 2 * HD * (m + 1)]),
            ],
            axis=1,
        ).astype(bf16)
        tables[m] = jnp.concatenate(
            [change[NSUB // 4 * n : NSUB // 4 * (n + 1), :] for n in range(4)], axis=1
        )
    size, quarter = b_ref.shape[1] // 2, b_ref.shape[2]
    for f in range(shards):
        gh[:, size * f : size * (f + 1)] = sum(
            dot_nt(gg_ref[:, quarter * t : quarter * (t + 1)], gate_part(b_ref, f * 4 + t))
            + dot_nt(gu_all[:, 2 * HD * t : 2 * HD * (t + 1)], a_ref[f * 4 + t, 0:size, :])
            for t in range(4)
        )
    upstream = gh[...]
    x = x_ref[...]
    gain = gain_ref[row : row + 1, :]
    factor, _ = rms(x, gain)
    dgain_ref[...] = jnp.sum(upstream * x * factor, axis=0, keepdims=True)
    gx = own_rows(g_ref, idx, plan, chunk) + rms_back(x, factor, gain, upstream)
    gx_ref[...] = gx
    go_ref[...] = gx.astype(bf16)
    for d, out in enumerate((b0, b1, b2, b3)):
        n = idx[plan.ti] ^ d
        out[:, 0 : 2 * HD] = gu_all[:, rows_at(n, 2 * HD)]
        out[:, 2 * HD : 10 * HD] = tables[n]


STEP_GROUPS = 4


def step_base(idx, step, pieces, per_piece):
    if pieces == 1:
        return step * STEP_GROUPS
    piece = step // per_piece
    return ((idx[0] ^ piece) * per_piece + step % per_piece) * STEP_GROUPS


def block_rows():
    return STEP_GROUPS * NSUB


def start_values(vs, layer, buffer, sems):
    copies = []
    for v in vs:
        for c in range(v.shape[1] // block_rows()):
            n = len(copies)
            copies.append(
                pltpu.make_async_copy(
                    v.at[layer, pl.ds(c * block_rows(), block_rows()), :],
                    buffer.at[pl.ds(n * block_rows(), block_rows()), :],
                    sems.at[n],
                )
            )
            copies[-1].start()
    return copies


def names_of(names_ref, src, layer):
    return names_ref[src, 32 + 16 * layer : 48 + 16 * layer, :].astype(f32)


def read_kernel(idx, w_ref, names_ref, *refs, plan, pieces, per_piece):
    vs = refs[:pieces]
    o0, o1, o2, o3, s_ref, partial, rows = refs[pieces:]
    step = pl.program_id(0)
    sources, _, width = w_ref.shape

    @pl.when(step == 0)
    def _():
        iota = lax.broadcasted_iota(jnp.int32, (NSUB, width), 0).astype(f32)

        def build(sa, carry):
            weights = sum(w_ref[plan.src(sa, ta)].astype(f32) for ta in range(4))
            for m in range(4):
                src = plan.src(sa, m)
                names = names_ref[src].astype(f32)
                dense = jnp.zeros((NSUB, width), f32)
                for b in range(8):
                    r = 8 * m + b
                    dense = jnp.where(iota == names[b : b + 1, :], weights[r : r + 1, :], dense)
                s_ref[src] = dense.T
            return carry

        lax.fori_loop(0, 4, build, 0)

    base = step_base(idx, step, pieces, per_piece)

    def multiply(v_ref):
        for k in range(STEP_GROUPS):
            at = rows_at(base + k, CAP)
            left = s_ref[:, at, :].reshape(sources * CAP, NSUB).astype(bf16)
            got = dot(left, v_ref[NSUB * k : NSUB * (k + 1), :])
            partial[:, at, :] = got.reshape(sources, CAP, v_ref.shape[1])

    for n in range(pieces):
        pl.when(step // per_piece == n)(functools.partial(multiply, vs[n]))

    @pl.when(step == pl.num_programs(0) - 1)
    def _():
        s, t = idx[plan.si], idx[plan.ti]
        tokens = rows.shape[0]
        chunk = tokens // 4
        outs = (o0, o1, o2, o3)
        iota = (lax.broadcasted_iota(jnp.int32, (tokens, width), 0) + 1).astype(f32)
        for ds in range(4):
            hits, parts = [], []
            for m in range(4):
                src = plan.src(s ^ ds, m)
                token = names_ref[src].astype(f32)[8:9, :]
                hits.append(jnp.where(iota == token, 1.0, 0.0).astype(bf16))
                parts.append(partial[src].astype(bf16))
            rows[...] = dot(
                jnp.concatenate(hits, axis=1), jnp.concatenate(parts, axis=0)
            ).astype(bf16)
            for dt in range(4):
                dp, dz = plan.rel(ds, dt)
                outs[dp][chunk * dz : chunk * (dz + 1), :] = rows[rows_at(t ^ dt, chunk), :]


def value_specs(values, layer):
    d_model = values[0].shape[2]
    per_piece = values[0].shape[1] // (STEP_GROUPS * NSUB)
    specs = []
    for n in range(len(values)):
        def index(g, n=n):
            return (layer, jnp.clip(g - n * per_piece, 0, per_piece - 1), 0)

        specs.append(pl.BlockSpec((None, STEP_GROUPS * NSUB, d_model), index))
    return specs, per_piece


def read_call(idx, weights, names, layer, values, plan, tokens):
    sources, _, width = weights.shape
    specs, per_piece = value_specs(values, layer)
    d_model = values[0].shape[2]
    out = shape((tokens, d_model), bf16)
    return pl.pallas_call(
        functools.partial(read_kernel, plan=plan, pieces=len(values), per_piece=per_piece),
        grid=(per_piece * len(values),),
        out_shape=[out, out, out, out, shape((sources, width, NSUB), f32)],
        in_specs=[
            pl.BlockSpec(memory_space=pltpu.SMEM),
            pl.BlockSpec((sources, 32, width), lambda g: (0, 0, 0)),
            pl.BlockSpec((sources, 16, width), lambda g: (0, 2 + layer, 0)),
        ]
        + specs,
        out_specs=[pl.BlockSpec((tokens, d_model), lambda g: (0, 0)) for _ in range(4)]
        + [pl.BlockSpec((sources, width, NSUB), lambda g: (0, 0, 0))],
        scratch_shapes=[
            pltpu.VMEM((sources, width, d_model), f32),
            pltpu.VMEM((tokens, d_model), bf16),
        ],
        compiler_params=pltpu.CompilerParams(vmem_limit_bytes=50 * MIB),
        cost_estimate=pl.CostEstimate(
            flops=4 * sources * width * NSUB * d_model, bytes_accessed=20 * MIB, transcendentals=0
        ),
        name="memory_read",
    )(idx, weights, names, *values)


def value_blocks(values):
    return sum(v.shape[1] for v in values) // block_rows()


def write_kernel(idx, g0, g1, g2, g3, names_ref, s_ref, *refs, plan, pieces, layer):
    vs, dvs = refs[:pieces], refs[pieces : 2 * pieces]
    gw_ref, grads, partial, cross, buffer, changes, sems, out_sems = refs[2 * pieces :]
    sources, width, _ = s_ref.shape
    d_model = buffer.shape[1]
    copies = start_values(vs, layer, buffer, sems)
    s, t = idx[plan.si], idx[plan.ti]
    tokens = grads.shape[1]
    chunk = tokens // 4
    for dp, g in enumerate((g0, g1, g2, g3)):
        for dz in range(4):
            ds, dt = plan.rel(dp, dz)
            grads[s ^ ds, rows_at(t ^ dt, chunk), :] = g[chunk * dz : chunk * (dz + 1), :]
    iota = (lax.broadcasted_iota(jnp.int32, (tokens, width), 0) + 1).astype(f32)
    for sa in range(4):
        hits = []
        for m in range(4):
            token = names_of(names_ref, plan.src(sa, m), layer)[8:9, :]
            hits.append(jnp.where(iota == token, 1.0, 0.0).astype(bf16))
        got = dot_tn(jnp.concatenate(hits, axis=1), grads[sa])
        for m in range(4):
            partial[plan.src(sa, m)] = got[width * m : width * (m + 1), :]
    leaving = []
    per_piece = len(copies) // pieces
    for step, copy in enumerate(copies):
        copy.wait()
        base = step_base(idx, step, pieces, per_piece)
        for k in range(STEP_GROUPS):
            at = rows_at(base + k, CAP)
            n = step * block_rows() + NSUB * k
            inbox = partial[:, at, :].reshape(sources * CAP, d_model).astype(bf16)
            left = s_ref[:, at, :].reshape(sources * CAP, NSUB).astype(bf16)
            changes[n : n + NSUB, :] = dot_tn(left, inbox).astype(bf16)
            cross[:, at, :] = dot_nt(inbox, buffer[n : n + NSUB, :]).reshape(sources, CAP, NSUB)
        leaving.append(
            pltpu.make_async_copy(
                changes.at[pl.ds(step * block_rows(), block_rows()), :],
                dvs[step // per_piece].at[pl.ds(step % per_piece * block_rows(), block_rows()), :],
                out_sems.at[step],
            )
        )
        leaving[-1].start()
    iota = lax.broadcasted_iota(jnp.int32, (NSUB, width), 0).astype(f32)

    def select(sa, carry):
        picked = []
        for m in range(4):
            src = plan.src(sa, m)
            turned = cross[src].T
            names = names_of(names_ref, src, layer)
            picked += [
                jnp.sum(jnp.where(iota == names[b : b + 1, :], turned, 0.0), axis=0, keepdims=True)
                for b in range(8)
            ]
        picked = jnp.concatenate(picked, axis=0).astype(bf16)
        for ta in range(4):
            gw_ref[plan.src(sa, ta)] = picked
        return carry

    lax.fori_loop(0, 4, select, 0)
    for copy in leaving:
        copy.wait()


def write_call(idx, grads, names, layer, dense, values, plan, tokens):
    sources, width, _ = dense.shape
    d_model = values[0].shape[2]
    pieces = len(values)
    blocks = value_blocks(values)
    whole = pltpu.VMEM((blocks * block_rows(), d_model), bf16)
    return pl.pallas_call(
        functools.partial(write_kernel, plan=plan, pieces=pieces, layer=layer),
        out_shape=[shape((v.shape[1], d_model), bf16) for v in values]
        + [shape((sources, 32, width), bf16)],
        in_specs=[pl.BlockSpec(memory_space=pltpu.SMEM)]
        + [pl.BlockSpec(memory_space=pltpu.VMEM)] * 6
        + [pl.BlockSpec(memory_space=pl.ANY)] * pieces,
        out_specs=[pl.BlockSpec(memory_space=pl.ANY)] * pieces
        + [pl.BlockSpec(memory_space=pltpu.VMEM)],
        scratch_shapes=[
            pltpu.VMEM((4, tokens, d_model), bf16),
            pltpu.VMEM((sources, width, d_model), f32),
            pltpu.VMEM((sources, width, NSUB), f32),
            whole,
            whole,
            pltpu.SemaphoreType.DMA((blocks,)),
            pltpu.SemaphoreType.DMA((blocks,)),
        ],
        compiler_params=pltpu.CompilerParams(vmem_limit_bytes=50 * MIB),
        cost_estimate=pl.CostEstimate(
            flops=6 * sources * width * NSUB * d_model, bytes_accessed=28 * MIB, transcendentals=0
        ),
        name="memory_write",
    )(idx, *grads, names, dense, *values)


def sum_kernel(idx, m0, r1, r2, r3, o0, o1, o2, o3):
    count = o0.shape[0]
    for dz, out in enumerate((o0, o1, o2, o3)):
        at = slice(count * dz, count * (dz + 1))
        out[...] = (
            (m0[at, :].astype(f32) + r1[at, :].astype(f32))
            + (r2[at, :].astype(f32) + r3[at, :].astype(f32))
        ).astype(bf16)


def table_grad_kernel(a_ref, b_ref, *refs):
    refs[-1][...] = a_ref[...].astype(f32) + b_ref[...].astype(f32)


def table_grad_call(mine, arrived, layer, layers, earlier):
    rows, d_model = mine.shape
    block = min(rows, 512)
    specs = [pl.BlockSpec((block, d_model), lambda g: (g, 0))] * 2
    args = [mine, arrived]
    if earlier is not None:
        specs = specs + [pl.BlockSpec(memory_space=pl.ANY)]
        args.append(earlier)
    return pl.pallas_call(
        table_grad_kernel,
        grid=(rows // block,),
        out_shape=shape((layers, rows, d_model), f32),
        in_specs=specs,
        out_specs=pl.BlockSpec((None, block, d_model), lambda g: (layer, g, 0)),
        input_output_aliases={} if earlier is None else {2: 0},
        compiler_params=pltpu.CompilerParams(vmem_limit_bytes=32 * MIB),
        cost_estimate=pl.CostEstimate(flops=0, bytes_accessed=16 * MIB, transcendentals=0),
        name="table_grad",
    )(*args)


def gather_shards(x, axis):
    if lax.axis_size("fsdp") != 2:
        return lax.all_gather(x, "fsdp", axis=axis, tiled=True)
    other = swap(x, "fsdp", 1)
    mine = lax.axis_index("fsdp") == 0
    return jnp.where(
        mine, jnp.concatenate([x, other], axis=axis), jnp.concatenate([other, x], axis=axis)
    )


def shard_pieces(x, axis):
    if lax.axis_size("fsdp") != 2:
        return [lax.all_gather(x, "fsdp", axis=axis, tiled=True)]
    return [x, swap(x, "fsdp", 1)]


def reduce_packs(group):
    scattered = [lax.psum_scatter(p, "fsdp", scatter_dimension=0, tiled=False) for p in group]
    return [lax.psum(p, "ctx") for p in scattered]


def after(xs, *others):
    return list(lax.optimization_barrier((tuple(xs), tuple(others)))[0])


def body(
    inputs,
    query_weight,
    key_weight,
    value_weight,
    attention_weight,
    lookup_weight,
    gate_weight,
    memory_weight,
    first_table,
    second_table,
    attention_gain,
    memory_gain,
    memory_values,
    blocks,
    first_picks,
    second_picks,
    cotangent,
):
    plan = PLAN
    SA, TA = plan.SA, plan.TA
    layers = query_weight.shape[0]
    tokens = inputs.shape[1]
    d_model = inputs.shape[2]
    chunk = tokens // 4
    width = query_weight.shape[2]
    shards = lax.axis_size("fsdp")
    owners = lax.axis_size("ctx") * lax.axis_size("tp")
    groups = memory_values.shape[1] // NSUB
    lanes = shards * groups * CAP
    gbits = groups.bit_length() - 1
    dbits = owners.bit_length() - 1
    idx = jnp.stack(
        [lax.axis_index("fsdp"), lax.axis_index("ctx"), lax.axis_index("tp"), 0]
    ).astype(jnp.int32)

    gains = gather_shards(
        jnp.concatenate([attention_gain, memory_gain], axis=0).astype(bf16), 1
    ).astype(f32)

    def qkv_weight(l, queries, keys, values_):
        joined = jnp.concatenate([queries[l], keys[l], values_[l]], axis=1).astype(bf16)
        return shard_pieces(joined, 0)

    def gather_all(x):
        return lax.all_gather(x, ("fsdp", "tp"), axis=0, tiled=False)

    w_qkv = [qkv_weight(0, query_weight, key_weight, value_weight)]
    w_o, w_a, w_b = [], [], []

    firsts = jnp.swapaxes(first_picks[:, 0, 0], 1, 2)
    seconds = jnp.swapaxes(second_picks[:, 0, 0].reshape(layers, tokens, -1), 1, 2)
    height = layers * (8 + seconds.shape[1])
    name_box, *tables = kernel_call(
        functools.partial(slots_kernel, plan=plan, gbits=gbits, dbits=dbits),
        "pick_slots",
        [shape((owners, 16 * layers, lanes), bf16)] + [shape((height, chunk), jnp.int32)] * 4,
        idx,
        [firsts, seconds],
        [pltpu.VMEM((4, height, chunk), jnp.int32)],
    )
    w_qkv[0][-1], name_box, *tables = after([w_qkv[0][-1], name_box, *tables])
    ids_row = blocks
    ids_col = blocks.reshape(-1, 1)
    heads_shape = shape((tokens * 3 // 2, 2 * HD), bf16)
    folded = shape((tokens // 2, 2 * HD), bf16)
    part_shape = shape((chunk, d_model), bf16)
    chunk_shape = shape((chunk, d_model), f32)
    full_shape = shape((tokens, d_model), bf16)
    gain_shape = shape((1, d_model), f32)
    box_shape = shape((chunk, 2 * d_model), bf16)
    chunk_scratch = pltpu.VMEM((chunk, d_model), bf16)
    pack_scratch = pltpu.VMEM((4, tokens * 3 // 2, 2 * HD), bf16)
    part_scratch = pltpu.VMEM((tokens, d_model), bf16)
    kv_scratch = [
        pltpu.VMEM((4 * tokens, HD), bf16),
        pltpu.VMEM((4 * tokens, HD), bf16),
        pltpu.VMEM((4 * tokens, 1), jnp.int32),
    ]
    x = inputs[0]
    h_chunk = names = table = None
    h_chunks = []
    kept = []
    for l in range(layers):
        if l == 0:
            h1, *es = kernel_call(
                functools.partial(qkv_first_kernel, plan=plan, row=l),
                "qkv_first",
                [full_shape] + [heads_shape] * 4,
                idx,
                [x, gains, *w_qkv[l]],
                [pack_scratch],
            )
            qw, kw, vw, ow, lw, gw_, pw, ta_, tb_, mv = after(
                (
                    query_weight, key_weight, value_weight, attention_weight, lookup_weight,
                    gate_weight, memory_weight, first_table, second_table, memory_values,
                ),
                es[0],
            )
            a_boxes, b_boxes = [], []
            for n in range(layers):
                w_o.append(shard_pieces(ow[n].astype(bf16), 1))
                a_boxes.append(
                    jnp.concatenate(
                        [lw[n], jnp.concatenate([ta_[n, 0], tb_[n, 0]], axis=1)], axis=0
                    ).astype(bf16)
                )
                b_boxes.append(jnp.concatenate([gw_[n], to_pack(pw[n])], axis=0).astype(bf16))
                if n > 0:
                    w_qkv.append(qkv_weight(n, qw, kw, vw))
            w_a.append(gather_all(a_boxes[0]))
        else:
            h1, *es = kernel_call(
                functools.partial(qkv_kernel, plan=plan),
                "qkv",
                [full_shape] + [heads_shape] * 4,
                idx,
                [*h_chunks, *w_qkv[l]],
                [pack_scratch],
            )
        es = swaps(es, SA)
        if l == 0:
            (table,) = kernel_call(
                functools.partial(pick_table_kernel, plan=plan),
                "pick_table",
                [shape((layers, height // layers, tokens), jnp.int32)],
                idx,
                swaps(tables, TA),
                [pltpu.VMEM((4, height, chunk), jnp.int32)],
            )
            if shards == 2:
                values = [memory_values, swap(mv, "fsdp", 1)]
            else:
                values = [lax.all_gather(mv, "fsdp", axis=1, tiled=True)]
        else:
            w_a.append(gather_all(after([a_boxes[l]], h1)[0]))
        heads = kernel_call(
            functools.partial(attend_kernel, plan=plan),
            "attend",
            [folded] * 4,
            idx,
            [*es, ids_row, ids_col],
            kv_scratch,
        )
        heads = swaps(heads, SA)
        if l == 0:
            heads[3], table = after([heads[3], table])
        attended, *parts = kernel_call(
            functools.partial(out_kernel, plan=plan),
            "attend_out",
            [shape((tokens, width), bf16)] + [part_shape] * 4,
            idx,
            [*heads, *w_o[l]],
            [pltpu.VMEM((4, tokens, HD), bf16), part_scratch],
        )
        parts = swaps(parts, TA)
        middle, h2, u, w, outbox = kernel_call(
            functools.partial(lookup_kernel, plan=plan, row=layers + l, layer=l, shards=shards),
            "lookup",
            [
                chunk_shape,
                part_shape,
                shape((chunk, 8 * HD), bf16),
                shape((32, tokens), f32),
                shape((owners, 32 if l else 32 + name_box.shape[1], lanes), bf16),
            ],
            idx,
            [x, *parts, gains, w_a[l], table] + ([] if l else [name_box]),
        )
        weights = lax.all_to_all(outbox, ("ctx", "tp"), 0, 0, tiled=True)
        if l == 0:
            names = weights
        w_b.append(gather_all(after([b_boxes[l]], h2)[0]))
        (gate,) = kernel_call(
            functools.partial(gate_values_kernel, shards=shards),
            "gate_values",
            [chunk_shape],
            idx,
            [h2, w_b[l]],
        )
        *reads, dense = read_call(idx, weights, names, l, values, plan, tokens)
        reads = swaps(reads, "ctx")
        sums = kernel_call(sum_kernel, "memory_sum", [part_shape] * 4, idx, reads)
        sums = swaps(sums, "tp")
        if l + 1 < layers:
            mem, box, x3, h_chunk = kernel_call(
                functools.partial(gate_kernel, row=l + 1, shards=shards),
                "gate",
                [chunk_shape, box_shape, chunk_shape, part_shape],
                idx,
                [*sums, gate, w_b[l], middle, h2, gains],
                [chunk_scratch],
            )
            h_chunks = spread(h_chunk, TA)
        else:
            mem = x3 = None
            gn, box, back_box = kernel_call(
                functools.partial(gate_last_kernel, plan=plan, shards=shards),
                "gate_last",
                [part_shape, box_shape, box_shape],
                idx,
                [*sums, gate, w_b[l], middle, h2, cotangent[0]],
                [
                    pltpu.VMEM((chunk, d_model), f32),
                    chunk_scratch,
                    pltpu.VMEM((chunk, d_model), f32),
                    chunk_scratch,
                ],
            )
        kept.append((x, h1, es, attended, middle, u, w, gate, dense, mem, box))
        x = x3

    g = cotangent[0]
    packs = [None] * layers
    gain_rows = [None] * (2 * layers)
    table_grads = None
    table_list = [None] * layers
    output = dvs_above = None
    for l in reversed(range(layers)):
        x, h1, es, attended, middle, u, w, gate, dense, mem, box = kept[l]
        top = l == layers - 1
        line = jnp.concatenate(spread(gn, "tp"), axis=0)
        planes = spread(line, "ctx")
        if not top and shards == 2:
            table_grads = table_grad_call(*dvs_above, l + 1, layers, table_grads)
            planes[3], table_grads = after([planes[3], table_grads])
        *dvs, gw = write_call(idx, planes, names, l, dense, values, plan, tokens)
        if shards == 2:
            dvs_above = [dvs[0], swap(dvs[1], "fsdp", 1)]
        else:
            table_list[l] = lax.psum_scatter(dvs[0], "fsdp", scatter_dimension=0, tiled=True).astype(f32)
        if not top:
            back_all = lax.all_gather(after([back_box], line)[0], TA, axis=0, tiled=False)
            gw, back_all = after([gw, back_all])
        gw = lax.all_to_all(gw, ("ctx", "tp"), 0, 0, tiled=True)
        back_shape = shape((chunk, 10 * HD), bf16)
        g_mid, go_chunk, gain_rows[layers + l], *back = kernel_call(
            functools.partial(lookup_back_kernel, plan=plan, row=layers + l, layer=l, shards=shards),
            "lookup_back",
            [chunk_shape, part_shape, gain_shape] + [back_shape] * 4,
            idx,
            [gw, table, w, w_a[l], u, back_box, w_b[l], middle, g, gains],
            [
                pltpu.VMEM(w.shape, f32),
                pltpu.VMEM(u.shape, bf16),
                pltpu.VMEM((4, NSUB // 4, 8 * HD), bf16),
                pltpu.VMEM((chunk, d_model), f32),
            ],
        )
        go_chunks = spread(go_chunk, TA)
        if l == 0 and shards == 2:
            table_grads = table_grad_call(*dvs_above, l, layers, table_grads)
            go_chunks[3], table_grads = after([go_chunks[3], table_grads])
        go, *ups = kernel_call(
            functools.partial(out_back_kernel, plan=plan),
            "attend_out_back",
            [full_shape] + [folded] * 4,
            idx,
            [*go_chunks, *w_o[l]],
            [pltpu.VMEM((4, tokens // 2, 2 * HD), bf16)],
        )
        ups = swaps(ups, SA)
        back = swaps(back, TA)
        ups[3], *back = after([ups[3], *back])
        shard_size = d_model // shards
        head_grads = kernel_call(
            functools.partial(attend_back_kernel, plan=plan),
            "attend_back",
            [heads_shape] * 4,
            idx,
            [*es, *ups, ids_row, ids_col],
            kv_scratch + [pltpu.VMEM((4 * tokens, HD), f32)] * 2,
        )
        head_grads = swaps(head_grads, SA)
        if top:
            forward_all = lax.all_gather(after([box], line)[0], TA, axis=0, tiled=False)
            below_all = lax.all_gather(after([kept[l - 1][10]], line)[0], TA, axis=0, tiled=False)
        else:
            forward_all = below_all
        if top:
            back_all = lax.all_gather(after([back_box], line)[0], TA, axis=0, tiled=False)
        if top:
            output = back_all[:, :, d_model:].reshape(tokens, d_model)
        riders = [] if l else [inputs[0], *gain_rows[1:]]
        g_qkv, *parts = kernel_call(
            functools.partial(qkv_back_kernel, plan=plan, row=l, gain_rows=len(riders)),
            "qkv_back",
            [shape((tokens, 3 * width), bf16)] + [part_shape if l else shape((chunk + 16, d_model), bf16)] * 4,
            idx,
            [*head_grads, *w_qkv[l], *riders],
            [pack_scratch, part_scratch],
        )
        parts = swaps(parts, TA)
        qkv_rows = 3 * shard_size
        weight_rows = shard_size * 7 // 2 + NSUB // shards // 2
        weight_scratch = [
            pltpu.VMEM((shards, weight_rows, 256), bf16),
            pltpu.VMEM((tokens, d_model), bf16),
            pltpu.VMEM((tokens, width), bf16),
            pltpu.VMEM((tokens, width), bf16),
            pltpu.VMEM((tokens, 2 * HD), bf16),
            pltpu.VMEM((tokens, d_model), bf16),
        ]
        qkv_scratch = [pltpu.VMEM((shards, qkv_rows, 256), bf16)]
        split = l == 0 and shards == 2
        weight_outs = [shape((weight_rows, 256), bf16)] * 2 if split else [shape((shards, weight_rows, 256), bf16)]
        qkv_outs = [shape((qkv_rows, 256), bf16)] * 2 if split else [shape((shards, qkv_rows, 256), bf16)]
        qkv_packs = kernel_call(
            qkv_grad_kernel, "qkv_grad", qkv_outs, idx, [h1, g_qkv], qkv_scratch
        )
        weight_packs = kernel_call(
            functools.partial(weight_grad_kernel, plan=plan, has_full=top),
            "weight_grad",
            weight_outs,
            idx,
            [forward_all, back_all, *back, attended, go] + ([cotangent[0]] if top else []),
            weight_scratch,
        )
        if split:
            quarter = shape((qkv_rows // 4, 256), bf16)
            qkv_quarters = kernel_call(
                add_two_kernel, "qkv_add", [quarter] * 4, idx, [qkv_packs[0], swap(qkv_packs[1], "fsdp", 1)]
            )
            quarter = shape((weight_rows // 4, 256), bf16)
            weight_quarters = kernel_call(
                add_two_kernel,
                "weight_add",
                [quarter] * 4,
                idx,
                [weight_packs[0], swap(weight_packs[1], "fsdp", 1)],
            )
            weight_quarters = swaps(weight_quarters, "ctx")
            parts[3], *weight_quarters = after([parts[3], *weight_quarters])
        else:
            parts[3], weight_packs[0], qkv_packs[0], below_all = after(
                [parts[3], weight_packs[0], qkv_packs[0], below_all]
            )
            packs[l] = reduce_packs([weight_packs[0], qkv_packs[0]])
        if l > 0:
            below = kept[l - 1]
            g, gain_rows[l], gn, back_box = kernel_call(
                functools.partial(norm_back_kernel, plan=plan, row=l, shards=shards),
                "norm_back",
                [chunk_shape, gain_shape, part_shape, box_shape],
                idx,
                [*parts, x, g_mid, gains, w_b[l - 1], below[7], below[9]],
                [chunk_scratch],
            )
        else:
            g, gain_all, *gain_halves = kernel_call(
                functools.partial(norm_back_last_kernel, plan=plan, row=l),
                "norm_back_last",
                [part_shape, shape((16, d_model), f32), shape((16, 256), bf16), shape((16, 256), bf16)],
                idx,
                [*parts, x, g_mid, gains],
            )
    (input_gradient,) = kernel_call(
        functools.partial(place_kernel, plan=plan),
        "input_gradient",
        [shape((tokens, d_model), f32)],
        idx,
        spread(g, TA),
    )
    if shards != 2:
        table_grads = jnp.stack(table_list)
    gain_shapes = []
    if shards == 2:
        rows = (weight_rows + qkv_rows) // 4
        (part,) = kernel_call(
            plane_sum_kernel,
            "plane_sum",
            [shape((rows + 16, 256), bf16)],
            idx,
            [*weight_quarters, *swaps(qkv_quarters, "ctx"), gain_halves[0], swap(gain_halves[1], "fsdp", 1)],
        )
        part, *packs[1] = after([part, *packs[1]])
        late = spread(part, "ctx")
        gain_shapes = [shape((layers, d_model // 2), f32)] * 2
        flat = late + [p for l in range(1, layers) for p in packs[l]]
    else:
        gain_all = lax.psum(
            lax.psum_scatter(gain_all[: 2 * layers], "fsdp", scatter_dimension=1, tiled=True), "ctx"
        )
        flat = [p for l in range(layers) for p in packs[l]]
    shard_size = d_model // shards
    tall = shape((layers, shard_size, width), f32)
    wide = shape((layers, width, shard_size), f32)
    sub = shape((layers, 1, HD, NSUB // shards), f32)
    grads = kernel_call(
        functools.partial(finalize_kernel, layers=layers, late=shards == 2),
        "finalize",
        [tall, tall, tall, wide, shape((layers, shard_size, 2 * HD), f32), tall, wide, sub, sub]
        + gain_shapes,
        idx,
        flat,
        [pltpu.VMEM((weight_rows, 256), bf16), pltpu.VMEM((qkv_rows, 256), bf16)] if shards == 2 else [],
    )
    gain_grads = grads[9:] if shards == 2 else [gain_all[:layers], gain_all[layers:]]
    return (
        output[None],
        input_gradient[None],
        *grads[:7],
        *[jnp.swapaxes(t, 2, 3) for t in grads[7:9]],
        *gain_grads,
        table_grads,
    )


def solution(mesh):
    placed = (
        P("fsdp", "ctx", None),
        P(None, "fsdp", "tp"),
        P(None, "fsdp", "tp"),
        P(None, "fsdp", "tp"),
        P(None, "tp", "fsdp"),
        P(None, "fsdp", "tp"),
        P(None, "fsdp", "tp"),
        P(None, "tp", "fsdp"),
        P(None, "tp", "fsdp", None),
        P(None, "tp", "fsdp", None),
        P(None, "fsdp"),
        P(None, "fsdp"),
        P(None, ("fsdp", "ctx", "tp"), None),
        P("fsdp", None),
        P(None, "fsdp", "tp", "ctx", None),
        P(None, "fsdp", "tp", "ctx", None, None),
        P("fsdp", "ctx", None),
    )
    return jax.shard_map(
        body,
        mesh=mesh,
        in_specs=placed,
        out_specs=(
            P("fsdp", "ctx", None),
            P("fsdp", "ctx", None),
            P(None, "fsdp", "tp"),
            P(None, "fsdp", "tp"),
            P(None, "fsdp", "tp"),
            P(None, "tp", "fsdp"),
            P(None, "fsdp", "tp"),
            P(None, "fsdp", "tp"),
            P(None, "tp", "fsdp"),
            P(None, "tp", "fsdp", None),
            P(None, "tp", "fsdp", None),
            P(None, "fsdp"),
            P(None, "fsdp"),
            P(None, ("fsdp", "ctx", "tp"), None),
        ),
        check_vma=False,
    )
```

```python
import functools

import jax
import jax.numpy as jnp
from jax import lax
from jax.experimental import pallas as pl
from jax.experimental.pallas import tpu as pltpu
from jax.sharding import PartitionSpec as P

HD = 64
NSUB = 256
CAP = 8
EPS = 1e-05
NEG = -1e30
f32 = jnp.float32
bf16 = jnp.bfloat16
MIB = 1 << 20


def dot(a, b):
    return jnp.dot(a, b, preferred_element_type=f32)


def dot_nt(a, b):
    return lax.dot_general(a, b, (((1,), (1,)), ((), ())), preferred_element_type=f32)


def dot_tn(a, b):
    return lax.dot_general(a, b, (((0,), (0,)), ((), ())), preferred_element_type=f32)


def swap(x, axis, step):
    size = lax.axis_size(axis)
    return lax.ppermute(x, axis, [(i, i ^ step) for i in range(size)])


def swaps(xs, axis):
    return [xs[0]] + [swap(xs[d], axis, d) for d in range(1, len(xs))]


def spread(x, axis):
    return [x] + [swap(x, axis, d) for d in range(1, lax.axis_size(axis))]


def shape(dims, dtype):
    return jax.ShapeDtypeStruct(dims, dtype)


def kernel_call(body, name, outs, idx, args, scratch=(), limit=50, flops=0):
    limit = {'norm_back_last': 16, 'plane_sum': 16, 'input_gradient': 16, 'finalize': 24, 'weight_add': 16, 'qkv_add': 16}.get(name, limit)
    in_specs = [pl.BlockSpec(memory_space=pltpu.SMEM)]
    in_specs += [pl.BlockSpec(memory_space=pltpu.VMEM) for _ in args]
    moved = sum(a.size * a.dtype.itemsize for a in args)
    moved += sum(o.size * o.dtype.itemsize for o in outs)
    out = pl.pallas_call(
        body,
        out_shape=outs,
        in_specs=in_specs,
        out_specs=[pl.BlockSpec(memory_space=pltpu.VMEM) for _ in outs],
        scratch_shapes=list(scratch),
        compiler_params=pltpu.CompilerParams(vmem_limit_bytes=limit * MIB),
        cost_estimate=pl.CostEstimate(flops=flops, bytes_accessed=moved, transcendentals=0),
        name=name,
    )(idx, *args)
    return list(out)


def rows_at(index, count):
    return pl.ds(pl.multiple_of(index * count, count), count)


def rms(x, gain):
    factor = lax.rsqrt(jnp.mean(x * x, axis=1, keepdims=True) + EPS)
    return factor, x * factor * gain


def rms_back(x, factor, gain, upstream):
    scaled = upstream * gain
    return factor * scaled - x * factor**3 * jnp.mean(scaled * x, axis=1, keepdims=True)


def total4(refs):
    return (refs[0][...].astype(f32) + refs[1][...].astype(f32)) + (
        refs[2][...].astype(f32) + refs[3][...].astype(f32)
    )


def fold(x):
    half = x.shape[0] // 2
    return jnp.concatenate([x[:half], x[half:]], axis=1)


def unfold(x):
    half = x.shape[1] // 2
    return jnp.concatenate([x[:, :half], x[:, half:]], axis=0)


class Plan:
    def __init__(self, SA, TA):
        self.SA, self.TA = SA, TA
        self.si = 1 if SA == "ctx" else 2
        self.ti = 1 if TA == "ctx" else 2

    def src(self, sa, ta):
        return sa * 4 + ta if self.SA == "ctx" else ta * 4 + sa

    def rel(self, ds, dt):
        return (ds, dt) if self.SA == "ctx" else (dt, ds)


PLAN = Plan("ctx", "tp")


def slots_kernel(idx, first_ref, second_ref, out_ref, t0, t1, t2, t3, table, plan, gbits, dbits):
    layers, picks, tokens = first_ref.shape
    inner = second_ref.shape[1]
    owners, _, width = out_ref.shape
    lanes = owners * width
    chunk = tokens // 4
    iota = lax.broadcasted_iota(jnp.int32, (NSUB, tokens), 0)
    before = lax.broadcasted_iota(jnp.int32, (tokens, tokens), 0) < lax.broadcasted_iota(
        jnp.int32, (tokens, tokens), 1
    )
    before = jnp.where(before, 1.0, 0.0).astype(bf16)
    row = lax.broadcasted_iota(jnp.int32, (lanes, tokens), 0)
    token_row = (lax.broadcasted_iota(jnp.int32, (8, tokens), 1) + 1).astype(f32)
    token_row = jnp.where(
        lax.broadcasted_iota(jnp.int32, (8, tokens), 0) == 0, token_row, 0.0
    )
    for l in range(layers):
        onehot = jnp.zeros((NSUB, tokens), f32)
        for i in range(picks):
            onehot = jnp.where(iota == first_ref[l, i : i + 1, :], 1.0, onehot)
        counts = dot(onehot.astype(bf16), before)
        total = jnp.zeros((16, lanes), f32)
        slots = []
        for i in range(picks):
            first = first_ref[l, i : i + 1, :]
            rank = jnp.sum(jnp.where(iota == first, counts, 0.0), axis=0, keepdims=True)
            shard = lax.shift_right_logical(first, gbits)
            group = lax.shift_right_logical(shard, dbits) * (1 << gbits) + (first & ((1 << gbits) - 1))
            slot = (shard & ((1 << dbits) - 1)) * width + group * CAP + rank.astype(jnp.int32)
            slots.append(slot)
            names = jnp.concatenate(
                [second_ref[l, 8 * i : 8 * i + 8, :].astype(f32), token_row], axis=0
            )
            hit = jnp.where(row == slot, 1.0, 0.0).astype(bf16)
            total = total + dot_nt(names.astype(bf16), hit)
        for d in range(owners):
            out_ref[d, 16 * l : 16 * l + 16, :] = total[:, d * width : (d + 1) * width].astype(bf16)
        both = jnp.concatenate([first_ref[l], jnp.concatenate(slots, axis=0)], axis=0)
        for n in range(4):
            cut = slice(n * chunk, (n + 1) * chunk)
            at = l * (8 + inner)
            table[n, at : at + 8, :] = both[:, cut]
            table[n, at + 8 : at + 8 + inner, :] = second_ref[l, :, cut]
    for d, out in enumerate((t0, t1, t2, t3)):
        out[...] = table[idx[plan.ti] ^ d]


def pick_table_kernel(idx, t0, t1, t2, t3, out_ref, table, plan):
    for d, t in enumerate((t0, t1, t2, t3)):
        table[idx[plan.ti] ^ d] = t[...]
    rows = out_ref.shape[1]
    for l in range(out_ref.shape[0]):
        out_ref[l] = jnp.concatenate([table[n, rows * l : rows * (l + 1), :] for n in range(4)], axis=1)


def head_mask(shape_, lanes_each):
    return lax.broadcasted_iota(jnp.int32, shape_, 1) // lanes_each


def place_chunks(refs, full, t):
    count = refs[0].shape[0]
    for d in range(4):
        full[rows_at(t ^ d, count), :] = refs[d][...]


def emit_chunks(part, outs, t):
    count = outs[0].shape[0]
    for d in range(4):
        outs[d][...] = part[rows_at(t ^ d, count), :]


def piece_at(f, j, pieces, size):
    return rows_at(f ^ j, size) if len(pieces) > 1 else slice(0, size)


def emit_heads(h_ref, pieces, pack, outs, idx, plan):
    width = pieces[0].shape[1] // 3
    size = pieces[0].shape[0]
    qkv = sum(
        dot(h_ref[:, piece_at(idx[0], j, pieces, size)], w[...]) for j, w in enumerate(pieces)
    ).astype(bf16)
    for j in range(4):
        q = qkv[:, HD * j : HD * (j + 1)]
        k = qkv[:, width + HD * j : width + HD * (j + 1)]
        v = qkv[:, 2 * width + HD * j : 2 * width + HD * (j + 1)]
        pack[j] = jnp.concatenate([jnp.concatenate([q, k], axis=1), fold(v)], axis=0)
    for d in range(4):
        outs[d][...] = pack[idx[plan.si] ^ d]


def qkv_first_kernel(idx, x_ref, gain_ref, *refs, plan, row):
    *pieces, h_ref, e0, e1, e2, e3, pack = refs
    _, normed = rms(x_ref[...].astype(f32), gain_ref[row : row + 1, :])
    h_ref[...] = normed.astype(bf16)
    emit_heads(h_ref, pieces, pack, (e0, e1, e2, e3), idx, plan)


def qkv_kernel(idx, h0, h1, h2, h3, *refs, plan):
    *pieces, h_ref, e0, e1, e2, e3, pack = refs
    place_chunks((h0, h1, h2, h3), h_ref, idx[plan.ti])
    emit_heads(h_ref, pieces, pack, (e0, e1, e2, e3), idx, plan)


def load_heads(es, kk, vv):
    for d in range(4):
        rows = es[d].shape[0] * 2 // 3
        kk[rows * d : rows * (d + 1), :] = es[d][0:rows, HD : 2 * HD]
        vv[rows * d : rows * (d + 1), :] = unfold(es[d][rows:, :])


def load_ids(col_ref, ids_col, s):
    count = col_ref.shape[0] // 4
    for d in range(4):
        ids_col[count * d : count * (d + 1), :] = col_ref[rows_at(s ^ d, count), :]


def probabilities(kk, q, key_ids, query_ids):
    scores = dot_nt(kk, q) * (HD ** (-0.5))
    scores = jnp.where(key_ids <= query_ids, scores, NEG)
    top = jnp.max(scores, axis=0, keepdims=True)
    exponent = jnp.exp(scores - top)
    return exponent * (1.0 / jnp.sum(exponent, axis=0, keepdims=True))


def attend_kernel(idx, e0, e1, e2, e3, row_ref, col_ref, a0, a1, a2, a3, kk, vv, ids_col, plan):
    es, outs = (e0, e1, e2, e3), (a0, a1, a2, a3)
    s = idx[plan.si]
    load_heads(es, kk, vv)
    load_ids(col_ref, ids_col, s)
    count = kk.shape[0] // 4
    for d in range(4):
        query_ids = row_ref[:, rows_at(s ^ d, count)]
        p = probabilities(kk[...], es[d][0:count, 0:HD], ids_col[...], query_ids)
        blended = dot_tn(vv[...], p.astype(bf16))
        outs[d][...] = fold(blended.T.astype(bf16))


def attend_back_kernel(
    idx, e0, e1, e2, e3, u0, u1, u2, u3, row_ref, col_ref, g0, g1, g2, g3, kk, vv, ids_col, gk, gv, plan
):
    es, us, outs = (e0, e1, e2, e3), (u0, u1, u2, u3), (g0, g1, g2, g3)
    s = idx[plan.si]
    load_heads(es, kk, vv)
    load_ids(col_ref, ids_col, s)
    count = kk.shape[0] // 4
    scale = HD ** (-0.5)
    for d in range(4):
        query_ids = row_ref[:, rows_at(s ^ d, count)]
        q = es[d][0:count, 0:HD]
        up = unfold(us[d][...])
        p = probabilities(kk[...], q, ids_col[...], query_ids)
        gp = dot_nt(vv[...], up)
        centre = jnp.sum(p * gp, axis=0, keepdims=True)
        gs = (p * (gp - centre)).astype(bf16)
        gq = (dot_tn(kk[...], gs) * scale).T.astype(bf16)
        outs[d][0:count, 0:HD] = gq
        key_term = dot(gs, q)
        value_term = dot(p.astype(bf16), up)
        if d == 0:
            gk[...] = key_term
            gv[...] = value_term
        else:
            gk[...] += key_term
            gv[...] += value_term
    for d in range(4):
        outs[d][0:count, HD : 2 * HD] = (gk[count * d : count * (d + 1), :] * scale).astype(bf16)
        outs[d][count:, :] = fold(gv[count * d : count * (d + 1), :].astype(bf16))


def out_kernel(idx, a0, a1, a2, a3, *refs, plan):
    *pieces, a_ref, p0, p1, p2, p3, heads, part = refs
    for d, a in enumerate((a0, a1, a2, a3)):
        heads[idx[plan.si] ^ d] = unfold(a[...])
    a_ref[...] = jnp.concatenate([heads[j] for j in range(4)], axis=1)
    size = pieces[0].shape[1]
    for j, w in enumerate(pieces):
        part[:, piece_at(idx[0], j, pieces, size)] = dot(a_ref[...], w[...]).astype(bf16)
    emit_chunks(part, (p0, p1, p2, p3), idx[plan.ti])


def out_back_kernel(idx, g0, g1, g2, g3, *refs, plan):
    *pieces, go_ref, u0, u1, u2, u3, pack = refs
    place_chunks((g0, g1, g2, g3), go_ref, idx[plan.ti])
    size = pieces[0].shape[1]
    up = sum(
        dot_nt(go_ref[:, piece_at(idx[0], j, pieces, size)], w[...]) for j, w in enumerate(pieces)
    ).astype(bf16)
    for j in range(4):
        pack[j] = fold(up[:, HD * j : HD * (j + 1)])
    for d, u in enumerate((u0, u1, u2, u3)):
        u[...] = pack[idx[plan.si] ^ d]


def qkv_back_kernel(idx, g0, g1, g2, g3, *refs, plan, row=None, gain_rows=0):
    *ins, g_ref, p0, p1, p2, p3, pack, part = refs
    x_ref, *rows_refs = ins[len(ins) - gain_rows :] if gain_rows else [None]
    pieces = ins[: len(ins) - gain_rows]
    for d, g in enumerate((g0, g1, g2, g3)):
        pack[idx[plan.si] ^ d] = g[...]
    rows = g_ref.shape[0]
    columns = [pack[j, 0:rows, 0:HD] for j in range(4)]
    columns += [pack[j, 0:rows, HD : 2 * HD] for j in range(4)]
    columns += [unfold(pack[j, rows:, :]) for j in range(4)]
    g_ref[...] = jnp.concatenate(columns, axis=1)
    size = pieces[0].shape[0]
    if not gain_rows:
        for j, w in enumerate(pieces):
            part[:, piece_at(idx[0], j, pieces, size)] = dot_nt(g_ref[...], w[...]).astype(bf16)
        emit_chunks(part, (p0, p1, p2, p3), idx[plan.ti])
        return
    x = x_ref[...].astype(f32)
    factor = lax.rsqrt(jnp.mean(x * x, axis=1, keepdims=True) + EPS)
    count = part.shape[0] // 4
    for j, w in enumerate(pieces):
        at = piece_at(idx[0], j, pieces, size)
        term = dot_nt(g_ref[...], w[...])
        part[:, at] = term.astype(bf16)
        change = jnp.sum(term * (x_ref[:, at].astype(f32) * factor), axis=0, keepdims=True)
        p0[count : count + 1, at] = change.astype(bf16)
    blank = jnp.zeros((p0.shape[0] - count - gain_rows, p0.shape[1]), f32)
    tail = [p0[count : count + 1, :].astype(f32)] + [r[...] for r in rows_refs] + [blank]
    tail = jnp.concatenate(tail, axis=0).astype(bf16)
    for d, out in enumerate((p0, p1, p2, p3)):
        out[0:count, :] = part[rows_at(idx[plan.ti] ^ d, count), :]
        out[count:, :] = tail


def to_pack(x):
    rows, width = x.shape
    if width >= 256:
        return jnp.concatenate([x[:, 256 * i : 256 * (i + 1)] for i in range(width // 256)], axis=0)
    fold_by = 256 // width
    rows = rows // fold_by
    return jnp.concatenate([x[rows * i : rows * (i + 1)] for i in range(fold_by)], axis=1)


def from_pack(p, rows, width):
    if width >= 256:
        return jnp.concatenate([p[rows * i : rows * (i + 1)] for i in range(width // 256)], axis=1)
    return jnp.concatenate([p[:, width * i : width * (i + 1)] for i in range(256 // width)], axis=0)


def shard_rows(x, f, shards):
    size = x.shape[0] // shards
    return x[size * f : size * (f + 1)]


def shard_columns(x, f, shards):
    size = x.shape[1] // shards
    return x[:, size * f : size * (f + 1)]


def emit_shards(pack, outs, idx):
    if len(outs) == 1:
        outs[0][...] = pack[...]
    else:
        outs[0][...] = pack[idx[0]]
        outs[1][...] = pack[idx[0] ^ 1]


def qkv_grad_kernel(idx, h_ref, g_ref, *refs):
    *outs, pack = refs
    shards = pack.shape[0]
    change = dot_tn(h_ref[...], g_ref[...])
    for f in range(shards):
        pack[f] = to_pack(shard_rows(change, f, shards)).astype(bf16)
    emit_shards(pack, outs, idx)


def weight_grad_kernel(idx, *refs, plan, has_full):
    forward, back, near, (a_ref, go_ref) = refs[0], refs[1], refs[2:6], refs[6:8]
    full = refs[8] if has_full else None
    *outs, pack, h, z, gg, gu, gy = refs[8 + has_full :]
    chunk = forward.shape[1]
    d_model = h.shape[1]
    quarter = z.shape[1]
    shards = pack.shape[0]
    tables = jnp.zeros((NSUB, 2 * HD), f32)
    mine = rows_at(idx[plan.ti], quarter)
    for d in range(4):
        at = slice(chunk * d, chunk * (d + 1))
        h[at, :] = forward[d, :, 0:d_model]
        z[at, :] = forward.at[:, :, d_model:][d, :, mine]
        gg[at, :] = back.at[:, :, 0:d_model][d, :, mine]
        gu[rows_at(idx[plan.ti] ^ d, chunk), :] = near[d][:, 0 : 2 * HD]
        folded = near[d][:, 2 * HD :].astype(f32)
        tables = tables + jnp.concatenate(
            [folded[:, 2 * HD * i : 2 * HD * (i + 1)] for i in range(4)], axis=0
        )
        gy[at, :] = full[at, :] if has_full else back[d, :, d_model:]
    gate_change = dot_tn(h[...], gg[...])
    look_change = dot_tn(h[...], gu[...])
    mem_change = dot_tn(z[...], gy[...])
    out_change = dot_tn(a_ref[...], go_ref[...])
    for f in range(shards):
        pack[f] = jnp.concatenate(
            [
                to_pack(shard_rows(gate_change, f, shards)),
                to_pack(shard_columns(mem_change, f, shards)),
                to_pack(shard_rows(look_change, f, shards)),
                to_pack(shard_rows(tables, f, shards)),
                to_pack(shard_columns(out_change, f, shards)),
            ],
            axis=0,
        ).astype(bf16)
    emit_shards(pack, outs, idx)


def finalize_kernel(idx, *refs, layers, late):
    count = 2 * layers + 2 * late
    ins, outs = refs[:count], refs[count:]
    q_ref, k_ref, v_ref, o_ref, look_ref, gate_ref, mem_ref, first_ref, second_ref = outs[:9]
    part = q_ref.shape[1]
    for l in range(layers):
        if l > 0 or not late:
            memory, qkv = ins[2 * l + 2 * late], ins[2 * l + 2 * late + 1]
        else:
            one_ref, two_ref, memory, qkv = outs[9:]
            rows, more = memory.shape[0] // 4, qkv.shape[0] // 4
            total = 0.0
            for d in range(4):
                memory[rows_at(idx[1] ^ d, rows), :] = ins[d][0:rows, :]
                qkv[rows_at(idx[1] ^ d, more), :] = ins[d][rows : rows + more, :]
                total = total + ins[d][rows + more :, :].astype(f32)
            total = jnp.concatenate([total[0:8], total[8:16]], axis=1)
            one_ref[...] = total[0:layers]
            two_ref[...] = total[layers : 2 * layers]
        for n, ref in enumerate((q_ref, k_ref, v_ref)):
            ref[l] = qkv[part * n : part * (n + 1), :].astype(f32)
        gate_ref[l] = memory[0:part, :].astype(f32)
        mem_ref[l] = from_pack(memory[part : 2 * part, :], mem_ref.shape[1], mem_ref.shape[2]).astype(f32)
        at = 2 * part + part // 2
        look_ref[l] = from_pack(memory[2 * part : at, :].astype(f32), part, look_ref.shape[2])
        rows = first_ref.shape[3]
        tables = from_pack(memory[at : at + rows // 2, :].astype(f32), rows, 2 * HD)
        first_ref[l, 0] = tables[:, :HD].T
        second_ref[l, 0] = tables[:, HD:].T
        at = at + rows // 2
        o_ref[l] = from_pack(memory[at : at + part, :], o_ref.shape[1], o_ref.shape[2]).astype(f32)


def add_two_kernel(idx, a, b, o0, o1, o2, o3):
    chunk = o0.shape[0]
    for d, out in enumerate((o0, o1, o2, o3)):
        at = rows_at(idx[1] ^ d, chunk)
        out[...] = (a[at, :].astype(f32) + b[at, :].astype(f32)).astype(bf16)


def plane_sum_kernel(idx, *refs):
    a, b, (g0, g1, out) = refs[0:4], refs[4:8], refs[8:]
    rows = a[0].shape[0]
    more = rows + b[0].shape[0]
    out[0:rows, :] = total4(a).astype(bf16)
    out[rows:more, :] = total4(b).astype(bf16)
    out[more:, :] = (g0[...].astype(f32) + g1[...].astype(f32)).astype(bf16)


def own_rows(ref, idx, plan, count):
    if ref.shape[0] == count:
        return ref[...].astype(f32)
    return ref[rows_at(idx[plan.ti], count), :].astype(f32)


def table_of(a_ref, m, shards):
    size = a_ref.shape[1] * 4 // 5
    both = [a_ref[f * 4 + m, size:, :] for f in range(shards)]
    both = both[0] if shards == 1 else jnp.concatenate(both, axis=0)
    return both[:, :HD], both[:, HD:]


def only_head(x, m, chunk):
    lane = lax.broadcasted_iota(jnp.int32, x.shape, 1)
    return jnp.where((lane >= m * chunk) & (lane < (m + 1) * chunk), x, 0.0)


def lookup_kernel(
    idx, x_ref, p0, r1, r2, r3, gain_ref, a_ref, pick_ref, *refs, plan, row, layer, shards
):
    *names_ref, x_out, h_ref, u_ref, w_ref, out_ref = refs
    chunk = p0.shape[0]
    x = own_rows(x_ref, idx, plan, chunk) + total4((p0, r1, r2, r3))
    x_out[...] = x
    _, normed = rms(x, gain_ref[row : row + 1, :])
    h_ref[...] = normed.astype(bf16)
    size = a_ref.shape[1] * 4 // 5
    c1, c2 = [], []
    for m in range(4):
        u = sum(
            dot(h_ref[:, size * f : size * (f + 1)], a_ref[f * 4 + m, 0:size, :]) for f in range(shards)
        ).astype(bf16)
        u_ref[:, 2 * HD * m : 2 * HD * (m + 1)] = u
        ka, kb = table_of(a_ref, m, shards)
        c1.append(dot_nt(ka, u[:, :HD]))
        c2.append(dot_nt(kb, u[:, HD:]))
    c1 = jnp.concatenate(c1, axis=1)
    c2 = jnp.concatenate(c2, axis=1)
    lanes = c1.shape[1]
    iota = lax.broadcasted_iota(jnp.int32, (NSUB, lanes), 0)
    for i in range(4):
        first = pick_ref[layer, i : i + 1, :]
        base = jnp.sum(jnp.where(iota == first, c1, 0.0), axis=0, keepdims=True)
        for b in range(8):
            r = i * 8 + b
            second = pick_ref[layer, 8 + r : 9 + r, :]
            picked = jnp.sum(jnp.where(iota == second, c2, 0.0), axis=0, keepdims=True)
            w_ref[r : r + 1, :] = base + picked
    logits = w_ref[...]
    exponent = jnp.exp(logits - jnp.max(logits, axis=0, keepdims=True))
    w = exponent * (1.0 / jnp.sum(exponent, axis=0, keepdims=True))
    w_ref[...] = w
    owners, _, width = out_ref.shape
    slots = lax.broadcasted_iota(jnp.int32, (owners * width, lanes), 0)
    total = jnp.zeros((32, owners * width), f32)
    for i in range(4):
        hit = jnp.where(slots == pick_ref[layer, 4 + i : 5 + i, :], 1.0, 0.0).astype(bf16)
        mine = w[8 * i : 8 * (i + 1), :]
        split = jnp.concatenate([only_head(mine, m, chunk) for m in range(4)], axis=0)
        total = total + dot_nt(split.astype(bf16), hit)
    for d in range(owners):
        out_ref[d, 0:32, :] = total[:, d * width : (d + 1) * width].astype(bf16)
        if names_ref:
            out_ref[d, 32:, :] = names_ref[0][d]


def gate_part(b_ref, n):
    return b_ref[n, 0 : b_ref.shape[1] // 2, :]


def memory_part(b_ref, n):
    size = b_ref.shape[1] // 2
    return from_pack(b_ref[n, size:, :], b_ref.shape[2], size)


def gate_values_kernel(idx, h_ref, b_ref, gate_ref, shards):
    size, quarter = b_ref.shape[1] // 2, b_ref.shape[2]
    for t in range(4):
        gate_ref[:, quarter * t : quarter * (t + 1)] = sum(
            dot(h_ref[:, size * f : size * (f + 1)], gate_part(b_ref, f * 4 + t)) for f in range(shards)
        )


def gate_sum(sums, gate_ref, b_ref, x_ref, mem_ref, z_ref, x_out, shards):
    mem = total4(sums)
    mem_ref[...] = mem
    gate = gate_ref[...]
    z_ref[...] = (mem * (gate * jax.nn.sigmoid(gate))).astype(bf16)
    size, quarter = b_ref.shape[1] // 2, b_ref.shape[2]
    for f in range(shards):
        at = slice(size * f, size * (f + 1))
        x_out[:, at] = x_ref[:, at] + sum(
            dot(z_ref[:, quarter * t : quarter * (t + 1)], memory_part(b_ref, f * 4 + t)) for t in range(4)
        )


def gate_kernel(
    idx, s0, s1, s2, s3, gate_ref, b_ref, x_ref, h_ref, gain_ref, mem_ref, box_ref, x_out, h_out, z, row, shards
):
    gate_sum((s0, s1, s2, s3), gate_ref, b_ref, x_ref, mem_ref, z, x_out, shards)
    h_out[...] = rms(x_out[...], gain_ref[row : row + 1, :])[1].astype(bf16)
    fill_box(box_ref, h_ref, z)


def fill_box(box_ref, left_ref, right_ref):
    width = left_ref.shape[1]
    box_ref[:, 0:width] = left_ref[...]
    box_ref[:, width:] = right_ref[...]


def gate_last_kernel(
    idx, s0, s1, s2, s3, gate_ref, b_ref, x_ref, h_ref, g_ref,
    n_ref, box_ref, back_ref, mem, z, x_out, gy, plan, shards,
):
    gate_sum((s0, s1, s2, s3), gate_ref, b_ref, x_ref, mem, z, x_out, shards)
    gy[...] = g_ref[rows_at(idx[plan.ti], gy.shape[0]), :]
    gate_back(gy, b_ref, gate_ref, mem, n_ref, back_ref, shards)
    back_ref[:, gy.shape[1] :] = x_out[...].astype(bf16)
    fill_box(box_ref, h_ref, z)


def gate_back(gy_ref, b_ref, gate_ref, mem_ref, gn_ref, gg_ref, shards):
    size, quarter = b_ref.shape[1] // 2, b_ref.shape[2]
    for t in range(4):
        at = slice(quarter * t, quarter * (t + 1))
        gz = sum(
            dot_nt(gy_ref[:, size * f : size * (f + 1)], memory_part(b_ref, f * 4 + t)) for f in range(shards)
        )
        gate = gate_ref[:, at]
        sigmoid = jax.nn.sigmoid(gate)
        gn_ref[:, at] = (gz * (gate * sigmoid)).astype(bf16)
        slope = sigmoid * (1.0 + gate * (1.0 - sigmoid))
        gg_ref[:, at] = (gz * mem_ref[:, at] * slope).astype(bf16)


def norm_back(idx, parts, x_ref, g_ref, gain_ref, dgain_ref, plan, row):
    count = parts[0].shape[0]
    upstream = total4(parts)
    x = own_rows(x_ref, idx, plan, count)
    gain = gain_ref[row : row + 1, :]
    factor, _ = rms(x, gain)
    dgain_ref[...] = jnp.sum(upstream * x * factor, axis=0, keepdims=True)
    return g_ref[...] + rms_back(x, factor, gain, upstream)


def norm_back_kernel(
    idx, p0, r1, r2, r3, x_ref, g_ref, gain_ref, b_ref, gate_ref, mem_ref,
    gx_ref, dgain_ref, gn_ref, back_ref, gy, plan, row, shards,
):
    gx = norm_back(idx, (p0, r1, r2, r3), x_ref, g_ref, gain_ref, dgain_ref, plan, row)
    gx_ref[...] = gx
    gy[...] = gx.astype(bf16)
    gate_back(gy, b_ref, gate_ref, mem_ref, gn_ref, back_ref, shards)
    back_ref[:, gy.shape[1] :] = gy[...]


def norm_back_last_kernel(
    idx, p0, r1, r2, r3, x_ref, g_ref, gain_ref, out_ref, all_ref, mine_ref, other_ref, plan, row
):
    count = out_ref.shape[0]
    refs = (p0, r1, r2, r3)
    upstream = total4([r.at[0:count] for r in refs])
    x = own_rows(x_ref, idx, plan, count)
    factor, _ = rms(x, gain_ref[row : row + 1, :])
    gx = g_ref[...] + rms_back(x, factor, gain_ref[row : row + 1, :], upstream)
    out_ref[...] = gx.astype(bf16)
    all_ref[...] = total4([r.at[count:] for r in refs])
    size = all_ref.shape[1] // 2
    for j, out in enumerate((mine_ref, other_ref)):
        half = all_ref[:, rows_at(idx[0] ^ j, size)]
        out[...] = jnp.concatenate([half[:8, 0:256], half[:8, 256:]], axis=0).astype(bf16)


def place_kernel(idx, c0, c1, c2, c3, out_ref, plan):
    chunk = c0.shape[0]
    for d, c in enumerate((c0, c1, c2, c3)):
        out_ref[rows_at(idx[plan.ti] ^ d, chunk), :] = c[...].astype(out_ref.dtype)


def lookup_back_kernel(
    idx, gw_ref, pick_ref, w_ref, a_ref, u_ref, gg_ref, b_ref, x_ref, g_ref, gain_ref,
    gx_ref, go_ref, dgain_ref, b0, b1, b2, b3, gl, gu_all, tables, gh, plan, row, layer, shards,
):
    chunk = u_ref.shape[0]
    owners, _, width = gw_ref.shape
    lanes = w_ref.shape[1]
    slots = lax.broadcasted_iota(jnp.int32, (owners * width, lanes), 0)
    arrived = jnp.concatenate([gw_ref[d] for d in range(owners)], axis=1)
    for i in range(4):
        hit = jnp.where(slots == pick_ref[layer, 4 + i : 5 + i, :], 1.0, 0.0).astype(bf16)
        mixed = dot(arrived, hit)
        gl[8 * i : 8 * (i + 1), :] = sum(
            only_head(mixed[8 * m : 8 * (m + 1), :], m, chunk) for m in range(4)
        )
    w = w_ref[...]
    gw = gl[...]
    gl[...] = w * (gw - jnp.sum(w * gw, axis=0, keepdims=True))
    iota = lax.broadcasted_iota(jnp.int32, (NSUB, lanes), 0)
    gc1 = jnp.zeros((NSUB, lanes), f32)
    gc2 = jnp.zeros((NSUB, lanes), f32)
    for i in range(4):
        both = jnp.sum(gl[8 * i : 8 * (i + 1), :], axis=0, keepdims=True)
        gc1 = jnp.where(iota == pick_ref[layer, i : i + 1, :], both, gc1)
        for b in range(8):
            r = i * 8 + b
            gc2 = gc2 + jnp.where(iota == pick_ref[layer, 8 + r : 9 + r, :], gl[r : r + 1, :], 0.0)
    gc1 = gc1.astype(bf16)
    gc2 = gc2.astype(bf16)
    for m in range(4):
        ka, kb = table_of(a_ref, m, shards)
        one = gc1[:, chunk * m : chunk * (m + 1)]
        two = gc2[:, chunk * m : chunk * (m + 1)]
        gu_all[:, 2 * HD * m : 2 * HD * (m + 1)] = jnp.concatenate(
            [dot_tn(one, ka), dot_tn(two, kb)], axis=1
        ).astype(bf16)
        change = jnp.concatenate(
            [
                dot(one, u_ref[:, 2 * HD * m : 2 * HD * m + HD]),
                dot(two, u_ref[:, 2 * HD * m + HD : 2 * HD * (m + 1)]),
            ],
            axis=1,
        ).astype(bf16)
        tables[m] = jnp.concatenate(
            [change[NSUB // 4 * n : NSUB // 4 * (n + 1), :] for n in range(4)], axis=1
        )
    size, quarter = b_ref.shape[1] // 2, b_ref.shape[2]
    for f in range(shards):
        gh[:, size * f : size * (f + 1)] = sum(
            dot_nt(gg_ref[:, quarter * t : quarter * (t + 1)], gate_part(b_ref, f * 4 + t))
            + dot_nt(gu_all[:, 2 * HD * t : 2 * HD * (t + 1)], a_ref[f * 4 + t, 0:size, :])
            for t in range(4)
        )
    upstream = gh[...]
    x = x_ref[...]
    gain = gain_ref[row : row + 1, :]
    factor, _ = rms(x, gain)
    dgain_ref[...] = jnp.sum(upstream * x * factor, axis=0, keepdims=True)
    gx = own_rows(g_ref, idx, plan, chunk) + rms_back(x, factor, gain, upstream)
    gx_ref[...] = gx
    go_ref[...] = gx.astype(bf16)
    for d, out in enumerate((b0, b1, b2, b3)):
        n = idx[plan.ti] ^ d
        out[:, 0 : 2 * HD] = gu_all[:, rows_at(n, 2 * HD)]
        out[:, 2 * HD : 10 * HD] = tables[n]


STEP_GROUPS = 4


def step_base(idx, step, pieces, per_piece):
    if pieces == 1:
        return step * STEP_GROUPS
    piece = step // per_piece
    return ((idx[0] ^ piece) * per_piece + step % per_piece) * STEP_GROUPS


def block_rows():
    return STEP_GROUPS * NSUB


def start_values(vs, layer, buffer, sems):
    copies = []
    for v in vs:
        for c in range(v.shape[1] // block_rows()):
            n = len(copies)
            copies.append(
                pltpu.make_async_copy(
                    v.at[layer, pl.ds(c * block_rows(), block_rows()), :],
                    buffer.at[pl.ds(n * block_rows(), block_rows()), :],
                    sems.at[n],
                )
            )
            copies[-1].start()
    return copies


def names_of(names_ref, src, layer):
    return names_ref[src, 32 + 16 * layer : 48 + 16 * layer, :].astype(f32)


def read_kernel(idx, w_ref, names_ref, *refs, plan, pieces, per_piece):
    vs = refs[:pieces]
    o0, o1, o2, o3, s_ref, partial, rows = refs[pieces:]
    step = pl.program_id(0)
    sources, _, width = w_ref.shape

    @pl.when(step == 0)
    def _():
        iota = lax.broadcasted_iota(jnp.int32, (NSUB, width), 0).astype(f32)

        def build(sa, carry):
            weights = sum(w_ref[plan.src(sa, ta)].astype(f32) for ta in range(4))
            for m in range(4):
                src = plan.src(sa, m)
                names = names_ref[src].astype(f32)
                dense = jnp.zeros((NSUB, width), f32)
                for b in range(8):
                    r = 8 * m + b
                    dense = jnp.where(iota == names[b : b + 1, :], weights[r : r + 1, :], dense)
                s_ref[src] = dense.T
            return carry

        lax.fori_loop(0, 4, build, 0)

    base = step_base(idx, step, pieces, per_piece)

    def multiply(v_ref):
        for k in range(STEP_GROUPS):
            at = rows_at(base + k, CAP)
            left = s_ref[:, at, :].reshape(sources * CAP, NSUB).astype(bf16)
            got = dot(left, v_ref[NSUB * k : NSUB * (k + 1), :])
            partial[:, at, :] = got.reshape(sources, CAP, v_ref.shape[1])

    for n in range(pieces):
        pl.when(step // per_piece == n)(functools.partial(multiply, vs[n]))

    @pl.when(step == pl.num_programs(0) - 1)
    def _():
        s, t = idx[plan.si], idx[plan.ti]
        tokens = rows.shape[0]
        chunk = tokens // 4
        outs = (o0, o1, o2, o3)
        iota = (lax.broadcasted_iota(jnp.int32, (tokens, width), 0) + 1).astype(f32)
        for ds in range(4):
            hits, parts = [], []
            for m in range(4):
                src = plan.src(s ^ ds, m)
                token = names_ref[src].astype(f32)[8:9, :]
                hits.append(jnp.where(iota == token, 1.0, 0.0).astype(bf16))
                parts.append(partial[src].astype(bf16))
            rows[...] = dot(
                jnp.concatenate(hits, axis=1), jnp.concatenate(parts, axis=0)
            ).astype(bf16)
            for dt in range(4):
                dp, dz = plan.rel(ds, dt)
                outs[dp][chunk * dz : chunk * (dz + 1), :] = rows[rows_at(t ^ dt, chunk), :]


def value_specs(values, layer):
    d_model = values[0].shape[2]
    per_piece = values[0].shape[1] // (STEP_GROUPS * NSUB)
    specs = []
    for n in range(len(values)):
        def index(g, n=n):
            return (layer, jnp.clip(g - n * per_piece, 0, per_piece - 1), 0)

        specs.append(pl.BlockSpec((None, STEP_GROUPS * NSUB, d_model), index))
    return specs, per_piece


def read_call(idx, weights, names, layer, values, plan, tokens):
    sources, _, width = weights.shape
    specs, per_piece = value_specs(values, layer)
    d_model = values[0].shape[2]
    out = shape((tokens, d_model), bf16)
    return pl.pallas_call(
        functools.partial(read_kernel, plan=plan, pieces=len(values), per_piece=per_piece),
        grid=(per_piece * len(values),),
        out_shape=[out, out, out, out, shape((sources, width, NSUB), f32)],
        in_specs=[
            pl.BlockSpec(memory_space=pltpu.SMEM),
            pl.BlockSpec((sources, 32, width), lambda g: (0, 0, 0)),
            pl.BlockSpec((sources, 16, width), lambda g: (0, 2 + layer, 0)),
        ]
        + specs,
        out_specs=[pl.BlockSpec((tokens, d_model), lambda g: (0, 0)) for _ in range(4)]
        + [pl.BlockSpec((sources, width, NSUB), lambda g: (0, 0, 0))],
        scratch_shapes=[
            pltpu.VMEM((sources, width, d_model), f32),
            pltpu.VMEM((tokens, d_model), bf16),
        ],
        compiler_params=pltpu.CompilerParams(vmem_limit_bytes=50 * MIB),
        cost_estimate=pl.CostEstimate(
            flops=4 * sources * width * NSUB * d_model, bytes_accessed=20 * MIB, transcendentals=0
        ),
        name="memory_read",
    )(idx, weights, names, *values)


def value_blocks(values):
    return sum(v.shape[1] for v in values) // block_rows()


def write_kernel(idx, g0, g1, g2, g3, names_ref, s_ref, *refs, plan, pieces, layer):
    vs, dvs = refs[:pieces], refs[pieces : 2 * pieces]
    gw_ref, grads, partial, cross, buffer, changes, sems, out_sems = refs[2 * pieces :]
    sources, width, _ = s_ref.shape
    d_model = buffer.shape[1]
    copies = start_values(vs, layer, buffer, sems)
    s, t = idx[plan.si], idx[plan.ti]
    tokens = grads.shape[1]
    chunk = tokens // 4
    for dp, g in enumerate((g0, g1, g2, g3)):
        for dz in range(4):
            ds, dt = plan.rel(dp, dz)
            grads[s ^ ds, rows_at(t ^ dt, chunk), :] = g[chunk * dz : chunk * (dz + 1), :]
    iota = (lax.broadcasted_iota(jnp.int32, (tokens, width), 0) + 1).astype(f32)
    for sa in range(4):
        hits = []
        for m in range(4):
            token = names_of(names_ref, plan.src(sa, m), layer)[8:9, :]
            hits.append(jnp.where(iota == token, 1.0, 0.0).astype(bf16))
        got = dot_tn(jnp.concatenate(hits, axis=1), grads[sa])
        for m in range(4):
            partial[plan.src(sa, m)] = got[width * m : width * (m + 1), :]
    leaving = []
    per_piece = len(copies) // pieces
    for step, copy in enumerate(copies):
        copy.wait()
        base = step_base(idx, step, pieces, per_piece)
        for k in range(STEP_GROUPS):
            at = rows_at(base + k, CAP)
            n = step * block_rows() + NSUB * k
            inbox = partial[:, at, :].reshape(sources * CAP, d_model).astype(bf16)
            left = s_ref[:, at, :].reshape(sources * CAP, NSUB).astype(bf16)
            changes[n : n + NSUB, :] = dot_tn(left, inbox).astype(bf16)
            cross[:, at, :] = dot_nt(inbox, buffer[n : n + NSUB, :]).reshape(sources, CAP, NSUB)
        leaving.append(
            pltpu.make_async_copy(
                changes.at[pl.ds(step * block_rows(), block_rows()), :],
                dvs[step // per_piece].at[pl.ds(step % per_piece * block_rows(), block_rows()), :],
                out_sems.at[step],
            )
        )
        leaving[-1].start()
    iota = lax.broadcasted_iota(jnp.int32, (NSUB, width), 0).astype(f32)

    def select(sa, carry):
        picked = []
        for m in range(4):
            src = plan.src(sa, m)
            turned = cross[src].T
            names = names_of(names_ref, src, layer)
            picked += [
                jnp.sum(jnp.where(iota == names[b : b + 1, :], turned, 0.0), axis=0, keepdims=True)
                for b in range(8)
            ]
        picked = jnp.concatenate(picked, axis=0).astype(bf16)
        for ta in range(4):
            gw_ref[plan.src(sa, ta)] = picked
        return carry

    lax.fori_loop(0, 4, select, 0)
    for copy in leaving:
        copy.wait()


def write_call(idx, grads, names, layer, dense, values, plan, tokens):
    sources, width, _ = dense.shape
    d_model = values[0].shape[2]
    pieces = len(values)
    blocks = value_blocks(values)
    whole = pltpu.VMEM((blocks * block_rows(), d_model), bf16)
    return pl.pallas_call(
        functools.partial(write_kernel, plan=plan, pieces=pieces, layer=layer),
        out_shape=[shape((v.shape[1], d_model), bf16) for v in values]
        + [shape((sources, 32, width), bf16)],
        in_specs=[pl.BlockSpec(memory_space=pltpu.SMEM)]
        + [pl.BlockSpec(memory_space=pltpu.VMEM)] * 6
        + [pl.BlockSpec(memory_space=pl.ANY)] * pieces,
        out_specs=[pl.BlockSpec(memory_space=pl.ANY)] * pieces
        + [pl.BlockSpec(memory_space=pltpu.VMEM)],
        scratch_shapes=[
            pltpu.VMEM((4, tokens, d_model), bf16),
            pltpu.VMEM((sources, width, d_model), f32),
            pltpu.VMEM((sources, width, NSUB), f32),
            whole,
            whole,
            pltpu.SemaphoreType.DMA((blocks,)),
            pltpu.SemaphoreType.DMA((blocks,)),
        ],
        compiler_params=pltpu.CompilerParams(vmem_limit_bytes=50 * MIB),
        cost_estimate=pl.CostEstimate(
            flops=6 * sources * width * NSUB * d_model, bytes_accessed=28 * MIB, transcendentals=0
        ),
        name="memory_write",
    )(idx, *grads, names, dense, *values)


def sum_kernel(idx, m0, r1, r2, r3, o0, o1, o2, o3):
    count = o0.shape[0]
    for dz, out in enumerate((o0, o1, o2, o3)):
        at = slice(count * dz, count * (dz + 1))
        out[...] = (
            (m0[at, :].astype(f32) + r1[at, :].astype(f32))
            + (r2[at, :].astype(f32) + r3[at, :].astype(f32))
        ).astype(bf16)


def table_grad_kernel(a_ref, b_ref, *refs):
    refs[-1][...] = a_ref[...].astype(f32) + b_ref[...].astype(f32)


def table_grad_call(mine, arrived, layer, layers, earlier):
    rows, d_model = mine.shape
    block = min(rows, 1024)
    specs = [pl.BlockSpec((block, d_model), lambda g: (g, 0))] * 2
    args = [mine, arrived]
    if earlier is not None:
        specs = specs + [pl.BlockSpec(memory_space=pl.ANY)]
        args.append(earlier)
    return pl.pallas_call(
        table_grad_kernel,
        grid=(rows // block,),
        out_shape=shape((layers, rows, d_model), f32),
        in_specs=specs,
        out_specs=pl.BlockSpec((None, block, d_model), lambda g: (layer, g, 0)),
        input_output_aliases={} if earlier is None else {2: 0},
        compiler_params=pltpu.CompilerParams(vmem_limit_bytes=50 * MIB),
        cost_estimate=pl.CostEstimate(flops=0, bytes_accessed=16 * MIB, transcendentals=0),
        name="table_grad",
    )(*args)


def gather_shards(x, axis):
    if lax.axis_size("fsdp") != 2:
        return lax.all_gather(x, "fsdp", axis=axis, tiled=True)
    other = swap(x, "fsdp", 1)
    mine = lax.axis_index("fsdp") == 0
    return jnp.where(
        mine, jnp.concatenate([x, other], axis=axis), jnp.concatenate([other, x], axis=axis)
    )


def shard_pieces(x, axis):
    if lax.axis_size("fsdp") != 2:
        return [lax.all_gather(x, "fsdp", axis=axis, tiled=True)]
    return [x, swap(x, "fsdp", 1)]


def reduce_packs(group):
    scattered = [lax.psum_scatter(p, "fsdp", scatter_dimension=0, tiled=False) for p in group]
    return [lax.psum(p, "ctx") for p in scattered]


def after(xs, *others):
    return list(lax.optimization_barrier((tuple(xs), tuple(others)))[0])


def body(
    inputs,
    query_weight,
    key_weight,
    value_weight,
    attention_weight,
    lookup_weight,
    gate_weight,
    memory_weight,
    first_table,
    second_table,
    attention_gain,
    memory_gain,
    memory_values,
    blocks,
    first_picks,
    second_picks,
    cotangent,
):
    plan = PLAN
    SA, TA = plan.SA, plan.TA
    layers = query_weight.shape[0]
    tokens = inputs.shape[1]
    d_model = inputs.shape[2]
    chunk = tokens // 4
    width = query_weight.shape[2]
    shards = lax.axis_size("fsdp")
    owners = lax.axis_size("ctx") * lax.axis_size("tp")
    groups = memory_values.shape[1] // NSUB
    lanes = shards * groups * CAP
    gbits = groups.bit_length() - 1
    dbits = owners.bit_length() - 1
    idx = jnp.stack(
        [lax.axis_index("fsdp"), lax.axis_index("ctx"), lax.axis_index("tp"), 0]
    ).astype(jnp.int32)

    gains = gather_shards(
        jnp.concatenate([attention_gain, memory_gain], axis=0).astype(bf16), 1
    ).astype(f32)

    def qkv_weight(l, queries, keys, values_):
        joined = jnp.concatenate([queries[l], keys[l], values_[l]], axis=1).astype(bf16)
        return shard_pieces(joined, 0)

    def gather_all(x):
        return lax.all_gather(x, ("fsdp", "tp"), axis=0, tiled=False)

    w_qkv = [qkv_weight(0, query_weight, key_weight, value_weight)]
    w_o, w_a, w_b = [], [], []

    firsts = jnp.swapaxes(first_picks[:, 0, 0], 1, 2)
    seconds = jnp.swapaxes(second_picks[:, 0, 0].reshape(layers, tokens, -1), 1, 2)
    height = layers * (8 + seconds.shape[1])
    name_box, *tables = kernel_call(
        functools.partial(slots_kernel, plan=plan, gbits=gbits, dbits=dbits),
        "pick_slots",
        [shape((owners, 16 * layers, lanes), bf16)] + [shape((height, chunk), jnp.int32)] * 4,
        idx,
        [firsts, seconds],
        [pltpu.VMEM((4, height, chunk), jnp.int32)],
    )
    w_qkv[0][-1], name_box, *tables = after([w_qkv[0][-1], name_box, *tables])
    ids_row = blocks
    ids_col = blocks.reshape(-1, 1)
    heads_shape = shape((tokens * 3 // 2, 2 * HD), bf16)
    folded = shape((tokens // 2, 2 * HD), bf16)
    part_shape = shape((chunk, d_model), bf16)
    chunk_shape = shape((chunk, d_model), f32)
    full_shape = shape((tokens, d_model), bf16)
    gain_shape = shape((1, d_model), f32)
    box_shape = shape((chunk, 2 * d_model), bf16)
    chunk_scratch = pltpu.VMEM((chunk, d_model), bf16)
    pack_scratch = pltpu.VMEM((4, tokens * 3 // 2, 2 * HD), bf16)
    part_scratch = pltpu.VMEM((tokens, d_model), bf16)
    kv_scratch = [
        pltpu.VMEM((4 * tokens, HD), bf16),
        pltpu.VMEM((4 * tokens, HD), bf16),
        pltpu.VMEM((4 * tokens, 1), jnp.int32),
    ]
    x = inputs[0]
    h_chunk = names = table = None
    h_chunks = []
    kept = []
    for l in range(layers):
        if l == 0:
            h1, *es = kernel_call(
                functools.partial(qkv_first_kernel, plan=plan, row=l),
                "qkv_first",
                [full_shape] + [heads_shape] * 4,
                idx,
                [x, gains, *w_qkv[l]],
                [pack_scratch],
            )
            qw, kw, vw, ow, lw, gw_, pw, ta_, tb_, mv = after(
                (
                    query_weight, key_weight, value_weight, attention_weight, lookup_weight,
                    gate_weight, memory_weight, first_table, second_table, memory_values,
                ),
                es[0],
            )
            a_boxes, b_boxes = [], []
            for n in range(layers):
                w_o.append(shard_pieces(ow[n].astype(bf16), 1))
                a_boxes.append(
                    jnp.concatenate(
                        [lw[n], jnp.concatenate([ta_[n, 0], tb_[n, 0]], axis=1)], axis=0
                    ).astype(bf16)
                )
                b_boxes.append(jnp.concatenate([gw_[n], to_pack(pw[n])], axis=0).astype(bf16))
                if n > 0:
                    w_qkv.append(qkv_weight(n, qw, kw, vw))
            w_a.append(gather_all(a_boxes[0]))
        else:
            h1, *es = kernel_call(
                functools.partial(qkv_kernel, plan=plan),
                "qkv",
                [full_shape] + [heads_shape] * 4,
                idx,
                [*h_chunks, *w_qkv[l]],
                [pack_scratch],
            )
        es = swaps(es, SA)
        if l == 0:
            (table,) = kernel_call(
                functools.partial(pick_table_kernel, plan=plan),
                "pick_table",
                [shape((layers, height // layers, tokens), jnp.int32)],
                idx,
                swaps(tables, TA),
                [pltpu.VMEM((4, height, chunk), jnp.int32)],
            )
            if shards == 2:
                values = [memory_values, swap(mv, "fsdp", 1)]
            else:
                values = [lax.all_gather(mv, "fsdp", axis=1, tiled=True)]
        else:
            w_a.append(gather_all(after([a_boxes[l]], h1)[0]))
        heads = kernel_call(
            functools.partial(attend_kernel, plan=plan),
            "attend",
            [folded] * 4,
            idx,
            [*es, ids_row, ids_col],
            kv_scratch,
        )
        heads = swaps(heads, SA)
        if l == 0:
            heads[3], table = after([heads[3], table])
        attended, *parts = kernel_call(
            functools.partial(out_kernel, plan=plan),
            "attend_out",
            [shape((tokens, width), bf16)] + [part_shape] * 4,
            idx,
            [*heads, *w_o[l]],
            [pltpu.VMEM((4, tokens, HD), bf16), part_scratch],
        )
        parts = swaps(parts, TA)
        middle, h2, u, w, outbox = kernel_call(
            functools.partial(lookup_kernel, plan=plan, row=layers + l, layer=l, shards=shards),
            "lookup",
            [
                chunk_shape,
                part_shape,
                shape((chunk, 8 * HD), bf16),
                shape((32, tokens), f32),
                shape((owners, 32 if l else 32 + name_box.shape[1], lanes), bf16),
            ],
            idx,
            [x, *parts, gains, w_a[l], table] + ([] if l else [name_box]),
        )
        weights = lax.all_to_all(outbox, ("ctx", "tp"), 0, 0, tiled=True)
        if l == 0:
            names = weights
        w_b.append(gather_all(after([b_boxes[l]], h2)[0]))
        (gate,) = kernel_call(
            functools.partial(gate_values_kernel, shards=shards),
            "gate_values",
            [chunk_shape],
            idx,
            [h2, w_b[l]],
        )
        *reads, dense = read_call(idx, weights, names, l, values, plan, tokens)
        reads = swaps(reads, "ctx")
        sums = kernel_call(sum_kernel, "memory_sum", [part_shape] * 4, idx, reads)
        sums = swaps(sums, "tp")
        if l + 1 < layers:
            mem, box, x3, h_chunk = kernel_call(
                functools.partial(gate_kernel, row=l + 1, shards=shards),
                "gate",
                [chunk_shape, box_shape, chunk_shape, part_shape],
                idx,
                [*sums, gate, w_b[l], middle, h2, gains],
                [chunk_scratch],
            )
            h_chunks = spread(h_chunk, TA)
        else:
            mem = x3 = None
            gn, box, back_box = kernel_call(
                functools.partial(gate_last_kernel, plan=plan, shards=shards),
                "gate_last",
                [part_shape, box_shape, box_shape],
                idx,
                [*sums, gate, w_b[l], middle, h2, cotangent[0]],
                [
                    pltpu.VMEM((chunk, d_model), f32),
                    chunk_scratch,
                    pltpu.VMEM((chunk, d_model), f32),
                    chunk_scratch,
                ],
            )
        kept.append((x, h1, es, attended, middle, u, w, gate, dense, mem, box))
        x = x3

    g = cotangent[0]
    packs = [None] * layers
    gain_rows = [None] * (2 * layers)
    table_grads = None
    table_list = [None] * layers
    output = dvs_above = None
    for l in reversed(range(layers)):
        x, h1, es, attended, middle, u, w, gate, dense, mem, box = kept[l]
        top = l == layers - 1
        line = jnp.concatenate(spread(gn, "tp"), axis=0)
        planes = spread(line, "ctx")
        if not top and shards == 2:
            table_grads = table_grad_call(*dvs_above, l + 1, layers, table_grads)
            planes[3], table_grads = after([planes[3], table_grads])
        *dvs, gw = write_call(idx, planes, names, l, dense, values, plan, tokens)
        if shards == 2:
            dvs_above = [dvs[0], swap(dvs[1], "fsdp", 1)]
        else:
            table_list[l] = lax.psum_scatter(dvs[0], "fsdp", scatter_dimension=0, tiled=True).astype(f32)
        if not top:
            back_all = lax.all_gather(after([back_box], line)[0], TA, axis=0, tiled=False)
            gw, back_all = after([gw, back_all])
        gw = lax.all_to_all(gw, ("ctx", "tp"), 0, 0, tiled=True)
        back_shape = shape((chunk, 10 * HD), bf16)
        g_mid, go_chunk, gain_rows[layers + l], *back = kernel_call(
            functools.partial(lookup_back_kernel, plan=plan, row=layers + l, layer=l, shards=shards),
            "lookup_back",
            [chunk_shape, part_shape, gain_shape] + [back_shape] * 4,
            idx,
            [gw, table, w, w_a[l], u, back_box, w_b[l], middle, g, gains],
            [
                pltpu.VMEM(w.shape, f32),
                pltpu.VMEM(u.shape, bf16),
                pltpu.VMEM((4, NSUB // 4, 8 * HD), bf16),
                pltpu.VMEM((chunk, d_model), f32),
            ],
        )
        go_chunks = spread(go_chunk, TA)
        if l == 0 and shards == 2:
            table_grads = table_grad_call(*dvs_above, l, layers, table_grads)
            go_chunks[3], table_grads = after([go_chunks[3], table_grads])
        go, *ups = kernel_call(
            functools.partial(out_back_kernel, plan=plan),
            "attend_out_back",
            [full_shape] + [folded] * 4,
            idx,
            [*go_chunks, *w_o[l]],
            [pltpu.VMEM((4, tokens // 2, 2 * HD), bf16)],
        )
        ups = swaps(ups, SA)
        back = swaps(back, TA)
        ups[3], *back = after([ups[3], *back])
        shard_size = d_model // shards
        head_grads = kernel_call(
            functools.partial(attend_back_kernel, plan=plan),
            "attend_back",
            [heads_shape] * 4,
            idx,
            [*es, *ups, ids_row, ids_col],
            kv_scratch + [pltpu.VMEM((4 * tokens, HD), f32)] * 2,
        )
        head_grads = swaps(head_grads, SA)
        if top:
            forward_all = lax.all_gather(after([box], line)[0], TA, axis=0, tiled=False)
            below_all = lax.all_gather(after([kept[l - 1][10]], line)[0], TA, axis=0, tiled=False)
        else:
            forward_all = below_all
        if top:
            back_all = lax.all_gather(after([back_box], line)[0], TA, axis=0, tiled=False)
        if top:
            output = back_all[:, :, d_model:].reshape(tokens, d_model)
        riders = [] if l else [inputs[0], *gain_rows[1:]]
        g_qkv, *parts = kernel_call(
            functools.partial(qkv_back_kernel, plan=plan, row=l, gain_rows=len(riders)),
            "qkv_back",
            [shape((tokens, 3 * width), bf16)] + [part_shape if l else shape((chunk + 16, d_model), bf16)] * 4,
            idx,
            [*head_grads, *w_qkv[l], *riders],
            [pack_scratch, part_scratch],
        )
        parts = swaps(parts, TA)
        qkv_rows = 3 * shard_size
        weight_rows = shard_size * 7 // 2 + NSUB // shards // 2
        weight_scratch = [
            pltpu.VMEM((shards, weight_rows, 256), bf16),
            pltpu.VMEM((tokens, d_model), bf16),
            pltpu.VMEM((tokens, width), bf16),
            pltpu.VMEM((tokens, width), bf16),
            pltpu.VMEM((tokens, 2 * HD), bf16),
            pltpu.VMEM((tokens, d_model), bf16),
        ]
        qkv_scratch = [pltpu.VMEM((shards, qkv_rows, 256), bf16)]
        split = l == 0 and shards == 2
        weight_outs = [shape((weight_rows, 256), bf16)] * 2 if split else [shape((shards, weight_rows, 256), bf16)]
        qkv_outs = [shape((qkv_rows, 256), bf16)] * 2 if split else [shape((shards, qkv_rows, 256), bf16)]
        qkv_packs = kernel_call(
            qkv_grad_kernel, "qkv_grad", qkv_outs, idx, [h1, g_qkv], qkv_scratch
        )
        weight_packs = kernel_call(
            functools.partial(weight_grad_kernel, plan=plan, has_full=top),
            "weight_grad",
            weight_outs,
            idx,
            [forward_all, back_all, *back, attended, go] + ([cotangent[0]] if top else []),
            weight_scratch,
        )
        if split:
            quarter = shape((qkv_rows // 4, 256), bf16)
            qkv_quarters = kernel_call(
                add_two_kernel, "qkv_add", [quarter] * 4, idx, [qkv_packs[0], swap(qkv_packs[1], "fsdp", 1)]
            )
            quarter = shape((weight_rows // 4, 256), bf16)
            weight_quarters = kernel_call(
                add_two_kernel,
                "weight_add",
                [quarter] * 4,
                idx,
                [weight_packs[0], swap(weight_packs[1], "fsdp", 1)],
            )
            weight_quarters = swaps(weight_quarters, "ctx")
            parts[3], *weight_quarters = after([parts[3], *weight_quarters])
        else:
            parts[3], weight_packs[0], qkv_packs[0], below_all = after(
                [parts[3], weight_packs[0], qkv_packs[0], below_all]
            )
            packs[l] = reduce_packs([weight_packs[0], qkv_packs[0]])
        if l > 0:
            below = kept[l - 1]
            g, gain_rows[l], gn, back_box = kernel_call(
                functools.partial(norm_back_kernel, plan=plan, row=l, shards=shards),
                "norm_back",
                [chunk_shape, gain_shape, part_shape, box_shape],
                idx,
                [*parts, x, g_mid, gains, w_b[l - 1], below[7], below[9]],
                [chunk_scratch],
            )
        else:
            g, gain_all, *gain_halves = kernel_call(
                functools.partial(norm_back_last_kernel, plan=plan, row=l),
                "norm_back_last",
                [part_shape, shape((16, d_model), f32), shape((16, 256), bf16), shape((16, 256), bf16)],
                idx,
                [*parts, x, g_mid, gains],
            )
    (input_gradient,) = kernel_call(
        functools.partial(place_kernel, plan=plan),
        "input_gradient",
        [shape((tokens, d_model), f32)],
        idx,
        spread(g, TA),
    )
    if shards != 2:
        table_grads = jnp.stack(table_list)
    gain_shapes = []
    if shards == 2:
        rows = (weight_rows + qkv_rows) // 4
        (part,) = kernel_call(
            plane_sum_kernel,
            "plane_sum",
            [shape((rows + 16, 256), bf16)],
            idx,
            [*weight_quarters, *swaps(qkv_quarters, "ctx"), gain_halves[0], swap(gain_halves[1], "fsdp", 1)],
        )
        part, *packs[1] = after([part, *packs[1]])
        late = spread(part, "ctx")
        gain_shapes = [shape((layers, d_model // 2), f32)] * 2
        flat = late + [p for l in range(1, layers) for p in packs[l]]
    else:
        gain_all = lax.psum(
            lax.psum_scatter(gain_all[: 2 * layers], "fsdp", scatter_dimension=1, tiled=True), "ctx"
        )
        flat = [p for l in range(layers) for p in packs[l]]
    shard_size = d_model // shards
    tall = shape((layers, shard_size, width), f32)
    wide = shape((layers, width, shard_size), f32)
    sub = shape((layers, 1, HD, NSUB // shards), f32)
    grads = kernel_call(
        functools.partial(finalize_kernel, layers=layers, late=shards == 2),
        "finalize",
        [tall, tall, tall, wide, shape((layers, shard_size, 2 * HD), f32), tall, wide, sub, sub]
        + gain_shapes,
        idx,
        flat,
        [pltpu.VMEM((weight_rows, 256), bf16), pltpu.VMEM((qkv_rows, 256), bf16)] if shards == 2 else [],
    )
    gain_grads = grads[9:] if shards == 2 else [gain_all[:layers], gain_all[layers:]]
    return (
        output[None],
        input_gradient[None],
        *grads[:7],
        *[jnp.swapaxes(t, 2, 3) for t in grads[7:9]],
        *gain_grads,
        table_grads,
    )


def solution(mesh):
    placed = (
        P("fsdp", "ctx", None),
        P(None, "fsdp", "tp"),
        P(None, "fsdp", "tp"),
        P(None, "fsdp", "tp"),
        P(None, "tp", "fsdp"),
        P(None, "fsdp", "tp"),
        P(None, "fsdp", "tp"),
        P(None, "tp", "fsdp"),
        P(None, "tp", "fsdp", None),
        P(None, "tp", "fsdp", None),
        P(None, "fsdp"),
        P(None, "fsdp"),
        P(None, ("fsdp", "ctx", "tp"), None),
        P("fsdp", None),
        P(None, "fsdp", "tp", "ctx", None),
        P(None, "fsdp", "tp", "ctx", None, None),
        P("fsdp", "ctx", None),
    )
    return jax.shard_map(
        body,
        mesh=mesh,
        in_specs=placed,
        out_specs=(
            P("fsdp", "ctx", None),
            P("fsdp", "ctx", None),
            P(None, "fsdp", "tp"),
            P(None, "fsdp", "tp"),
            P(None, "fsdp", "tp"),
            P(None, "tp", "fsdp"),
            P(None, "fsdp", "tp"),
            P(None, "fsdp", "tp"),
            P(None, "tp", "fsdp"),
            P(None, "tp", "fsdp", None),
            P(None, "tp", "fsdp", None),
            P(None, "fsdp"),
            P(None, "fsdp"),
            P(None, ("fsdp", "ctx", "tp"), None),
        ),
        check_vma=False,
    )
```
